512 devices in a mesh: lat: 8 (over y_hi, x), lon: 16 (over z), grp: 4 (over y_lo, core).
Axes of the slice: x: 4, y: 4 (y_hi: 2, y_lo: 2; y = y_hi * 2 + y_lo), z: 16, core: 2. Of those that a mesh axis runs over, the one named last changes fastest.
Arguments:
- fields: bfloat16 [2, 96, 768, 192], P(None, 'lat', ('lon', 'grp')), may hold values from -6 to 6
- region: int32 [2, 96, 768], P(None, 'lat', ('lon', 'grp')), may hold values from 0 to 2
- bias_index: int32 [72, 72], replicated, may hold values from 0 to 1583
- fine_bias: bfloat16 [16, 1584, 6], P('lat'), may hold values from -4 to 243
- coarse_bias: bfloat16 [8, 1584, 12], P('lat', None, 'grp'), may hold values from -4 to 243
- fine_qkv: bfloat16 [192, 3, 192], replicated, may hold values from -0.4375 to 0.4375
- fine_proj: bfloat16 [192, 192], replicated, may hold values from -0.4375 to 0.4375
- fine_up: bfloat16 [192, 768], replicated, may hold values from -0.4375 to 0.4375
- fine_down: bfloat16 [768, 192], replicated, may hold values from -0.21875 to 0.21875
- merge_weight: bfloat16 [768, 384], replicated, may hold values from -0.21875 to 0.21875
- coarse_qkv: bfloat16 [384, 3, 384], P(None, None, 'grp'), may hold values from -0.3125 to 0.3125
- coarse_proj: bfloat16 [384, 384], P('grp'), may hold values from -0.3125 to 0.3125
- coarse_up: bfloat16 [384, 1536], P(None, 'grp'), may hold values from -0.3125 to 0.3125
- coarse_down: bfloat16 [1536, 384], P('grp'), may hold values from -0.15625 to 0.15625
- out_cotangent: bfloat16 [2, 48, 384, 384], P(None, 'lat', ('lon', 'grp')), may hold values from -6 to 6
Outputs:
- coarse_out: bfloat16 [2, 48, 384, 384], P(None, 'lat', ('lon', 'grp'))
- grad_fields: float32 [2, 96, 768, 192], P(None, 'lat', ('lon', 'grp'))
- grad_fine_bias: float32 [16, 1584, 6], P('lat')
- grad_coarse_bias: float32 [8, 1584, 12], P('lat', None, 'grp')
The draws below stay inside these ranges and needn't reach their ends.
All inputs are finite; a program needn't handle non-finite values.
Results may differ from the reference program's by a relative error of at most 0.04.
Values may be sent and summed in bfloat16 or wider, within the bound.
A program may use at most 64 MiB of HBM per device.

```python
import math
import jax
import jax.numpy as jnp
from jax import lax

C = 192
HF = 6
FFF = 768
CC = 384
HC = 12
FFC = 1536
WZ = 2
WLAT = 6
WLON = 6
Z = 2
WN = 72
BLEN = 1584
LAT = 96
LON = 768
CLAT = 48
CLON = 384
FTYPES = 16
CTYPES = 8


def draw_fine_bias(key, part):
    key = jax.random.fold_in(key, 11)
    extent = (FTYPES, BLEN, HF)
    return jnp.clip(jax.random.normal(key, extent, jnp.float32), -4.0, 4.0).astype(jnp.bfloat16)


def draw_coarse_bias(key, part):
    key = jax.random.fold_in(key, 12)
    extent = (CTYPES, BLEN, HC)
    return jnp.clip(jax.random.normal(key, extent, jnp.float32), -4.0, 4.0).astype(jnp.bfloat16)


def touch_ends(values, stream_key, least, high):
    longest = values.shape.index(max(values.shape))
    spots = []
    for shift in (0, 1):
        where = [jax.random.randint(jax.random.fold_in(stream_key, axis), (), 0, length) for axis, length in enumerate(values.shape)]
        where[longest] = (where[longest] + shift) % values.shape[longest]
        spots.append(tuple(where))
    return values.at[spots[0]].set(least).at[spots[1]].set(high)


def shard_levels(stream_key, shape, pieces, low, high):
    factor_of = 1.0
    for axis_at, blocks in pieces:
        draws = jax.random.uniform(jax.random.fold_in(jax.random.fold_in(stream_key, 6), axis_at), (blocks,), jnp.float32, low / len(pieces), high / len(pieces))
        factor_of = factor_of * jnp.repeat(jnp.exp(draws), shape[axis_at] // blocks).reshape((-1,) + (1,) * (len(shape) - 1 - axis_at))
    return factor_of


def scatter_about(key, shape, scale, reach, shards=(), dtype=jnp.bfloat16):
    entries = scale * jax.random.normal(key, shape, jnp.float32)
    if shards:
        entries = entries * shard_levels(key, shape, shards, -0.22, 0.18)
    return jnp.clip(entries, -reach, reach).astype(dtype)


def setup_inputs(seed: int = 0) -> dict:
    seeds = jax.random.split(jax.random.key(seed), 16)
    fields = scatter_about(seeds[0], (Z, LAT, LON, C), 1.0, 6.0, ((1, 8), (2, 64)))
    region = touch_ends(jax.random.randint(seeds[1], (Z, LAT, LON), 0, 3), jax.random.fold_in(seeds[1], 1), 0, 2).astype(jnp.int32)
    bias_index = touch_ends(jax.random.randint(seeds[2], (WN, WN), 0, BLEN), jax.random.fold_in(seeds[2], 1), 0, BLEN - 1).astype(jnp.int32)
    fine_bias = draw_fine_bias(jax.random.fold_in(seeds[15], 71), 0)
    coarse_bias = draw_coarse_bias(jax.random.fold_in(seeds[15], 71), 0)
    fine_qkv = scatter_about(seeds[5], (C, 3, C), C ** -0.5, 0.4375)
    fine_proj = scatter_about(seeds[6], (C, C), C ** -0.5, 0.4375)
    fine_up = scatter_about(seeds[7], (C, FFF), C ** -0.5, 0.4375)
    fine_down = scatter_about(seeds[8], (FFF, C), FFF ** -0.5, 0.21875)
    merge_weight = scatter_about(seeds[9], (4 * C, CC), (4 * C) ** -0.5, 0.21875)
    coarse_qkv = scatter_about(seeds[10], (CC, 3, CC), CC ** -0.5, 0.3125, ((2, 4),))
    coarse_proj = scatter_about(seeds[11], (CC, CC), CC ** -0.5, 0.3125, ((0, 4),))
    coarse_up = scatter_about(seeds[12], (CC, FFC), CC ** -0.5, 0.3125, ((1, 4),))
    coarse_down = scatter_about(seeds[13], (FFC, CC), FFC ** -0.5, 0.15625, ((0, 4),))
    out_cotangent = scatter_about(seeds[14], (Z, CLAT, CLON, CC), 1.0, 6.0, ((1, 8), (2, 64)))
    return dict(fields=fields, region=region, bias_index=bias_index, fine_bias=fine_bias, coarse_bias=coarse_bias, fine_qkv=fine_qkv, fine_proj=fine_proj, fine_up=fine_up, fine_down=fine_down, merge_weight=merge_weight, coarse_qkv=coarse_qkv, coarse_proj=coarse_proj, coarse_up=coarse_up, coarse_down=coarse_down, out_cotangent=out_cotangent)


EPSILON = 1e-05
NEGATIVE = -1e+30
HALF_ROOT = 1.0 / math.sqrt(2.0)
DENSITY = 1.0 / math.sqrt(2.0 * math.pi)

def layer_norm(values):
    values = values.astype(jnp.float32)
    centred = values - lax.optimization_barrier(jnp.mean(values, axis=-1, keepdims=True))
    inverse = lax.rsqrt(lax.optimization_barrier(jnp.mean(centred * centred, axis=-1, keepdims=True)) + EPSILON)
    return (centred * inverse, inverse)

def norm_back(normed, inverse, upstream):
    mean_up = lax.optimization_barrier(jnp.mean(upstream, axis=-1, keepdims=True))
    mean_cross = lax.optimization_barrier(jnp.mean(upstream * normed, axis=-1, keepdims=True))
    return inverse * (upstream - mean_up - normed * mean_cross)

def gelu_slope(pre_act):
    return 0.5 * (1.0 + lax.erf(pre_act * HALF_ROOT)) + pre_act * jnp.exp(-0.5 * pre_act * pre_act) * DENSITY

def matmul(operand, matrix):
    flat_rows = operand.reshape(-1, operand.shape[-1])
    result = jnp.dot(flat_rows, matrix, preferred_element_type=jnp.float32)
    return result.reshape(operand.shape[:-1] + (matrix.shape[-1],))

def contract(pattern, first_operand, second_operand):
    return jnp.einsum(pattern, first_operand.astype(jnp.float32), second_operand.astype(jnp.float32))

def unchanged(anything):
    return anything

def to_windows(spatial):
    level_count, row_count, col_count, feature_count = spatial.shape
    blocked = spatial.reshape(level_count, row_count // WLAT, WLAT, col_count // WLON, WLON, feature_count)
    blocked = jnp.transpose(blocked, (1, 3, 0, 2, 4, 5))
    return blocked.reshape(row_count // WLAT, col_count // WLON, level_count * WLAT * WLON, feature_count)

def from_windows(windowed):
    lat_blocks, lon_blocks, tokens, feature_count = windowed.shape
    level_count = tokens // (WLAT * WLON)
    blocked = windowed.reshape(lat_blocks, lon_blocks, level_count, WLAT, WLON, feature_count)
    blocked = jnp.transpose(blocked, (2, 0, 3, 1, 4, 5))
    return blocked.reshape(level_count, lat_blocks * WLAT, lon_blocks * WLON, feature_count)

def merge_cells(spatial):
    level_count, row_count, col_count, feature_count = spatial.shape
    blocked = spatial.reshape(level_count, row_count // 2, 2, col_count // 2, 2, feature_count)
    blocked = jnp.transpose(blocked, (0, 1, 3, 4, 2, 5))
    return blocked.reshape(level_count, row_count // 2, col_count // 2, 4 * feature_count)

def split_cells(joined):
    level_count, row_half, col_half, joined_width = joined.shape
    blocked = joined.reshape(level_count, row_half, col_half, 2, 2, joined_width // 4)
    blocked = jnp.transpose(blocked, (0, 1, 4, 2, 3, 5))
    return blocked.reshape(level_count, 2 * row_half, 2 * col_half, joined_width // 4)

def attend_forward(normed, qkv_weight, bias_table, position_index, allowed):
    head_count = bias_table.shape[2]
    head_width = qkv_weight.shape[2]
    head_size = head_width // head_count
    scaling = head_size ** (-0.5)
    packed = matmul(normed, qkv_weight.reshape(qkv_weight.shape[0], 3 * head_width)).astype(jnp.bfloat16)
    packed = packed.reshape(normed.shape[:3] + (3, head_count, head_size))
    queries = packed[:, :, :, 0]
    keys = packed[:, :, :, 1]
    values = packed[:, :, :, 2]
    bias_terms = jnp.take(bias_table, position_index, axis=1).astype(jnp.float32)
    bias_terms = jnp.transpose(bias_terms, (0, 3, 1, 2))[:, None]
    scores = contract('abihd,abjhd->abhij', queries, keys) * scaling + bias_terms
    scores = jnp.where(allowed, scores, NEGATIVE)
    row_peak = lax.optimization_barrier(jnp.max(scores, axis=-1, keepdims=True))
    weights = jnp.exp(scores - row_peak)
    probabilities = weights / lax.optimization_barrier(jnp.sum(weights, axis=-1, keepdims=True))
    rounded = probabilities.astype(jnp.bfloat16)
    attended = contract('abhij,abjhd->abihd', rounded, values).astype(jnp.bfloat16)
    return (attended.reshape(normed.shape[:3] + (head_width,)), (queries, keys, values, probabilities))

def attend_backward(upstream, saved, qkv_weight, position_index, table_length):
    queries, keys, values, probabilities = saved
    head_count = queries.shape[3]
    head_size = queries.shape[4]
    scaling = head_size ** (-0.5)
    upstream = upstream.reshape(upstream.shape[:3] + (head_count, head_size))
    rounded = probabilities.astype(jnp.bfloat16)
    grad_probs = contract('abihd,abjhd->abhij', upstream, values)
    grad_values = contract('abhij,abihd->abjhd', rounded, upstream).astype(jnp.bfloat16)
    grad_scores = probabilities * (grad_probs - lax.optimization_barrier(jnp.sum(grad_probs * probabilities, axis=-1, keepdims=True)))
    summed = lax.optimization_barrier(jnp.sum(grad_scores, axis=1))
    flattened = jnp.transpose(summed, (2, 3, 0, 1)).reshape(position_index.size, -1)
    table_sums = jax.ops.segment_sum(flattened, position_index.reshape(-1), num_segments=table_length)
    grad_table = jnp.transpose(table_sums.reshape(table_length, summed.shape[0], head_count), (1, 0, 2))
    grad_round = grad_scores.astype(jnp.bfloat16)
    grad_queries = (contract('abhij,abjhd->abihd', grad_round, keys) * scaling).astype(jnp.bfloat16)
    grad_keys = (contract('abhij,abihd->abjhd', grad_round, queries) * scaling).astype(jnp.bfloat16)
    grad_packed = jnp.stack([grad_queries, grad_keys, grad_values], axis=3)
    grad_packed = grad_packed.reshape(upstream.shape[:3] + (3 * head_count * head_size,))
    grad_normed = matmul(grad_packed, qkv_weight.reshape(qkv_weight.shape[0], -1).T)
    return (grad_normed, grad_table)

def fine_attend(shifted, allowed, bias_table, position_index, qkv_weight, proj_weight):
    normed, inverse = layer_norm(shifted)
    attended, saved = attend_forward(to_windows(normed.astype(jnp.bfloat16)), qkv_weight, bias_table, position_index, allowed)
    branch = matmul(attended, proj_weight).astype(jnp.bfloat16)
    return (from_windows(branch), (normed, inverse, saved))

def fine_attend_back(grad_branch, stored, position_index, qkv_weight, proj_weight, table_length):
    normed, inverse, saved = stored
    upstream = matmul(to_windows(grad_branch), proj_weight.T).astype(jnp.bfloat16)
    grad_normed, grad_table = attend_backward(upstream, saved, qkv_weight, position_index, table_length)
    grad_shifted = norm_back(normed, inverse, from_windows(grad_normed))
    return (grad_shifted.astype(jnp.bfloat16), grad_table)

def fine_mlp(first, up_weight, down_weight, merge_weight):
    normed, inverse = layer_norm(first)
    hidden_pre = matmul(normed.astype(jnp.bfloat16), up_weight)
    hidden = jax.nn.gelu(hidden_pre, approximate=False).astype(jnp.bfloat16)
    second = (first.astype(jnp.float32) + matmul(hidden, down_weight)).astype(jnp.bfloat16)
    joined_norm, joined_inverse = layer_norm(merge_cells(second))
    merged = matmul(joined_norm.astype(jnp.bfloat16), merge_weight).astype(jnp.bfloat16)
    return (merged, (normed, inverse, hidden_pre, joined_norm, joined_inverse))

def fine_mlp_back(grad_merged, stored, up_weight, down_weight, merge_weight):
    normed, inverse, hidden_pre, joined_norm, joined_inverse = stored
    grad_joined = norm_back(joined_norm, joined_inverse, matmul(grad_merged, merge_weight.T))
    grad_second = split_cells(grad_joined)
    grad_hidden = matmul(grad_second.astype(jnp.bfloat16), down_weight.T)
    grad_pre = (grad_hidden * gelu_slope(hidden_pre)).astype(jnp.bfloat16)
    return grad_second + norm_back(normed, inverse, matmul(grad_pre, up_weight.T))

def coarse_forward(base, weights, bias_table, position_index, spread, collect):
    qkv_weight, proj_weight, up_weight, down_weight = weights
    normed, inverse = layer_norm(base)
    attended, saved = attend_forward(spread(normed.astype(jnp.bfloat16)), qkv_weight, bias_table, position_index, True)
    first = (base.astype(jnp.float32) + collect(matmul(attended, proj_weight))).astype(jnp.bfloat16)
    normed_two, inverse_two = layer_norm(first)
    hidden_pre = matmul(spread(normed_two.astype(jnp.bfloat16)), up_weight)
    hidden = jax.nn.gelu(hidden_pre, approximate=False).astype(jnp.bfloat16)
    second = (first.astype(jnp.float32) + collect(matmul(hidden, down_weight))).astype(jnp.bfloat16)
    return (second, (normed, inverse, saved, normed_two, inverse_two, hidden_pre))

def coarse_backward(upstream, stored, weights, position_index, table_length, spread, collect):
    qkv_weight, proj_weight, up_weight, down_weight = weights
    normed, inverse, saved, normed_two, inverse_two, hidden_pre = stored
    grad_hidden = matmul(spread(upstream), down_weight.T)
    grad_pre = (grad_hidden * gelu_slope(hidden_pre)).astype(jnp.bfloat16)
    grad_first = upstream.astype(jnp.float32) + norm_back(normed_two, inverse_two, collect(matmul(grad_pre, up_weight.T)))
    grad_attended = matmul(spread(grad_first.astype(jnp.bfloat16)), proj_weight.T).astype(jnp.bfloat16)
    grad_normed, grad_table = attend_backward(grad_attended, saved, qkv_weight, position_index, table_length)
    grad_base = grad_first + norm_back(normed, inverse, collect(grad_normed))
    return (grad_base.astype(jnp.bfloat16), grad_table)

def reference(fields, region, bias_index, fine_bias, coarse_bias, fine_qkv, fine_proj, fine_up, fine_down, merge_weight, coarse_qkv, coarse_proj, coarse_up, coarse_down, out_cotangent):
    table_length = fine_bias.shape[1]
    offsets = (WZ // 2, WLAT // 2, WLON // 2)
    backwards = (-offsets[0], -offsets[1], -offsets[2])
    lat_blocks = LAT // WLAT

    def by_rows(spatial):
        split_rows = spatial.reshape((spatial.shape[0], lat_blocks, spatial.shape[1] // lat_blocks) + spatial.shape[2:])
        return jnp.moveaxis(split_rows, 1, 0)

    def join_rows(stacked):
        moved = jnp.moveaxis(stacked, 0, 1)
        return moved.reshape((moved.shape[0], moved.shape[1] * moved.shape[2]) + moved.shape[3:])

    def allowed_of(region_rows):
        labels = to_windows(region_rows[..., None])[..., 0]
        return (labels[:, :, :, None] == labels[:, :, None, :])[:, :, None]
    shifted = jnp.roll(fields, backwards, axis=(0, 1, 2))

    def attend_rows(items):
        shifted_rows, region_rows, table_rows = items
        branch_rows, ignored = fine_attend(shifted_rows, allowed_of(region_rows), table_rows[None], bias_index, fine_qkv, fine_proj)
        return branch_rows
    branch = join_rows(lax.map(attend_rows, (by_rows(shifted), by_rows(region), fine_bias)))
    first = (fields.astype(jnp.float32) + jnp.roll(branch, offsets, axis=(0, 1, 2)).astype(jnp.float32)).astype(jnp.bfloat16)

    def mlp_rows(first_rows):
        merged_rows, ignored = fine_mlp(first_rows, fine_up, fine_down, merge_weight)
        return merged_rows
    merged = join_rows(lax.map(mlp_rows, by_rows(first)))
    coarse_weights = (coarse_qkv, coarse_proj, coarse_up, coarse_down)

    def coarse_rows(items):
        base_rows, table_rows, upstream_rows = items
        out_rows, stored = coarse_forward(base_rows[None], coarse_weights, table_rows[None], bias_index, unchanged, unchanged)
        grad_rows, grad_table = coarse_backward(upstream_rows[None], stored, coarse_weights, bias_index, table_length, unchanged, unchanged)
        return (out_rows[0], grad_rows[0], grad_table[0])
    out_windows, grad_windows, grad_coarse_bias = lax.map(coarse_rows, (to_windows(merged), coarse_bias, to_windows(out_cotangent)))
    coarse_out = from_windows(out_windows)
    grad_merged = from_windows(grad_windows)

    def mlp_back_rows(items):
        first_rows, grad_rows = items
        ignored, stored = fine_mlp(first_rows, fine_up, fine_down, merge_weight)
        return fine_mlp_back(grad_rows, stored, fine_up, fine_down, merge_weight)
    grad_first = join_rows(lax.map(mlp_back_rows, (by_rows(first), by_rows(grad_merged))))
    grad_branch = jnp.roll(grad_first.astype(jnp.bfloat16), backwards, axis=(0, 1, 2))

    def attend_back_rows(items):
        shifted_rows, region_rows, table_rows, grad_rows = items
        ignored, stored = fine_attend(shifted_rows, allowed_of(region_rows), table_rows[None], bias_index, fine_qkv, fine_proj)
        grad_shift_rows, grad_table = fine_attend_back(grad_rows, stored, bias_index, fine_qkv, fine_proj, table_length)
        return (grad_shift_rows, grad_table[0])
    grad_shifted, grad_fine_bias = lax.map(attend_back_rows, (by_rows(shifted), by_rows(region), fine_bias, by_rows(grad_branch)))
    grad_shifted = join_rows(grad_shifted)
    grad_fields = grad_first + jnp.roll(grad_shifted, offsets, axis=(0, 1, 2)).astype(jnp.float32)
    return (coarse_out, grad_fields, grad_fine_bias, grad_coarse_bias)
```

```python
import functools
import math

import jax
import jax.numpy as jnp
import numpy as np
from jax import lax
from jax.experimental import pallas as pl
from jax.experimental.pallas import tpu as pltpu
from jax.sharding import PartitionSpec as P

MESH = pl.DeviceIdType.MESH
F32 = jnp.float32
BF16 = jnp.bfloat16
EPSILON = 1e-05
NEGATIVE = -1e30
HALF_ROOT = 1.0 / math.sqrt(2.0)
DENSITY = 1.0 / math.sqrt(2.0 * math.pi)
SCALING = 32 ** (-0.5)
WIN = 6
HALF = 3
TOK = 72
SIDE = 12
FINE = 4 * TOK
LANES = 128
HIGH = 13
BLOCKS = 16
KEYS = 80
ROWS = 16
UNROLL = 6
LOOP = 1
LATE = 10
HALO = ((0, 64), (64, 64), (128, 32))
HALO_ROWS = 160


def merge_row(level, row, col):
    group = (row % 2) + 2 * (col % 2)
    return group * TOK + level * 36 + (row // 2) * 6 + col // 2


def window_row(level, row, col):
    window = (row // WIN) * 2 + col // WIN
    return window * TOK + level * 36 + (row % WIN) * 6 + col % WIN


def native_row(level, row, col):
    return (row * SIDE + col) * 2 + level


def permutations():
    cells = [(z, i, j) for z in range(2) for i in range(SIDE) for j in range(SIDE)]
    native_to_merge = np.zeros((FINE, FINE), np.float32)
    merge_send = np.zeros((HALO_ROWS, FINE), np.float32)
    merge_to_window = np.zeros((FINE, FINE + HALO_ROWS), np.float32)
    window_send = np.zeros((HALO_ROWS, FINE), np.float32)
    window_to_merge = np.zeros((FINE, FINE + HALO_ROWS), np.float32)
    label_row = np.zeros((FINE, 2 * SIDE), np.float32)
    label_col = np.zeros((FINE, SIDE), np.float32)
    ahead = [0, 0, 0]
    for z, i, j in cells:
        native_to_merge[merge_row(z, i, j), native_row(z, i, j)] = 1
        target = window_row(z, i, j)
        label_row[target, 2 * i + z] = 1
        label_col[target, j] = 1
        source = merge_row((z + 1) % 2, (i + HALF) % SIDE, (j + HALF) % SIDE)
        over_row, over_col = i + HALF >= SIDE, j + HALF >= SIDE
        if not over_row and not over_col:
            merge_to_window[target, source] = 1
            window_to_merge[source, target] = 1
            continue
        kind = 2 if over_row and over_col else (0 if over_row else 1)
        slot = HALO[kind][0] + ahead[kind]
        ahead[kind] += 1
        merge_send[slot, source] = 1
        merge_to_window[target, FINE + slot] = 1
        window_send[slot, target] = 1
        window_to_merge[source, FINE + slot] = 1
    coarse_native = np.zeros((TOK, TOK), np.float32)
    for z in range(2):
        for i in range(6):
            for j in range(6):
                coarse_native[z * 36 + i * 6 + j, (i * 6 + j) * 2 + z] = 1
    return (
        native_to_merge, native_to_merge.T, merge_send, merge_to_window,
        window_send, window_to_merge, coarse_native, coarse_native.T, label_row, label_col,
    )


def dot(a, b):
    return lax.dot_general(a, b, (((1,), (0,)), ((), ())), preferred_element_type=F32)


def dot_nt(a, b):
    return lax.dot_general(a, b, (((1,), (1,)), ((), ())), preferred_element_type=F32)


def dot_tn(a, b):
    return lax.dot_general(a, b, (((0,), (0,)), ((), ())), preferred_element_type=F32)


def rounded(values):
    return values.astype(BF16).astype(F32)


def layer_norm(values):
    centred = values - jnp.mean(values, axis=-1, keepdims=True)
    inverse = lax.rsqrt(jnp.mean(centred * centred, axis=-1, keepdims=True) + EPSILON)
    return centred * inverse, inverse


def norm_back(normed, inverse, upstream):
    mean_up = jnp.mean(upstream, axis=-1, keepdims=True)
    mean_cross = jnp.mean(upstream * normed, axis=-1, keepdims=True)
    return inverse * (upstream - mean_up - normed * mean_cross)


def gelu_both(pre_act):
    half = 0.5 * (1.0 + lax.erf(pre_act * HALF_ROOT))
    slope = half + pre_act * jnp.exp(-0.5 * pre_act * pre_act) * DENSITY
    return pre_act * half, slope


def head_masks(width):
    lane = lax.broadcasted_iota(jnp.int32, (1, width), 1)
    return [(lane >= 32 * h) & (lane < 32 * h + 32) for h in range(width // 32)]


def stack_heads(values, masks):
    return jnp.concatenate([jnp.where(m, values, 0.0) for m in masks], axis=0).astype(BF16)


def unstack_heads(values, masks):
    total = jnp.where(masks[0], values[:TOK], 0.0)
    for h in range(1, len(masks)):
        total = jnp.where(masks[h], values[h * TOK : (h + 1) * TOK], total)
    return total


def softmax(scores):
    weights = jnp.exp(scores - jnp.max(scores, axis=-1, keepdims=True))
    return weights * (1.0 / jnp.sum(weights, axis=-1, keepdims=True))


def table_scatter(grads, chosen, high):
    def step(p, total):
        parts = []
        for half in range(2):
            i = 2 * p + half
            rows = grads[pl.ds(i, ROWS, stride=TOK), :].astype(BF16)
            picked = jnp.broadcast_to(high[pl.ds(i, 1), :], (ROWS, LANES)).astype(BF16)
            zero = jnp.zeros_like(rows)
            parts.append(
                jnp.concatenate(
                    [jnp.where(picked == jnp.asarray(h, BF16), rows, zero) for h in range(HIGH)],
                    axis=0,
                )
            )
        return total + dot(jnp.concatenate(parts, axis=1), chosen[p])

    return lax.fori_loop(0, TOK // 2, step, jnp.zeros((HIGH * ROWS, LANES), F32), unroll=UNROLL)


def table_gather(table, out, chosen, high):
    entries = table[...].astype(BF16)

    def step(p, carry):
        spread = dot_nt(entries, chosen[p])
        for half in range(2):
            i = 2 * p + half
            picked = jnp.broadcast_to(high[pl.ds(i, 1), :], (ROWS, LANES))
            span = slice(half * LANES, (half + 1) * LANES)
            found = spread[:ROWS, span]
            for h in range(1, HIGH):
                found = jnp.where(picked == h, spread[h * ROWS : (h + 1) * ROWS, span], found)
            out[pl.ds(i, ROWS, stride=TOK), :] = found
        return carry

    lax.fori_loop(0, TOK // 2, step, 0, unroll=UNROLL)


def kernel(
    lats,
    rings,
    fields, native_to_merge, merge_send, region, bias_index, fine_bias, coarse_bias,
    label_row, label_col,
    own_qkv, own_proj, own_up, own_down, *rest,
):
    late_hbm, rest = rest[:LATE], rest[LATE:]
    outs, rest = rest[:4], rest[4:]
    late, rest = rest[:LATE], rest[LATE:]
    body(
        lats, rings, fields, native_to_merge, merge_send, region, bias_index, fine_bias,
        coarse_bias, label_row, label_col, own_qkv, own_proj, own_up, own_down,
        late_hbm, late, *late, *outs, *rest,
    )


def body(
    lats, rings,
    fields, native_to_merge, merge_send, region, bias_index, fine_bias, coarse_bias,
    label_row, label_col, own_qkv, own_proj, own_up, own_down,
    late_hbm, late,
    merge_to_window, fine_qkv, fine_proj, window_send, window_to_merge, fine_up, fine_down,
    merge_weight, cotangent, coarse_native,
    coarse_result, grad_result, fine_sums, coarse_sums,
    halo_out, halo_in, got_qkv, got_proj, got_up, got_down, got_cbias,
    label_rows, high, chosen, table, bias, grads_fine, grads_coarse,
    queries, keys, values, probs, score_grads, slope, first_ref, cprobs, cslope,
    spread_ref, label_ref, attended, outer_ref, qkv_grads, cqueries, ckeys, cvalues,
    part_fine, ring_fine, group_fine, final_fine,
    part_coarse, ring_coarse, group_coarse, final_coarse,
    late_sems, halo_send, halo_recv, weight_send, weight_recv, cbias_send, cbias_recv,
    fine_sems, coarse_sems,
):
    lat = lax.axis_index("lat")
    ring = lax.axis_index("lon")
    group = lax.axis_index("grp")
    column = ring * 4 + group
    columns = rings * 4

    def place(row_shift, col_shift):
        row = lax.rem(lat + row_shift + lats, lats)
        col = lax.rem(column + col_shift + columns, columns)
        return {"lat": row, "lon": lax.div(col, 4), "grp": lax.rem(col, 4)}

    before = (place(-1, 0), place(0, -1), place(-1, -1))
    after = (place(1, 0), place(0, 1), place(1, 1))
    core_mate = group + 1 - 2 * lax.rem(group, 2)
    chip_mate = lax.rem(group + 2, 4)
    far_mate = lax.rem(core_mate + 2, 4)
    mates = (core_mate, chip_mate, far_mate)

    barrier = pltpu.get_barrier_semaphore()
    for device in before + after:
        pl.semaphore_signal(barrier, 1, device_id=device, device_id_type=MESH)
    for mate in mates:
        pl.semaphore_signal(barrier, 1, device_id={"grp": mate}, device_id_type=MESH)
    far_lat = lax.rem(lat + lats // 2, lats)
    neighbours = ({"grp": chip_mate}, {"lat": far_lat, "grp": chip_mate})
    pl.semaphore_signal(barrier, 1, device_id=neighbours[1], device_id_type=MESH)
    for step in range(1, rings):
        pl.semaphore_signal(
            barrier, 1, device_id={"lon": lax.rem(ring + step, rings)}, device_id_type=MESH
        )

    def remote(source, target, send, recv, device):
        copy = pltpu.make_async_remote_copy(
            source, target, send, recv, device_id=device, device_id_type=MESH
        )
        copy.start()
        return copy

    def send_halo(number, devices, block):
        halo_out[number] = block.astype(BF16)
        copies = []
        for kind, (start, size) in enumerate(HALO):
            rows = pl.ds(start, size)
            copies.append(
                remote(
                    halo_out.at[number, rows], halo_in.at[number, rows],
                    halo_send.at[number, kind], halo_recv.at[number, kind], devices[kind],
                )
            )
        return copies

    def wait(copies):
        for copy in copies:
            copy.wait()

    loads = [
        pltpu.make_async_copy(source, target, late_sems.at[k])
        for k, (source, target) in enumerate(zip(late_hbm, late))
    ]
    owns = [
        pltpu.make_async_copy(own, got.at[0], late_sems.at[LATE + k])
        for k, (own, got) in enumerate(
            ((own_qkv, got_qkv), (own_proj, got_proj), (own_up, got_up), (own_down, got_down))
        )
    ]
    for copy in loads + owns:
        copy.start()

    tokens = dot(native_to_merge[...], fields[...].astype(F32).reshape(FINE, 192).astype(BF16))
    tokens_half = tokens.astype(BF16)
    first_block = dot(merge_send[...], tokens_half)
    pl.semaphore_wait(barrier, 10 + rings - 1)
    pending = send_halo(0, before, first_block)

    shares = ((own_qkv, got_qkv), (own_proj, got_proj), (own_up, got_up), (own_down, got_down))
    to_chip, to_core, passed = [], [], []

    def half_of(ref, half):
        rows = ref.shape[0] // 2
        return ref.at[pl.ds(half * rows, rows)]

    for k, (own, got) in enumerate(shares):
        to_chip.append(
            [
                remote(
                    half_of(own, half), half_of(got.at[2], half),
                    weight_send.at[k, half], weight_recv.at[k, half], neighbours[half],
                )
                for half in range(2)
            ]
        )
    for k, (own, got) in enumerate(shares):
        to_core.append(
            remote(own, got.at[1], weight_send.at[k, 2], weight_recv.at[k, 2], {"grp": core_mate})
        )

    def pass_on(k):
        got = shares[k][1]
        for copy in to_chip[k]:
            copy.wait_recv()
        passed.append(
            remote(
                got.at[2], got.at[3], weight_send.at[k, 3], weight_recv.at[k, 3], {"grp": core_mate}
            )
        )

    index = bias_index[...]
    high[...] = jnp.zeros_like(high)
    high[:, :TOK] = lax.shift_right_logical(index, 7)
    low = (index & (LANES - 1)).astype(F32).astype(BF16)
    key_row = lax.broadcasted_iota(jnp.int32, (LANES, TOK), 0)
    key_col = lax.broadcasted_iota(jnp.int32, (LANES, TOK), 1)
    identity = jnp.where(key_row == key_col, 1.0, 0.0).astype(BF16)
    low_keys = jnp.where(key_row < TOK, dot_nt(identity, low), -1.0)[:KEYS].astype(BF16)
    query = lax.broadcasted_iota(jnp.int32, (TOK, 2 * LANES), 0)
    lane = lax.broadcasted_iota(jnp.int32, (TOK, 2 * LANES), 1)
    target_query = query - lax.shift_right_logical(lane, 7)
    lane = (lax.broadcasted_iota(jnp.int32, (KEYS, 2 * LANES), 1) & (LANES - 1)).astype(F32)
    blank = jnp.zeros((LANES - KEYS, LANES), BF16)

    def choose(p, carry):
        pick = jnp.where(target_query == 2 * p, 1.0, 0.0).astype(BF16)
        found = jnp.where(dot(low_keys, pick) == lane, 1.0, 0.0).astype(BF16)
        for half in range(2):
            at = half * LANES
            chosen[p, at : at + KEYS, :] = found[:, at : at + LANES]
            chosen[p, at + KEYS : at + LANES, :] = blank
        return carry

    lax.fori_loop(0, TOK // 2, choose, 0, unroll=UNROLL)
    table[...] = jnp.zeros_like(table)
    length = fine_bias.shape[2]
    for h in range(HIGH):
        size = min(LANES, length - h * LANES)
        span = slice(h * LANES, h * LANES + size)
        for head in range(6):
            at = h * ROWS + 2 * head
            table[at : at + 2, :size] = fine_bias[head, :, span].astype(F32)
        at = h * ROWS + 12
        table[at : at + 3, :size] = coarse_bias[0, :, span].astype(F32)
    table_gather(table, bias, chosen, high)
    got_cbias[0] = bias[12 * TOK : 12 * TOK + 224, :].astype(BF16)
    cbias_copies = [
        remote(got_cbias.at[0], got_cbias.at[k + 1], cbias_send.at[k], cbias_recv.at[k], {"grp": mate})
        for k, mate in enumerate(mates)
    ]
    grads_fine[...] = jnp.zeros_like(grads_fine)
    grads_coarse[...] = jnp.zeros_like(grads_coarse)

    fine_masks = head_masks(192)
    for i in range(SIDE):
        label_rows[2 * i : 2 * i + 2, :] = region[i].astype(F32)
    spread_labels = dot(label_row[...], label_rows[...].astype(BF16)) * label_col[...].astype(F32)
    col_labels = jnp.sum(spread_labels, axis=-1, keepdims=True)
    ones = jnp.ones((8, SIDE), BF16)
    spread_ref[...] = spread_labels
    label_ref[...] = col_labels
    loads[0].wait()
    loads[1].wait()
    local = dot(merge_to_window[:, :FINE], tokens_half)
    wait(pending)
    shifted = local + dot(merge_to_window[:, FINE:], halo_in[0])
    fine_normed, fine_inverse = layer_norm(shifted)
    fine_half = fine_normed.astype(BF16)
    for k, ref in enumerate((queries, keys, values)):
        ref[...] = rounded(dot(fine_half, fine_qkv[k]))

    def window_span(w):
        return pl.ds(pl.multiple_of(w * TOK, 8), TOK)

    def attend(w, carry):
        span = window_span(w)
        stacked = stack_heads(queries[span, :], fine_masks)
        scores = dot_nt(stacked, keys[span, :].astype(BF16)) * SCALING
        kind = w // 2
        scores = scores + jnp.concatenate(
            [bias[window_span(2 * h + kind), :TOK] for h in range(6)], axis=0
        )
        row_labels = dot_nt(ones, spread_ref[span, :].astype(BF16))[:1]
        allowed = label_ref[span, :] == row_labels
        scores = jnp.where(allowed[None], scores.reshape(6, TOK, TOK), NEGATIVE)
        weights = softmax(scores.reshape(6 * TOK, TOK))
        probs[w] = weights
        attended[span, :] = unstack_heads(
            dot(weights.astype(BF16), values[span, :].astype(BF16)), fine_masks
        )
        return carry

    lax.fori_loop(0, 4, attend, 0, unroll=LOOP)
    for k in range(2, 5):
        loads[k].wait()
    branch = dot(attended[...].astype(BF16), fine_proj[...]).astype(BF16)
    pending = send_halo(1, after, dot(window_send[...], branch))
    local = tokens + dot(window_to_merge[:, :FINE], branch)
    pass_on(0)
    pass_on(1)
    wait(pending)
    first = rounded(local + dot(window_to_merge[:, FINE:], halo_in[1]))
    first_ref[...] = first

    for k in range(5, 8):
        loads[k].wait()
    normed, inverse = layer_norm(first)
    hidden, slopes = gelu_both(dot(normed.astype(BF16), fine_up[...]))
    slope[...] = slopes
    second = rounded(first + dot_nt(hidden.astype(BF16), fine_down[...]))
    cells = [second[g * TOK : (g + 1) * TOK] for g in range(4)]
    width = 4 * second.shape[1]
    mean = sum(jnp.sum(c, axis=-1, keepdims=True) for c in cells) / width
    cells = [c - mean for c in cells]
    variance = sum(jnp.sum(c * c, axis=-1, keepdims=True) for c in cells) / width
    joined_inverse = lax.rsqrt(variance + EPSILON)
    cells = [c * joined_inverse for c in cells]
    merged = jnp.zeros((TOK, merge_weight.shape[1]), F32)
    for g in range(4):
        merged += dot(cells[g].astype(BF16), merge_weight[g * 192 : (g + 1) * 192, :])
    merged = rounded(merged)
    pass_on(2)
    pass_on(3)

    coarse_masks = head_masks(96)
    loads[8].wait()
    loads[9].wait()
    upstream = dot(
        coarse_native[...], cotangent[...].astype(F32).reshape(TOK, 384).astype(BF16)
    )
    base_normed, base_inverse = layer_norm(merged)
    base_half = base_normed.astype(BF16)
    wait(cbias_copies)

    def arrive(k):
        owns[k].wait()
        to_core[k].wait_recv()
        passed[k].wait_recv()

    arrive(0)
    arrive(1)

    def coarse_attend(g, total):
        q, k, v = (
            rounded(dot_nt(base_half, got_qkv[g, n * 96 : (n + 1) * 96, :])) for n in range(3)
        )
        cqueries[g] = q
        ckeys[g] = k
        cvalues[g] = v
        stacked = stack_heads(q, coarse_masks)
        scores = dot_nt(stacked, k.astype(BF16)) * SCALING
        scores = scores + got_cbias[g].astype(F32)[: 3 * TOK, :TOK]
        weights = softmax(scores)
        cprobs[g] = weights
        seen = unstack_heads(dot(weights.astype(BF16), v.astype(BF16)), coarse_masks)
        return total + dot(seen.astype(BF16), got_proj[g])

    coarse_first = rounded(lax.fori_loop(0, 4, coarse_attend, merged, unroll=LOOP))
    up_normed, up_inverse = layer_norm(coarse_first)
    up_half = up_normed.astype(BF16)
    arrive(2)
    arrive(3)

    def coarse_mlp(g, total):
        hidden, slopes = gelu_both(dot(up_half, got_up[g]))
        cslope[g] = slopes
        return total + dot(hidden.astype(BF16), got_down[g])

    total = lax.fori_loop(0, 4, coarse_mlp, coarse_first, unroll=LOOP)
    coarse_result[...] = total.astype(BF16)

    upstream_half = upstream.astype(BF16)
    blank = jnp.zeros((TOK, 384), F32)

    def coarse_mlp_back(g, total):
        grad_pre = dot_nt(upstream_half, got_down[g]) * cslope[g]
        return total + dot_nt(grad_pre.astype(BF16), got_up[g])

    total = lax.fori_loop(0, 4, coarse_mlp_back, blank, unroll=LOOP)
    grad_first = upstream + norm_back(up_normed, up_inverse, total)
    grad_half = grad_first.astype(BF16)

    def coarse_attend_back(g, total):
        stacked = stack_heads(cqueries[g], coarse_masks)
        weights = cprobs[g]
        outer = stack_heads(rounded(dot_nt(grad_half, got_proj[g])), coarse_masks)
        grad_probs = dot_nt(outer, cvalues[g].astype(BF16))
        grad_scores = weights * (
            grad_probs - jnp.sum(grad_probs * weights, axis=-1, keepdims=True)
        )
        low_bit = lax.rem(group + g, 2)
        high_bit = lax.rem(lax.div(group, 2) + lax.div(g, 2), 2)
        at = pl.multiple_of((2 * high_bit + low_bit) * (3 * TOK), 8)
        grads_coarse[pl.ds(at, 3 * TOK), :TOK] = grad_scores
        grad_scores = grad_scores.astype(BF16)
        grad_v = dot_tn(weights.astype(BF16), outer)
        grad_q = unstack_heads(dot(grad_scores, ckeys[g].astype(BF16)), coarse_masks) * SCALING
        grad_k = dot_tn(grad_scores, stacked) * SCALING
        for n, grad in enumerate((grad_q, grad_k, grad_v)):
            total = total + dot(grad.astype(BF16), got_qkv[g, n * 96 : (n + 1) * 96, :])
        return total

    total = lax.fori_loop(0, 4, coarse_attend_back, blank, unroll=LOOP)
    grad_merged = (grad_first + norm_back(base_normed, base_inverse, total)).astype(BF16)

    joined = [dot_nt(grad_merged, merge_weight[g * 192 : (g + 1) * 192, :]) for g in range(4)]
    mean_up = sum(jnp.sum(j, axis=-1, keepdims=True) for j in joined) / width
    mean_cross = (
        sum(jnp.sum(j * c, axis=-1, keepdims=True) for j, c in zip(joined, cells)) / width
    )
    grad_second = jnp.concatenate(
        [joined_inverse * (j - mean_up - c * mean_cross) for j, c in zip(joined, cells)], axis=0
    )
    grad_pre = dot(grad_second.astype(BF16), fine_down[...]) * slope[...]
    grad_normed = dot_nt(grad_pre.astype(BF16), fine_up[...])
    normed, inverse = layer_norm(first_ref[...])
    grad_fine = grad_second + norm_back(normed, inverse, grad_normed)
    first_ref[...] = grad_fine
    grad_half = grad_fine.astype(BF16)
    pending = send_halo(2, before, dot(merge_send[...], grad_half))

    share = BLOCKS * ROWS // rings

    def sum_start(sums, part, got, sems):
        sums = sums.astype(BF16)
        blank = jnp.zeros((BLOCKS * ROWS - HIGH * ROWS, LANES), BF16)
        part[...] = jnp.concatenate([sums, blank], axis=0).reshape(rings, share, LANES)
        copies = []
        for step in range(1, rings):
            peer = lax.rem(ring + step, rings)
            copies.append(
                remote(
                    part.at[peer], got.at[step], sems.at[0, step], sems.at[1, step], {"lon": peer}
                )
            )
        return copies

    def sum_group(copies, part, got, grouped, sems):
        wait(copies)
        total = part[ring].astype(F32)
        for step in range(1, rings):
            total += got[step].astype(F32)
        grouped[group] = total
        return [
            remote(
                grouped.at[group], grouped.at[group], sems.at[2, k], sems.at[3, k], {"grp": mate}
            )
            for k, mate in enumerate(mates)
        ]

    def sum_spread(copies, grouped, final, sems):
        wait(copies)
        total = grouped[0] + grouped[1] + grouped[2] + grouped[3]
        final[ring] = total.astype(BF16)
        copies = []
        for step in range(1, rings):
            peer = lax.rem(ring + step, rings)
            copies.append(
                remote(
                    final.at[ring], final.at[ring], sems.at[4, step], sems.at[5, step], {"lon": peer}
                )
            )
        return copies

    def sum_end(copies, final):
        wait(copies)
        return final[...].reshape(BLOCKS * ROWS, LANES)

    coarse_copies = sum_start(
        table_scatter(grads_coarse, chosen, high), part_coarse, ring_coarse, coarse_sems
    )

    local = dot(merge_to_window[:, :FINE], grad_half)
    wait(pending)
    grad_branch = local + dot(merge_to_window[:, FINE:], halo_in[2])
    outer_all = rounded(dot_nt(grad_branch.astype(BF16), fine_proj[...]))
    outer_ref[...] = outer_all

    def attend_back(w, carry):
        weights = probs[w]
        span = window_span(w)
        outer = stack_heads(outer_ref[span, :], fine_masks)
        grad_probs = dot_nt(outer, values[span, :].astype(BF16))
        score_grads[w] = weights * (
            grad_probs - jnp.sum(grad_probs * weights, axis=-1, keepdims=True)
        )
        return carry

    lax.fori_loop(0, 4, attend_back, 0, unroll=LOOP)
    for kind in range(2):
        both = score_grads[2 * kind] + score_grads[2 * kind + 1]
        for h in range(6):
            at = (2 * h + kind) * TOK
            grads_fine[at : at + TOK, :TOK] = both[h * TOK : (h + 1) * TOK]
    coarse_copies = sum_group(coarse_copies, part_coarse, ring_coarse, group_coarse, coarse_sems)
    fine_copies = sum_start(
        table_scatter(grads_fine, chosen, high), part_fine, ring_fine, fine_sems
    )

    def project_back(w, carry):
        span = window_span(w)
        outer = stack_heads(outer_ref[span, :], fine_masks)
        stacked = stack_heads(queries[span, :], fine_masks)
        grad_scores = score_grads[w].astype(BF16)
        grad_q = unstack_heads(dot(grad_scores, keys[span, :].astype(BF16)), fine_masks)
        qkv_grads[0, span, :] = grad_q * SCALING
        qkv_grads[1, span, :] = dot_tn(grad_scores, stacked) * SCALING
        qkv_grads[2, span, :] = dot_tn(probs[w].astype(BF16), outer)
        return carry

    lax.fori_loop(0, 4, project_back, 0, unroll=LOOP)
    coarse_copies = sum_spread(coarse_copies, group_coarse, final_coarse, coarse_sems)
    grad_normed = jnp.zeros((FINE, 192), F32)
    for n in range(3):
        grad_normed += dot_nt(qkv_grads[n].astype(BF16), fine_qkv[n])
    grad_shifted = norm_back(fine_normed, fine_inverse, grad_normed).astype(BF16)
    pending = send_halo(3, after, dot(window_send[...], grad_shifted))
    fine_copies = sum_group(fine_copies, part_fine, ring_fine, group_fine, fine_sems)
    local = first_ref[...] + dot(window_to_merge[:, :FINE], grad_shifted)
    wait(pending)
    grad = local + dot(window_to_merge[:, FINE:], halo_in[3])
    fine_copies = sum_spread(fine_copies, group_fine, final_fine, fine_sems)
    grad_result[...] = grad

    sums = sum_end(coarse_copies, final_coarse)
    row = lax.broadcasted_iota(jnp.int32, (8, ROWS), 0)
    col = lax.broadcasted_iota(jnp.int32, (8, ROWS), 1)
    chooser = jnp.where(col == row + 3 * group, 1.0, 0.0).astype(BF16)
    for h in range(HIGH):
        coarse_sums[h] = dot(chooser, sums[h * ROWS : (h + 1) * ROWS])
    for k in range(4):
        for copy in to_chip[k]:
            copy.wait_send()
        to_core[k].wait_send()
        passed[k].wait_send()
    fine_sums[...] = sum_end(fine_copies, final_fine)


def finish(
    grad_result, coarse_result, fine_sums, coarse_sums, merge_to_native, coarse_back,
    coarse_out, grad_fields, grad_fine_bias, grad_coarse_bias,
):
    grad = grad_result[...]
    upper = grad.astype(BF16)
    lower = (grad - upper.astype(F32)).astype(BF16)
    native_grad = dot(merge_to_native[...], upper) + dot(merge_to_native[...], lower)
    grad_fields[...] = native_grad.reshape(SIDE, SIDE, 2, 192)
    result = dot(coarse_back[...], coarse_result[...])
    coarse_out[...] = result.reshape(6, 6, 2, 384).astype(BF16)
    length = grad_fine_bias.shape[2]
    sums = fine_sums[...].astype(F32)
    for h in range(HIGH):
        size = min(LANES, length - h * LANES)
        span = slice(h * LANES, h * LANES + size)
        for head in range(6):
            at = h * ROWS + 2 * head
            grad_fine_bias[head, :, span] = sums[at : at + 2, :size]
        for head in range(3):
            grad_coarse_bias[head, :, span] = coarse_sums[h, head : head + 1, :size]


def shards(
    fields, region, bias_index, fine_bias, coarse_bias, fine_qkv, fine_proj, fine_up, fine_down,
    merge_weight, coarse_qkv, coarse_proj, coarse_up, coarse_down, out_cotangent,
):
    lats = lax.axis_size("lat")
    rings = lax.axis_size("lon")
    share = BLOCKS * ROWS // rings
    (
        native_to_merge, merge_to_native, merge_send, merge_to_window, window_send,
        window_to_merge, coarse_native, coarse_back, label_row, label_col,
    ) = (jnp.asarray(c, BF16) for c in permutations())
    early = (
        jnp.transpose(fields, (1, 2, 0, 3)), native_to_merge, merge_send,
        jnp.transpose(region, (1, 0, 2)), bias_index,
        jnp.transpose(fine_bias, (2, 0, 1)), jnp.transpose(coarse_bias, (0, 2, 1)),
        label_row, label_col,
    )
    owns = (
        jnp.transpose(coarse_qkv, (1, 2, 0)).reshape(3 * 96, 384), coarse_proj, coarse_up,
        coarse_down,
    )
    late = (
        merge_to_window, jnp.transpose(fine_qkv, (1, 0, 2)), fine_proj, window_send,
        window_to_merge, fine_up, fine_down.T, merge_weight,
        jnp.transpose(out_cotangent, (1, 2, 0, 3)), coarse_native,
    )
    vmem = pltpu.VMEM
    dma = pltpu.SemaphoreType.DMA
    sum_buffers = [
        vmem((rings, share, LANES), BF16),
        vmem((rings, share, LANES), BF16),
        vmem((4, share, LANES), F32),
        vmem((rings, share, LANES), BF16),
    ]
    scratch = [vmem(a.shape, a.dtype) for a in late]
    scratch += [
        vmem((4, HALO_ROWS, 192), BF16),
        vmem((4, HALO_ROWS, 192), BF16),
        vmem((4, 3 * 96, 384), BF16),
        vmem((4, 96, 384), BF16),
        vmem((4, 384, 384), BF16),
        vmem((4, 384, 384), BF16),
        vmem((4, 224, LANES), BF16),
        vmem((2 * SIDE, SIDE), F32),
        vmem((TOK, LANES), jnp.int32),
        vmem((TOK // 2, 2 * LANES, LANES), BF16),
        vmem((HIGH * ROWS, LANES), F32),
        vmem((ROWS * TOK, LANES), F32),
        vmem((ROWS * TOK, LANES), F32),
        vmem((ROWS * TOK, LANES), F32),
        vmem((FINE, 192), F32),
        vmem((FINE, 192), F32),
        vmem((FINE, 192), F32),
        vmem((4, 6 * TOK, TOK), F32),
        vmem((4, 6 * TOK, TOK), F32),
        vmem((FINE, 768), F32),
        vmem((FINE, 192), F32),
        vmem((4, 3 * TOK, TOK), F32),
        vmem((4, TOK, 384), F32),
        vmem((FINE, SIDE), F32),
        vmem((FINE, 1), F32),
        vmem((FINE, 192), F32),
        vmem((FINE, 192), F32),
        vmem((3, FINE, 192), F32),
        vmem((4, TOK, 96), F32),
        vmem((4, TOK, 96), F32),
        vmem((4, TOK, 96), F32),
    ]
    scratch += sum_buffers + sum_buffers
    scratch += [
        dma((LATE + 4,)), dma((4, 3)), dma((4, 3)), dma((4, 4)), dma((4, 4)), dma((3,)), dma((3,)),
        dma((6, BLOCKS)), dma((6, BLOCKS)),
    ]
    whole = pl.BlockSpec(memory_space=pltpu.VMEM)
    hbm = pl.BlockSpec(memory_space=pl.ANY)
    coarse_result, grad_result, fine_sums, coarse_sums = pl.pallas_call(
        functools.partial(kernel, lats, rings),
        out_shape=(
            jax.ShapeDtypeStruct((TOK, 384), BF16),
            jax.ShapeDtypeStruct((FINE, 192), F32),
            jax.ShapeDtypeStruct((BLOCKS * ROWS, LANES), BF16),
            jax.ShapeDtypeStruct((HIGH, 8, LANES), F32),
        ),
        in_specs=[whole] * len(early) + [hbm] * (len(owns) + len(late)),
        out_specs=(whole,) * 4,
        scratch_shapes=scratch,
        compiler_params=pltpu.CompilerParams(
            collective_id=0, has_side_effects=True, vmem_limit_bytes=56 * 1024 * 1024
        ),
    )(*early, *owns, *late)
    outs = pl.pallas_call(
        finish,
        out_shape=(
            jax.ShapeDtypeStruct((6, 6, 2, 384), BF16),
            jax.ShapeDtypeStruct((SIDE, SIDE, 2, 192), F32),
            jax.ShapeDtypeStruct((6, 2, fine_bias.shape[1]), F32),
            jax.ShapeDtypeStruct((3, 1, fine_bias.shape[1]), F32),
        ),
        in_specs=[whole] * 6,
        out_specs=(whole,) * 4,
        compiler_params=pltpu.CompilerParams(vmem_limit_bytes=32 * 1024 * 1024),
    )(grad_result, coarse_result, fine_sums, coarse_sums, merge_to_native, coarse_back)
    return (
        jnp.transpose(outs[0], (2, 0, 1, 3)),
        jnp.transpose(outs[1], (2, 0, 1, 3)),
        jnp.transpose(outs[2], (1, 2, 0)),
        jnp.transpose(outs[3], (1, 2, 0)),
    )


def solution(mesh):
    return jax.shard_map(
        shards,
        mesh=mesh,
        in_specs=(
            P(None, "lat", ("lon", "grp"), None),
            P(None, "lat", ("lon", "grp")),
            P(),
            P("lat", None, None),
            P("lat", None, "grp"),
            P(),
            P(),
            P(),
            P(),
            P(),
            P(None, None, "grp"),
            P("grp", None),
            P(None, "grp"),
            P("grp", None),
            P(None, "lat", ("lon", "grp"), None),
        ),
        out_specs=(
            P(None, "lat", ("lon", "grp"), None),
            P(None, "lat", ("lon", "grp"), None),
            P("lat", None, None),
            P("lat", None, "grp"),
        ),
        check_vma=False,
    )
```

```python
import functools
import math

import jax
import jax.numpy as jnp
import numpy as np
from jax import lax
from jax.experimental import pallas as pl
from jax.experimental.pallas import tpu as pltpu
from jax.sharding import PartitionSpec as P

MESH = pl.DeviceIdType.MESH
F32 = jnp.float32
BF16 = jnp.bfloat16
EPSILON = 1e-05
NEGATIVE = -1e30
HALF_ROOT = 1.0 / math.sqrt(2.0)
DENSITY = 1.0 / math.sqrt(2.0 * math.pi)
SCALING = 32 ** (-0.5)
WIN = 6
HALF = 3
TOK = 72
SIDE = 12
FINE = 4 * TOK
LANES = 128
HIGH = 13
BLOCKS = 16
KEYS = 80
ROWS = 16
UNROLL = 12
LOOP = 4
FETCHED = 19
EARLY = 9
HALO = ((0, 64), (64, 64), (128, 32))
HALO_ROWS = 160


def merge_row(level, row, col):
    group = (row % 2) + 2 * (col % 2)
    return group * TOK + level * 36 + (row // 2) * 6 + col // 2


def window_row(level, row, col):
    window = (row // WIN) * 2 + col // WIN
    return window * TOK + level * 36 + (row % WIN) * 6 + col % WIN


def native_row(level, row, col):
    return (row * SIDE + col) * 2 + level


def permutations():
    cells = [(z, i, j) for z in range(2) for i in range(SIDE) for j in range(SIDE)]
    native_to_merge = np.zeros((FINE, FINE), np.float32)
    merge_send = np.zeros((HALO_ROWS, FINE), np.float32)
    merge_to_window = np.zeros((FINE, FINE + HALO_ROWS), np.float32)
    window_send = np.zeros((HALO_ROWS, FINE), np.float32)
    window_to_merge = np.zeros((FINE, FINE + HALO_ROWS), np.float32)
    label_row = np.zeros((FINE, 2 * SIDE), np.float32)
    label_col = np.zeros((FINE, SIDE), np.float32)
    ahead = [0, 0, 0]
    for z, i, j in cells:
        native_to_merge[merge_row(z, i, j), native_row(z, i, j)] = 1
        target = window_row(z, i, j)
        label_row[target, 2 * i + z] = 1
        label_col[target, j] = 1
        source = merge_row((z + 1) % 2, (i + HALF) % SIDE, (j + HALF) % SIDE)
        over_row, over_col = i + HALF >= SIDE, j + HALF >= SIDE
        if not over_row and not over_col:
            merge_to_window[target, source] = 1
            window_to_merge[source, target] = 1
            continue
        kind = 2 if over_row and over_col else (0 if over_row else 1)
        slot = HALO[kind][0] + ahead[kind]
        ahead[kind] += 1
        merge_send[slot, source] = 1
        merge_to_window[target, FINE + slot] = 1
        window_send[slot, target] = 1
        window_to_merge[source, FINE + slot] = 1
    coarse_native = np.zeros((TOK, TOK), np.float32)
    for z in range(2):
        for i in range(6):
            for j in range(6):
                coarse_native[z * 36 + i * 6 + j, (i * 6 + j) * 2 + z] = 1
    return (
        native_to_merge, native_to_merge.T, merge_send, merge_to_window,
        window_send, window_to_merge, coarse_native, coarse_native.T, label_row, label_col,
    )


def dot(a, b):
    return lax.dot_general(a, b, (((1,), (0,)), ((), ())), preferred_element_type=F32)


def dot_nt(a, b):
    return lax.dot_general(a, b, (((1,), (1,)), ((), ())), preferred_element_type=F32)


def dot_tn(a, b):
    return lax.dot_general(a, b, (((0,), (0,)), ((), ())), preferred_element_type=F32)


def rounded(values):
    return values.astype(BF16).astype(F32)


def layer_norm(values):
    centred = values - jnp.mean(values, axis=-1, keepdims=True)
    inverse = lax.rsqrt(jnp.mean(centred * centred, axis=-1, keepdims=True) + EPSILON)
    return centred * inverse, inverse


def norm_back(normed, inverse, upstream):
    mean_up = jnp.mean(upstream, axis=-1, keepdims=True)
    mean_cross = jnp.mean(upstream * normed, axis=-1, keepdims=True)
    return inverse * (upstream - mean_up - normed * mean_cross)


def gelu_both(pre_act):
    decay = jnp.exp(-0.5 * pre_act * pre_act)
    t = 1.0 / (1.0 + (0.3275911 * HALF_ROOT) * jnp.abs(pre_act))
    poly = 0.5 * 1.061405429
    for factor in (-1.453152027, 1.421413741, -0.284496736, 0.254829592):
        poly = poly * t + 0.5 * factor
    tail = poly * t * decay
    half = jnp.where(pre_act < 0.0, tail, 1.0 - tail)
    return pre_act * half, half + pre_act * decay * DENSITY


def head_masks(width):
    lane = lax.broadcasted_iota(jnp.int32, (1, width), 1)
    return [(lane >= 32 * h) & (lane < 32 * h + 32) for h in range(width // 32)]


def stack_heads(values, masks):
    return jnp.concatenate([jnp.where(m, values, 0.0) for m in masks], axis=0).astype(BF16)


def unstack_heads(values, masks):
    total = jnp.where(masks[0], values[:TOK], 0.0)
    for h in range(1, len(masks)):
        total = jnp.where(masks[h], values[h * TOK : (h + 1) * TOK], total)
    return total


def softmax(scores):
    weights = jnp.exp(scores - jnp.max(scores, axis=-1, keepdims=True))
    return weights * (1.0 / jnp.sum(weights, axis=-1, keepdims=True))


def table_scatter(grads, chosen, high):
    def step(p, total):
        parts = []
        for half in range(2):
            i = 2 * p + half
            rows = grads[pl.ds(i, ROWS, stride=TOK), :].astype(BF16)
            picked = jnp.broadcast_to(high[pl.ds(i, 1), :], (ROWS, LANES)).astype(BF16)
            zero = jnp.zeros_like(rows)
            parts.append(
                jnp.concatenate(
                    [jnp.where(picked == jnp.asarray(h, BF16), rows, zero) for h in range(HIGH)],
                    axis=0,
                )
            )
        return total + dot(jnp.concatenate(parts, axis=1), chosen[p])

    return lax.fori_loop(0, TOK // 2, step, jnp.zeros((HIGH * ROWS, LANES), F32), unroll=UNROLL)


def table_gather(table, out, chosen, high):
    entries = table[...].astype(BF16)

    def step(p, carry):
        spread = dot_nt(entries, chosen[p])
        for half in range(2):
            i = 2 * p + half
            picked = jnp.broadcast_to(high[pl.ds(i, 1), :], (ROWS, LANES))
            span = slice(half * LANES, (half + 1) * LANES)
            found = spread[:ROWS, span]
            for h in range(1, HIGH):
                found = jnp.where(picked == h, spread[h * ROWS : (h + 1) * ROWS, span], found)
            out[pl.ds(i, ROWS, stride=TOK), :] = found
        return carry

    lax.fori_loop(0, TOK // 2, step, 0, unroll=UNROLL)


def kernel(
    lats,
    rings,
    own_qkv, own_proj, own_up, own_down, *rest,
):
    stored, rest = rest[:FETCHED], rest[FETCHED:]
    outs, rest = rest[:4], rest[4:]
    held, rest = rest[:FETCHED], rest[FETCHED:]
    body(
        lats, rings, own_qkv, own_proj, own_up, own_down, stored, held, *held, *outs, *rest
    )


def body(
    lats, rings, own_qkv, own_proj, own_up, own_down, stored, held,
    fields, native_to_merge, merge_send, region, bias_index, fine_bias, coarse_bias,
    label_row, label_col,
    merge_to_window, fine_qkv, fine_proj, window_send, window_to_merge, fine_up, fine_down,
    merge_weight, cotangent, coarse_native,
    coarse_result, grad_result, fine_sums, coarse_sums,
    halo_out, halo_in, got_qkv, got_proj, got_up, got_down, got_cbias,
    label_rows, high, chosen, table, bias, grads_fine, grads_coarse,
    queries, keys, values, probs, score_grads, slope, first_ref, cprobs, cslope,
    spread_ref, label_ref, attended, outer_ref, qkv_grads, cqueries, ckeys, cvalues,
    part_fine, ring_fine, group_fine, final_fine,
    part_coarse, ring_coarse, group_coarse, final_coarse,
    late_sems, halo_send, halo_recv, weight_send, weight_recv, cbias_send, cbias_recv,
    fine_sems, coarse_sems,
):
    lat = lax.axis_index("lat")
    ring = lax.axis_index("lon")
    group = lax.axis_index("grp")
    column = ring * 4 + group
    columns = rings * 4

    def place(row_shift, col_shift):
        row = lax.rem(lat + row_shift + lats, lats)
        col = lax.rem(column + col_shift + columns, columns)
        return {"lat": row, "lon": lax.div(col, 4), "grp": lax.rem(col, 4)}

    before = (place(-1, 0), place(0, -1), place(-1, -1))
    after = (place(1, 0), place(0, 1), place(1, 1))
    core_mate = group + 1 - 2 * lax.rem(group, 2)
    chip_mate = lax.rem(group + 2, 4)
    far_mate = lax.rem(core_mate + 2, 4)
    mates = (core_mate, chip_mate, far_mate)

    copies = [
        pltpu.make_async_copy(source, target, late_sems.at[k])
        for k, (source, target) in enumerate(zip(stored, held))
    ]
    early, loads = copies[:EARLY], copies[EARLY:]
    owns = [
        pltpu.make_async_copy(own, got.at[0], late_sems.at[FETCHED + k])
        for k, (own, got) in enumerate(
            ((own_qkv, got_qkv), (own_proj, got_proj), (own_up, got_up), (own_down, got_down))
        )
    ]
    for copy in copies:
        copy.start()
    barrier = pltpu.get_barrier_semaphore()
    for device in before + after:
        pl.semaphore_signal(barrier, 1, device_id=device, device_id_type=MESH)
    for mate in mates:
        pl.semaphore_signal(barrier, 1, device_id={"grp": mate}, device_id_type=MESH)
    far_lat = lax.rem(lat + lats // 2, lats)
    neighbours = ({"grp": chip_mate}, {"lat": far_lat, "grp": chip_mate})
    pl.semaphore_signal(barrier, 1, device_id=neighbours[1], device_id_type=MESH)
    for step in range(1, rings):
        pl.semaphore_signal(
            barrier, 1, device_id={"lon": lax.rem(ring + step, rings)}, device_id_type=MESH
        )

    def remote(source, target, send, recv, device):
        copy = pltpu.make_async_remote_copy(
            source, target, send, recv, device_id=device, device_id_type=MESH
        )
        copy.start()
        return copy

    def send_halo(number, devices, block):
        halo_out[number] = block.astype(BF16)
        copies = []
        for kind, (start, size) in enumerate(HALO):
            rows = pl.ds(start, size)
            copies.append(
                remote(
                    halo_out.at[number, rows], halo_in.at[number, rows],
                    halo_send.at[number, kind], halo_recv.at[number, kind], devices[kind],
                )
            )
        return copies

    def wait(copies):
        for copy in copies:
            copy.wait()

    for copy in owns:
        copy.start()
    for copy in early[:3]:
        copy.wait()

    tokens = dot(native_to_merge[...], fields[...].astype(F32).reshape(FINE, 192).astype(BF16))
    tokens_half = tokens.astype(BF16)
    first_block = dot(merge_send[...], tokens_half)
    pl.semaphore_wait(barrier, 10 + rings - 1)
    pending = send_halo(0, before, first_block)

    shares = ((own_qkv, got_qkv), (own_proj, got_proj), (own_up, got_up), (own_down, got_down))
    to_chip, to_core, passed = [], [], []

    def half_of(ref, half):
        rows = ref.shape[0] // 2
        return ref.at[pl.ds(half * rows, rows)]

    for k, (own, got) in enumerate(shares):
        to_chip.append(
            [
                remote(
                    half_of(own, half), half_of(got.at[2], half),
                    weight_send.at[k, half], weight_recv.at[k, half], neighbours[half],
                )
                for half in range(2)
            ]
        )
    for k, (own, got) in enumerate(shares):
        to_core.append(
            remote(own, got.at[1], weight_send.at[k, 2], weight_recv.at[k, 2], {"grp": core_mate})
        )

    def pass_on(k):
        got = shares[k][1]
        for copy in to_chip[k]:
            copy.wait_recv()
        passed.append(
            remote(
                got.at[2], got.at[3], weight_send.at[k, 3], weight_recv.at[k, 3], {"grp": core_mate}
            )
        )

    for copy in early[3:]:
        copy.wait()
    index = bias_index[...]
    high[...] = jnp.zeros_like(high)
    high[:, :TOK] = lax.shift_right_logical(index, 7)
    low = (index & (LANES - 1)).astype(F32).astype(BF16)
    key_row = lax.broadcasted_iota(jnp.int32, (LANES, TOK), 0)
    key_col = lax.broadcasted_iota(jnp.int32, (LANES, TOK), 1)
    identity = jnp.where(key_row == key_col, 1.0, 0.0).astype(BF16)
    low_keys = jnp.where(key_row < TOK, dot_nt(identity, low), -1.0)[:KEYS].astype(BF16)
    query = lax.broadcasted_iota(jnp.int32, (TOK, 2 * LANES), 0)
    lane = lax.broadcasted_iota(jnp.int32, (TOK, 2 * LANES), 1)
    target_query = query - lax.shift_right_logical(lane, 7)
    lane = (lax.broadcasted_iota(jnp.int32, (KEYS, 2 * LANES), 1) & (LANES - 1)).astype(F32)
    blank = jnp.zeros((LANES - KEYS, LANES), BF16)

    def choose(p, carry):
        pick = jnp.where(target_query == 2 * p, 1.0, 0.0).astype(BF16)
        found = jnp.where(dot(low_keys, pick) == lane, 1.0, 0.0).astype(BF16)
        for half in range(2):
            at = half * LANES
            chosen[p, at : at + KEYS, :] = found[:, at : at + LANES]
            chosen[p, at + KEYS : at + LANES, :] = blank
        return carry

    lax.fori_loop(0, TOK // 2, choose, 0, unroll=UNROLL)
    table[...] = jnp.zeros_like(table)
    length = fine_bias.shape[2]
    for h in range(HIGH):
        size = min(LANES, length - h * LANES)
        span = slice(h * LANES, h * LANES + size)
        for head in range(6):
            at = h * ROWS + 2 * head
            table[at : at + 2, :size] = fine_bias[head, :, span].astype(F32)
        at = h * ROWS + 12
        table[at : at + 3, :size] = coarse_bias[0, :, span].astype(F32)
    table_gather(table, bias, chosen, high)
    got_cbias[0] = bias[12 * TOK : 12 * TOK + 224, :].astype(BF16)
    cbias_copies = [
        remote(got_cbias.at[0], got_cbias.at[k + 1], cbias_send.at[k], cbias_recv.at[k], {"grp": mate})
        for k, mate in enumerate(mates)
    ]
    grads_fine[...] = jnp.zeros_like(grads_fine)
    grads_coarse[...] = jnp.zeros_like(grads_coarse)

    fine_masks = head_masks(192)
    for i in range(SIDE):
        label_rows[2 * i : 2 * i + 2, :] = region[i].astype(F32)
    spread_labels = dot(label_row[...], label_rows[...].astype(BF16)) * label_col[...].astype(F32)
    col_labels = jnp.sum(spread_labels, axis=-1, keepdims=True)
    ones = jnp.ones((8, SIDE), BF16)
    spread_ref[...] = spread_labels
    label_ref[...] = col_labels
    loads[0].wait()
    loads[1].wait()
    local = dot(merge_to_window[:, :FINE], tokens_half)
    wait(pending)
    shifted = local + dot(merge_to_window[:, FINE:], halo_in[0])
    fine_normed, fine_inverse = layer_norm(shifted)
    fine_half = fine_normed.astype(BF16)
    for k, ref in enumerate((queries, keys, values)):
        ref[...] = rounded(dot(fine_half, fine_qkv[k]))

    def window_span(w):
        return pl.ds(pl.multiple_of(w * TOK, 8), TOK)

    def attend(w, carry):
        span = window_span(w)
        stacked = stack_heads(queries[span, :], fine_masks)
        scores = dot_nt(stacked, keys[span, :].astype(BF16)) * SCALING
        kind = w // 2
        scores = scores + jnp.concatenate(
            [bias[window_span(2 * h + kind), :TOK] for h in range(6)], axis=0
        )
        row_labels = dot_nt(ones, spread_ref[span, :].astype(BF16))[:1]
        allowed = label_ref[span, :] == row_labels
        scores = jnp.where(allowed[None], scores.reshape(6, TOK, TOK), NEGATIVE)
        weights = softmax(scores.reshape(6 * TOK, TOK))
        probs[w] = weights
        attended[span, :] = unstack_heads(
            dot(weights.astype(BF16), values[span, :].astype(BF16)), fine_masks
        )
        return carry

    lax.fori_loop(0, 4, attend, 0, unroll=LOOP)
    for k in range(2, 5):
        loads[k].wait()
    branch = dot(attended[...].astype(BF16), fine_proj[...]).astype(BF16)
    pending = send_halo(1, after, dot(window_send[...], branch))
    local = tokens + dot(window_to_merge[:, :FINE], branch)
    pass_on(0)
    pass_on(1)
    wait(pending)
    first = rounded(local + dot(window_to_merge[:, FINE:], halo_in[1]))
    first_ref[...] = first

    for k in range(5, 8):
        loads[k].wait()
    normed, inverse = layer_norm(first)
    hidden, slopes = gelu_both(dot(normed.astype(BF16), fine_up[...]))
    slope[...] = slopes
    second = rounded(first + dot_nt(hidden.astype(BF16), fine_down[...]))
    cells = [second[g * TOK : (g + 1) * TOK] for g in range(4)]
    width = 4 * second.shape[1]
    mean = sum(jnp.sum(c, axis=-1, keepdims=True) for c in cells) / width
    cells = [c - mean for c in cells]
    variance = sum(jnp.sum(c * c, axis=-1, keepdims=True) for c in cells) / width
    joined_inverse = lax.rsqrt(variance + EPSILON)
    cells = [c * joined_inverse for c in cells]
    merged = jnp.zeros((TOK, merge_weight.shape[1]), F32)
    for g in range(4):
        merged += dot(cells[g].astype(BF16), merge_weight[g * 192 : (g + 1) * 192, :])
    merged = rounded(merged)
    pass_on(2)
    pass_on(3)

    coarse_masks = head_masks(96)
    loads[8].wait()
    loads[9].wait()
    upstream = dot(
        coarse_native[...], cotangent[...].astype(F32).reshape(TOK, 384).astype(BF16)
    )
    base_normed, base_inverse = layer_norm(merged)
    base_half = base_normed.astype(BF16)
    wait(cbias_copies)

    def arrive(k):
        owns[k].wait()
        to_core[k].wait_recv()
        passed[k].wait_recv()

    arrive(0)
    arrive(1)

    def coarse_attend(g, total):
        q, k, v = (
            rounded(dot_nt(base_half, got_qkv[g, n * 96 : (n + 1) * 96, :])) for n in range(3)
        )
        cqueries[g] = q
        ckeys[g] = k
        cvalues[g] = v
        stacked = stack_heads(q, coarse_masks)
        scores = dot_nt(stacked, k.astype(BF16)) * SCALING
        scores = scores + got_cbias[g].astype(F32)[: 3 * TOK, :TOK]
        weights = softmax(scores)
        cprobs[g] = weights
        seen = unstack_heads(dot(weights.astype(BF16), v.astype(BF16)), coarse_masks)
        return total + dot(seen.astype(BF16), got_proj[g])

    coarse_first = rounded(lax.fori_loop(0, 4, coarse_attend, merged, unroll=LOOP))
    up_normed, up_inverse = layer_norm(coarse_first)
    up_half = up_normed.astype(BF16)
    arrive(2)
    arrive(3)

    def coarse_mlp(g, total):
        hidden, slopes = gelu_both(dot(up_half, got_up[g]))
        cslope[g] = slopes
        return total + dot(hidden.astype(BF16), got_down[g])

    total = lax.fori_loop(0, 4, coarse_mlp, coarse_first, unroll=LOOP)
    coarse_result[...] = total.astype(BF16)

    upstream_half = upstream.astype(BF16)
    blank = jnp.zeros((TOK, 384), F32)

    def coarse_mlp_back(g, total):
        grad_pre = dot_nt(upstream_half, got_down[g]) * cslope[g]
        return total + dot_nt(grad_pre.astype(BF16), got_up[g])

    total = lax.fori_loop(0, 4, coarse_mlp_back, blank, unroll=LOOP)
    grad_first = upstream + norm_back(up_normed, up_inverse, total)
    grad_half = grad_first.astype(BF16)

    def coarse_attend_back(g, total):
        stacked = stack_heads(cqueries[g], coarse_masks)
        weights = cprobs[g]
        outer = stack_heads(rounded(dot_nt(grad_half, got_proj[g])), coarse_masks)
        grad_probs = dot_nt(outer, cvalues[g].astype(BF16))
        grad_scores = weights * (
            grad_probs - jnp.sum(grad_probs * weights, axis=-1, keepdims=True)
        )
        low_bit = lax.rem(group + g, 2)
        high_bit = lax.rem(lax.div(group, 2) + lax.div(g, 2), 2)
        at = pl.multiple_of((2 * high_bit + low_bit) * (3 * TOK), 8)
        grads_coarse[pl.ds(at, 3 * TOK), :TOK] = grad_scores
        grad_scores = grad_scores.astype(BF16)
        grad_v = dot_tn(weights.astype(BF16), outer)
        grad_q = unstack_heads(dot(grad_scores, ckeys[g].astype(BF16)), coarse_masks) * SCALING
        grad_k = dot_tn(grad_scores, stacked) * SCALING
        for n, grad in enumerate((grad_q, grad_k, grad_v)):
            total = total + dot(grad.astype(BF16), got_qkv[g, n * 96 : (n + 1) * 96, :])
        return total

    total = lax.fori_loop(0, 4, coarse_attend_back, blank, unroll=LOOP)
    grad_merged = (grad_first + norm_back(base_normed, base_inverse, total)).astype(BF16)

    joined = [dot_nt(grad_merged, merge_weight[g * 192 : (g + 1) * 192, :]) for g in range(4)]
    mean_up = sum(jnp.sum(j, axis=-1, keepdims=True) for j in joined) / width
    mean_cross = (
        sum(jnp.sum(j * c, axis=-1, keepdims=True) for j, c in zip(joined, cells)) / width
    )
    grad_second = jnp.concatenate(
        [joined_inverse * (j - mean_up - c * mean_cross) for j, c in zip(joined, cells)], axis=0
    )
    grad_pre = dot(grad_second.astype(BF16), fine_down[...]) * slope[...]
    grad_normed = dot_nt(grad_pre.astype(BF16), fine_up[...])
    normed, inverse = layer_norm(first_ref[...])
    grad_fine = grad_second + norm_back(normed, inverse, grad_normed)
    first_ref[...] = grad_fine
    grad_half = grad_fine.astype(BF16)
    pending = send_halo(2, before, dot(merge_send[...], grad_half))

    share = BLOCKS * ROWS // rings

    def sum_start(sums, part, got, sems):
        sums = sums.astype(BF16)
        blank = jnp.zeros((BLOCKS * ROWS - HIGH * ROWS, LANES), BF16)
        part[...] = jnp.concatenate([sums, blank], axis=0).reshape(rings, share, LANES)
        copies = []
        for step in range(1, rings):
            peer = lax.rem(ring + step, rings)
            copies.append(
                remote(
                    part.at[peer], got.at[step], sems.at[0, step], sems.at[1, step], {"lon": peer}
                )
            )
        return copies

    def sum_group(copies, part, got, grouped, sems):
        wait(copies)
        total = part[ring].astype(F32)
        for step in range(1, rings):
            total += got[step].astype(F32)
        grouped[group] = total
        return [
            remote(
                grouped.at[group], grouped.at[group], sems.at[2, k], sems.at[3, k], {"grp": mate}
            )
            for k, mate in enumerate(mates)
        ]

    def sum_spread(copies, grouped, final, sems):
        wait(copies)
        total = grouped[0] + grouped[1] + grouped[2] + grouped[3]
        final[ring] = total.astype(BF16)
        copies = []
        for step in range(1, rings):
            peer = lax.rem(ring + step, rings)
            copies.append(
                remote(
                    final.at[ring], final.at[ring], sems.at[4, step], sems.at[5, step], {"lon": peer}
                )
            )
        return copies

    def sum_end(copies, final):
        wait(copies)
        return final[...].reshape(BLOCKS * ROWS, LANES)

    coarse_copies = sum_start(
        table_scatter(grads_coarse, chosen, high), part_coarse, ring_coarse, coarse_sems
    )

    local = dot(merge_to_window[:, :FINE], grad_half)
    wait(pending)
    grad_branch = local + dot(merge_to_window[:, FINE:], halo_in[2])
    outer_all = rounded(dot_nt(grad_branch.astype(BF16), fine_proj[...]))
    outer_ref[...] = outer_all

    def attend_back(w, carry):
        weights = probs[w]
        span = window_span(w)
        outer = stack_heads(outer_ref[span, :], fine_masks)
        grad_probs = dot_nt(outer, values[span, :].astype(BF16))
        score_grads[w] = weights * (
            grad_probs - jnp.sum(grad_probs * weights, axis=-1, keepdims=True)
        )
        return carry

    lax.fori_loop(0, 4, attend_back, 0, unroll=LOOP)
    for kind in range(2):
        both = score_grads[2 * kind] + score_grads[2 * kind + 1]
        for h in range(6):
            at = (2 * h + kind) * TOK
            grads_fine[at : at + TOK, :TOK] = both[h * TOK : (h + 1) * TOK]
    coarse_copies = sum_group(coarse_copies, part_coarse, ring_coarse, group_coarse, coarse_sems)
    fine_copies = sum_start(
        table_scatter(grads_fine, chosen, high), part_fine, ring_fine, fine_sems
    )

    def project_back(w, carry):
        span = window_span(w)
        outer = stack_heads(outer_ref[span, :], fine_masks)
        stacked = stack_heads(queries[span, :], fine_masks)
        grad_scores = score_grads[w].astype(BF16)
        grad_q = unstack_heads(dot(grad_scores, keys[span, :].astype(BF16)), fine_masks)
        qkv_grads[0, span, :] = grad_q * SCALING
        qkv_grads[1, span, :] = dot_tn(grad_scores, stacked) * SCALING
        qkv_grads[2, span, :] = dot_tn(probs[w].astype(BF16), outer)
        return carry

    lax.fori_loop(0, 4, project_back, 0, unroll=LOOP)
    coarse_copies = sum_spread(coarse_copies, group_coarse, final_coarse, coarse_sems)
    grad_normed = jnp.zeros((FINE, 192), F32)
    for n in range(3):
        grad_normed += dot_nt(qkv_grads[n].astype(BF16), fine_qkv[n])
    grad_shifted = norm_back(fine_normed, fine_inverse, grad_normed).astype(BF16)
    pending = send_halo(3, after, dot(window_send[...], grad_shifted))
    fine_copies = sum_group(fine_copies, part_fine, ring_fine, group_fine, fine_sems)
    local = first_ref[...] + dot(window_to_merge[:, :FINE], grad_shifted)
    wait(pending)
    grad = local + dot(window_to_merge[:, FINE:], halo_in[3])
    fine_copies = sum_spread(fine_copies, group_fine, final_fine, fine_sems)
    grad_result[...] = grad

    sums = sum_end(coarse_copies, final_coarse)
    row = lax.broadcasted_iota(jnp.int32, (8, ROWS), 0)
    col = lax.broadcasted_iota(jnp.int32, (8, ROWS), 1)
    chooser = jnp.where(col == row + 3 * group, 1.0, 0.0).astype(BF16)
    for h in range(HIGH):
        coarse_sums[h] = dot(chooser, sums[h * ROWS : (h + 1) * ROWS])
    for k in range(4):
        for copy in to_chip[k]:
            copy.wait_send()
        to_core[k].wait_send()
        passed[k].wait_send()
    fine_sums[...] = sum_end(fine_copies, final_fine)


def finish(
    grad_result, coarse_result, fine_sums, coarse_sums, merge_to_native, coarse_back,
    coarse_out, grad_fields, grad_fine_bias, grad_coarse_bias,
):
    grad = grad_result[...]
    upper = grad.astype(BF16)
    lower = (grad - upper.astype(F32)).astype(BF16)
    native_grad = dot(merge_to_native[...], upper) + dot(merge_to_native[...], lower)
    grad_fields[...] = native_grad.reshape(SIDE, SIDE, 2, 192)
    result = dot(coarse_back[...], coarse_result[...])
    coarse_out[...] = result.reshape(6, 6, 2, 384).astype(BF16)
    length = grad_fine_bias.shape[2]
    sums = fine_sums[...].astype(F32)
    for h in range(HIGH):
        size = min(LANES, length - h * LANES)
        span = slice(h * LANES, h * LANES + size)
        for head in range(6):
            at = h * ROWS + 2 * head
            grad_fine_bias[head, :, span] = sums[at : at + 2, :size]
        for head in range(3):
            grad_coarse_bias[head, :, span] = coarse_sums[h, head : head + 1, :size]


def shards(
    fields, region, bias_index, fine_bias, coarse_bias, fine_qkv, fine_proj, fine_up, fine_down,
    merge_weight, coarse_qkv, coarse_proj, coarse_up, coarse_down, out_cotangent,
):
    lats = lax.axis_size("lat")
    rings = lax.axis_size("lon")
    share = BLOCKS * ROWS // rings
    (
        native_to_merge, merge_to_native, merge_send, merge_to_window, window_send,
        window_to_merge, coarse_native, coarse_back, label_row, label_col,
    ) = (jnp.asarray(c, BF16) for c in permutations())
    early = (
        jnp.transpose(fields, (1, 2, 0, 3)), native_to_merge, merge_send,
        jnp.transpose(region, (1, 0, 2)), bias_index,
        jnp.transpose(fine_bias, (2, 0, 1)), jnp.transpose(coarse_bias, (0, 2, 1)),
        label_row, label_col,
    )
    owns = (
        jnp.transpose(coarse_qkv, (1, 2, 0)).reshape(3 * 96, 384), coarse_proj, coarse_up,
        coarse_down,
    )
    late = (
        merge_to_window, jnp.transpose(fine_qkv, (1, 0, 2)), fine_proj, window_send,
        window_to_merge, fine_up, fine_down.T, merge_weight,
        jnp.transpose(out_cotangent, (1, 2, 0, 3)), coarse_native,
    )
    vmem = pltpu.VMEM
    dma = pltpu.SemaphoreType.DMA
    sum_buffers = [
        vmem((rings, share, LANES), BF16),
        vmem((rings, share, LANES), BF16),
        vmem((4, share, LANES), F32),
        vmem((rings, share, LANES), BF16),
    ]
    scratch = [vmem(a.shape, a.dtype) for a in early + late]
    scratch += [
        vmem((4, HALO_ROWS, 192), BF16),
        vmem((4, HALO_ROWS, 192), BF16),
        vmem((4, 3 * 96, 384), BF16),
        vmem((4, 96, 384), BF16),
        vmem((4, 384, 384), BF16),
        vmem((4, 384, 384), BF16),
        vmem((4, 224, LANES), BF16),
        vmem((2 * SIDE, SIDE), F32),
        vmem((TOK, LANES), jnp.int32),
        vmem((TOK // 2, 2 * LANES, LANES), BF16),
        vmem((HIGH * ROWS, LANES), F32),
        vmem((ROWS * TOK, LANES), F32),
        vmem((ROWS * TOK, LANES), F32),
        vmem((ROWS * TOK, LANES), F32),
        vmem((FINE, 192), F32),
        vmem((FINE, 192), F32),
        vmem((FINE, 192), F32),
        vmem((4, 6 * TOK, TOK), F32),
        vmem((4, 6 * TOK, TOK), F32),
        vmem((FINE, 768), F32),
        vmem((FINE, 192), F32),
        vmem((4, 3 * TOK, TOK), F32),
        vmem((4, TOK, 384), F32),
        vmem((FINE, SIDE), F32),
        vmem((FINE, 1), F32),
        vmem((FINE, 192), F32),
        vmem((FINE, 192), F32),
        vmem((3, FINE, 192), F32),
        vmem((4, TOK, 96), F32),
        vmem((4, TOK, 96), F32),
        vmem((4, TOK, 96), F32),
    ]
    scratch += sum_buffers + sum_buffers
    scratch += [
        dma((FETCHED + 4,)), dma((4, 3)), dma((4, 3)), dma((4, 4)), dma((4, 4)), dma((3,)), dma((3,)),
        dma((6, BLOCKS)), dma((6, BLOCKS)),
    ]
    whole = pl.BlockSpec(memory_space=pltpu.VMEM)
    hbm = pl.BlockSpec(memory_space=pl.ANY)
    coarse_result, grad_result, fine_sums, coarse_sums = pl.pallas_call(
        functools.partial(kernel, lats, rings),
        out_shape=(
            jax.ShapeDtypeStruct((TOK, 384), BF16),
            jax.ShapeDtypeStruct((FINE, 192), F32),
            jax.ShapeDtypeStruct((BLOCKS * ROWS, LANES), BF16),
            jax.ShapeDtypeStruct((HIGH, 8, LANES), F32),
        ),
        in_specs=[hbm] * (len(owns) + FETCHED),
        out_specs=(whole,) * 4,
        scratch_shapes=scratch,
        compiler_params=pltpu.CompilerParams(
            collective_id=0, has_side_effects=True, vmem_limit_bytes=56 * 1024 * 1024
        ),
    )(*owns, *early, *late)
    outs = pl.pallas_call(
        finish,
        out_shape=(
            jax.ShapeDtypeStruct((6, 6, 2, 384), BF16),
            jax.ShapeDtypeStruct((SIDE, SIDE, 2, 192), F32),
            jax.ShapeDtypeStruct((6, 2, fine_bias.shape[1]), F32),
            jax.ShapeDtypeStruct((3, 1, fine_bias.shape[1]), F32),
        ),
        in_specs=[whole] * 6,
        out_specs=(whole,) * 4,
        compiler_params=pltpu.CompilerParams(vmem_limit_bytes=60 * 1024 * 1024),
    )(grad_result, coarse_result, fine_sums, coarse_sums, merge_to_native, coarse_back)
    return (
        jnp.transpose(outs[0], (2, 0, 1, 3)),
        jnp.transpose(outs[1], (2, 0, 1, 3)),
        jnp.transpose(outs[2], (1, 2, 0)),
        jnp.transpose(outs[3], (1, 2, 0)),
    )


def solution(mesh):
    return jax.shard_map(
        shards,
        mesh=mesh,
        in_specs=(
            P(None, "lat", ("lon", "grp"), None),
            P(None, "lat", ("lon", "grp")),
            P(),
            P("lat", None, None),
            P("lat", None, "grp"),
            P(),
            P(),
            P(),
            P(),
            P(),
            P(None, None, "grp"),
            P("grp", None),
            P(None, "grp"),
            P("grp", None),
            P(None, "lat", ("lon", "grp"), None),
        ),
        out_specs=(
            P(None, "lat", ("lon", "grp"), None),
            P(None, "lat", ("lon", "grp"), None),
            P("lat", None, None),
            P("lat", None, "grp"),
        ),
        check_vma=False,
    )
```

```python
import functools
import math

import jax
import jax.numpy as jnp
import numpy as np
from jax import lax
from jax.experimental import pallas as pl
from jax.experimental.pallas import tpu as pltpu
from jax.sharding import PartitionSpec as P

MESH = pl.DeviceIdType.MESH
F32 = jnp.float32
BF16 = jnp.bfloat16
EPSILON = 1e-05
NEGATIVE = -1e30
HALF_ROOT = 1.0 / math.sqrt(2.0)
DENSITY = 1.0 / math.sqrt(2.0 * math.pi)
SCALING = 32 ** (-0.5)
WIN = 6
HALF = 3
TOK = 72
SIDE = 12
FINE = 4 * TOK
LANES = 128
HIGH = 13
BLOCKS = 16
KEYS = 80
ROWS = 16
UNROLL = 12
LOOP = 4
FETCHED = 21
EARLY = 9
HALO = ((0, 64), (64, 64), (128, 32))
HALO_ROWS = 160


def merge_row(level, row, col):
    group = (row % 2) + 2 * (col % 2)
    return group * TOK + level * 36 + (row // 2) * 6 + col // 2


def window_row(level, row, col):
    window = (row // WIN) * 2 + col // WIN
    return window * TOK + level * 36 + (row % WIN) * 6 + col % WIN


def native_row(level, row, col):
    return (row * SIDE + col) * 2 + level


def permutations():
    cells = [(z, i, j) for z in range(2) for i in range(SIDE) for j in range(SIDE)]
    native_to_merge = np.zeros((FINE, FINE), np.float32)
    merge_send = np.zeros((HALO_ROWS, FINE), np.float32)
    merge_to_window = np.zeros((FINE, FINE + HALO_ROWS), np.float32)
    window_send = np.zeros((HALO_ROWS, FINE), np.float32)
    window_to_merge = np.zeros((FINE, FINE + HALO_ROWS), np.float32)
    label_row = np.zeros((FINE, 2 * SIDE), np.float32)
    label_col = np.zeros((FINE, SIDE), np.float32)
    ahead = [0, 0, 0]
    for z, i, j in cells:
        native_to_merge[merge_row(z, i, j), native_row(z, i, j)] = 1
        target = window_row(z, i, j)
        label_row[target, 2 * i + z] = 1
        label_col[target, j] = 1
        source = merge_row((z + 1) % 2, (i + HALF) % SIDE, (j + HALF) % SIDE)
        over_row, over_col = i + HALF >= SIDE, j + HALF >= SIDE
        if not over_row and not over_col:
            merge_to_window[target, source] = 1
            window_to_merge[source, target] = 1
            continue
        kind = 2 if over_row and over_col else (0 if over_row else 1)
        slot = HALO[kind][0] + ahead[kind]
        ahead[kind] += 1
        merge_send[slot, source] = 1
        merge_to_window[target, FINE + slot] = 1
        window_send[slot, target] = 1
        window_to_merge[source, FINE + slot] = 1
    coarse_native = np.zeros((TOK, TOK), np.float32)
    for z in range(2):
        for i in range(6):
            for j in range(6):
                coarse_native[z * 36 + i * 6 + j, (i * 6 + j) * 2 + z] = 1
    return (
        native_to_merge, native_to_merge.T, merge_send, merge_to_window,
        window_send, window_to_merge, coarse_native, coarse_native.T, label_row, label_col,
    )


def dot(a, b):
    return lax.dot_general(a, b, (((1,), (0,)), ((), ())), preferred_element_type=F32)


def dot_nt(a, b):
    return lax.dot_general(a, b, (((1,), (1,)), ((), ())), preferred_element_type=F32)


def dot_tn(a, b):
    return lax.dot_general(a, b, (((0,), (0,)), ((), ())), preferred_element_type=F32)


def rounded(values):
    return values.astype(BF16).astype(F32)


def layer_norm(values):
    centred = values - jnp.mean(values, axis=-1, keepdims=True)
    inverse = lax.rsqrt(jnp.mean(centred * centred, axis=-1, keepdims=True) + EPSILON)
    return centred * inverse, inverse


def norm_back(normed, inverse, upstream):
    mean_up = jnp.mean(upstream, axis=-1, keepdims=True)
    mean_cross = jnp.mean(upstream * normed, axis=-1, keepdims=True)
    return inverse * (upstream - mean_up - normed * mean_cross)


def gelu_both(pre_act):
    decay = jnp.exp(-0.5 * pre_act * pre_act)
    t = 1.0 / (1.0 + (0.3275911 * HALF_ROOT) * jnp.abs(pre_act))
    poly = 0.5 * 1.061405429
    for factor in (-1.453152027, 1.421413741, -0.284496736, 0.254829592):
        poly = poly * t + 0.5 * factor
    tail = poly * t * decay
    half = jnp.where(pre_act < 0.0, tail, 1.0 - tail)
    return pre_act * half, half + pre_act * decay * DENSITY


def head_masks(width):
    lane = lax.broadcasted_iota(jnp.int32, (1, width), 1)
    return [(lane >= 32 * h) & (lane < 32 * h + 32) for h in range(width // 32)]


def stack_heads(values, masks):
    return jnp.concatenate([jnp.where(m, values, 0.0) for m in masks], axis=0).astype(BF16)


def unstack_heads(values, masks):
    total = jnp.where(masks[0], values[:TOK], 0.0)
    for h in range(1, len(masks)):
        total = jnp.where(masks[h], values[h * TOK : (h + 1) * TOK], total)
    return total


def softmax(scores):
    weights = jnp.exp(scores - jnp.max(scores, axis=-1, keepdims=True))
    return weights * (1.0 / jnp.sum(weights, axis=-1, keepdims=True))


def table_scatter(grads, chosen, high):
    def step(p, total):
        parts = []
        for half in range(2):
            i = 2 * p + half
            rows = grads[pl.ds(i, ROWS, stride=TOK), :].astype(BF16)
            picked = jnp.broadcast_to(high[pl.ds(i, 1), :], (ROWS, LANES)).astype(BF16)
            zero = jnp.zeros_like(rows)
            parts.append(
                jnp.concatenate(
                    [jnp.where(picked == jnp.asarray(h, BF16), rows, zero) for h in range(HIGH)],
                    axis=0,
                )
            )
        return total + dot(jnp.concatenate(parts, axis=1), chosen[p])

    return lax.fori_loop(0, TOK // 2, step, jnp.zeros((HIGH * ROWS, LANES), F32), unroll=UNROLL)


def table_gather(table, out, chosen, high):
    entries = table[...].astype(BF16)

    def step(p, carry):
        spread = dot_nt(entries, chosen[p])
        for half in range(2):
            i = 2 * p + half
            picked = jnp.broadcast_to(high[pl.ds(i, 1), :], (ROWS, LANES))
            span = slice(half * LANES, (half + 1) * LANES)
            found = spread[:ROWS, span]
            for h in range(1, HIGH):
                found = jnp.where(picked == h, spread[h * ROWS : (h + 1) * ROWS, span], found)
            out[pl.ds(i, ROWS, stride=TOK), :] = found
        return carry

    lax.fori_loop(0, TOK // 2, step, 0, unroll=UNROLL)


def kernel(
    lats,
    rings,
    own_qkv, own_proj, own_up, own_down, *rest,
):
    stored, rest = rest[:FETCHED], rest[FETCHED:]
    outs, rest = rest[:4], rest[4:]
    held, rest = rest[:FETCHED], rest[FETCHED:]
    body(
        lats, rings, own_qkv, own_proj, own_up, own_down, stored, held, *held, *outs, *rest
    )


def body(
    lats, rings, own_qkv, own_proj, own_up, own_down, stored, held,
    fields, native_to_merge, merge_send, region, bias_index, fine_bias, coarse_bias,
    label_row, label_col,
    merge_to_window, fine_qkv, fine_proj, window_send, window_to_merge, fine_up, fine_down,
    merge_weight, cotangent, coarse_native, coarse_back, merge_to_native,
    coarse_result, grad_result, fine_sums, coarse_sums,
    halo_out, halo_in, got_qkv, got_proj, got_up, got_down, got_cbias,
    label_rows, high, chosen, table, bias, grads_fine, grads_coarse,
    queries, keys, values, probs, score_grads, slope, first_ref, cprobs, chidden, coarse_ref,
    spread_ref, label_ref, attended, outer_ref, qkv_grads, cqueries, ckeys, cvalues,
    part_fine, ring_fine, group_fine, final_fine,
    part_coarse, ring_coarse, group_coarse, final_coarse,
    late_sems, halo_send, halo_recv, weight_send, weight_recv, cbias_send, cbias_recv,
    fine_sems, coarse_sems,
):
    lat = lax.axis_index("lat")
    ring = lax.axis_index("lon")
    group = lax.axis_index("grp")
    column = ring * 4 + group
    columns = rings * 4

    def place(row_shift, col_shift):
        row = lax.rem(lat + row_shift + lats, lats)
        col = lax.rem(column + col_shift + columns, columns)
        return {"lat": row, "lon": lax.div(col, 4), "grp": lax.rem(col, 4)}

    before = (place(-1, 0), place(0, -1), place(-1, -1))
    after = (place(1, 0), place(0, 1), place(1, 1))
    core_mate = group + 1 - 2 * lax.rem(group, 2)
    chip_mate = lax.rem(group + 2, 4)
    far_mate = lax.rem(core_mate + 2, 4)
    mates = (core_mate, chip_mate, far_mate)

    copies = [
        pltpu.make_async_copy(source, target, late_sems.at[k])
        for k, (source, target) in enumerate(zip(stored, held))
    ]
    early, loads = copies[:EARLY], copies[EARLY:]
    owns = [
        pltpu.make_async_copy(own, got.at[0], late_sems.at[FETCHED + k])
        for k, (own, got) in enumerate(
            ((own_qkv, got_qkv), (own_proj, got_proj), (own_up, got_up), (own_down, got_down))
        )
    ]
    for copy in copies:
        copy.start()
    barrier = pltpu.get_barrier_semaphore()
    for device in before + after:
        pl.semaphore_signal(barrier, 1, device_id=device, device_id_type=MESH)
    for mate in mates:
        pl.semaphore_signal(barrier, 1, device_id={"grp": mate}, device_id_type=MESH)
    far_lat = lax.rem(lat + lats // 2, lats)
    neighbours = ({"grp": chip_mate}, {"lat": far_lat, "grp": chip_mate})
    pl.semaphore_signal(barrier, 1, device_id=neighbours[1], device_id_type=MESH)
    for step in range(1, rings):
        pl.semaphore_signal(
            barrier, 1, device_id={"lon": lax.rem(ring + step, rings)}, device_id_type=MESH
        )

    def remote(source, target, send, recv, device):
        copy = pltpu.make_async_remote_copy(
            source, target, send, recv, device_id=device, device_id_type=MESH
        )
        copy.start()
        return copy

    def send_halo(number, devices, block):
        halo_out[number] = block.astype(BF16)
        copies = []
        for kind, (start, size) in enumerate(HALO):
            rows = pl.ds(start, size)
            copies.append(
                remote(
                    halo_out.at[number, rows], halo_in.at[number, rows],
                    halo_send.at[number, kind], halo_recv.at[number, kind], devices[kind],
                )
            )
        return copies

    def wait(copies):
        for copy in copies:
            copy.wait()

    for copy in owns:
        copy.start()
    for copy in early[:3]:
        copy.wait()

    tokens = dot(native_to_merge[...], fields[...].astype(F32).reshape(FINE, 192).astype(BF16))
    tokens_half = tokens.astype(BF16)
    first_block = dot(merge_send[...], tokens_half)
    pl.semaphore_wait(barrier, 10 + rings - 1)
    pending = send_halo(0, before, first_block)

    shares = ((own_qkv, got_qkv), (own_proj, got_proj), (own_up, got_up), (own_down, got_down))
    to_chip, to_core, passed = [], [], []

    def half_of(ref, half):
        rows = ref.shape[0] // 2
        return ref.at[pl.ds(half * rows, rows)]

    for k, (own, got) in enumerate(shares):
        to_chip.append(
            [
                remote(
                    half_of(own, half), half_of(got.at[2], half),
                    weight_send.at[k, half], weight_recv.at[k, half], neighbours[half],
                )
                for half in range(2)
            ]
        )
    for k, (own, got) in enumerate(shares):
        to_core.append(
            remote(own, got.at[1], weight_send.at[k, 2], weight_recv.at[k, 2], {"grp": core_mate})
        )

    def pass_on(k):
        got = shares[k][1]
        for copy in to_chip[k]:
            copy.wait_recv()
        passed.append(
            remote(
                got.at[2], got.at[3], weight_send.at[k, 3], weight_recv.at[k, 3], {"grp": core_mate}
            )
        )

    for copy in early[3:]:
        copy.wait()
    index = bias_index[...]
    high[...] = jnp.zeros_like(high)
    high[:, :TOK] = lax.shift_right_logical(index, 7)
    low = (index & (LANES - 1)).astype(F32).astype(BF16)
    key_row = lax.broadcasted_iota(jnp.int32, (LANES, TOK), 0)
    key_col = lax.broadcasted_iota(jnp.int32, (LANES, TOK), 1)
    identity = jnp.where(key_row == key_col, 1.0, 0.0).astype(BF16)
    low_keys = jnp.where(key_row < TOK, dot_nt(identity, low), -1.0)[:KEYS].astype(BF16)
    query = lax.broadcasted_iota(jnp.int32, (TOK, 2 * LANES), 0)
    lane = lax.broadcasted_iota(jnp.int32, (TOK, 2 * LANES), 1)
    target_query = query - lax.shift_right_logical(lane, 7)
    lane = (lax.broadcasted_iota(jnp.int32, (KEYS, 2 * LANES), 1) & (LANES - 1)).astype(F32)
    blank = jnp.zeros((LANES - KEYS, LANES), BF16)

    def choose(p, carry):
        pick = jnp.where(target_query == 2 * p, 1.0, 0.0).astype(BF16)
        found = jnp.where(dot(low_keys, pick) == lane, 1.0, 0.0).astype(BF16)
        for half in range(2):
            at = half * LANES
            chosen[p, at : at + KEYS, :] = found[:, at : at + LANES]
            chosen[p, at + KEYS : at + LANES, :] = blank
        return carry

    lax.fori_loop(0, TOK // 2, choose, 0, unroll=UNROLL)
    table[...] = jnp.zeros_like(table)
    length = fine_bias.shape[2]
    for h in range(HIGH):
        size = min(LANES, length - h * LANES)
        span = slice(h * LANES, h * LANES + size)
        for head in range(6):
            at = h * ROWS + 2 * head
            table[at : at + 2, :size] = fine_bias[head, :, span].astype(F32)
        at = h * ROWS + 12
        table[at : at + 3, :size] = coarse_bias[0, :, span].astype(F32)
    table_gather(table, bias, chosen, high)
    got_cbias[0] = bias[12 * TOK : 12 * TOK + 224, :].astype(BF16)
    cbias_copies = [
        remote(got_cbias.at[0], got_cbias.at[k + 1], cbias_send.at[k], cbias_recv.at[k], {"grp": mate})
        for k, mate in enumerate(mates)
    ]
    grads_fine[...] = jnp.zeros_like(grads_fine)
    grads_coarse[...] = jnp.zeros_like(grads_coarse)

    fine_masks = head_masks(192)
    for i in range(SIDE):
        label_rows[2 * i : 2 * i + 2, :] = region[i].astype(F32)
    spread_labels = dot(label_row[...], label_rows[...].astype(BF16)) * label_col[...].astype(F32)
    col_labels = jnp.sum(spread_labels, axis=-1, keepdims=True)
    ones = jnp.ones((8, SIDE), BF16)
    spread_ref[...] = spread_labels
    label_ref[...] = col_labels
    loads[0].wait()
    loads[1].wait()
    local = dot(merge_to_window[:, :FINE], tokens_half)
    wait(pending)
    shifted = local + dot(merge_to_window[:, FINE:], halo_in[0])
    fine_normed, fine_inverse = layer_norm(shifted)
    fine_half = fine_normed.astype(BF16)
    for k, ref in enumerate((queries, keys, values)):
        ref[...] = rounded(dot(fine_half, fine_qkv[k]))

    def window_span(w):
        return pl.ds(pl.multiple_of(w * TOK, 8), TOK)

    def attend(w, carry):
        span = window_span(w)
        stacked = stack_heads(queries[span, :], fine_masks)
        scores = dot_nt(stacked, keys[span, :].astype(BF16)) * SCALING
        kind = w // 2
        scores = scores + jnp.concatenate(
            [bias[window_span(2 * h + kind), :TOK] for h in range(6)], axis=0
        )
        row_labels = dot_nt(ones, spread_ref[span, :].astype(BF16))[:1]
        allowed = label_ref[span, :] == row_labels
        scores = jnp.where(allowed[None], scores.reshape(6, TOK, TOK), NEGATIVE)
        weights = softmax(scores.reshape(6 * TOK, TOK))
        probs[w] = weights
        attended[span, :] = unstack_heads(
            dot(weights.astype(BF16), values[span, :].astype(BF16)), fine_masks
        )
        return carry

    lax.fori_loop(0, 4, attend, 0, unroll=LOOP)
    for k in range(2, 5):
        loads[k].wait()
    branch = dot(attended[...].astype(BF16), fine_proj[...]).astype(BF16)
    pending = send_halo(1, after, dot(window_send[...], branch))
    local = tokens + dot(window_to_merge[:, :FINE], branch)
    pass_on(0)
    pass_on(1)
    wait(pending)
    first = rounded(local + dot(window_to_merge[:, FINE:], halo_in[1]))
    first_ref[...] = first

    for k in range(5, 8):
        loads[k].wait()
    normed, inverse = layer_norm(first)
    hidden, slopes = gelu_both(dot(normed.astype(BF16), fine_up[...]))
    slope[...] = slopes
    second = rounded(first + dot_nt(hidden.astype(BF16), fine_down[...]))
    cells = [second[g * TOK : (g + 1) * TOK] for g in range(4)]
    width = 4 * second.shape[1]
    mean = sum(jnp.sum(c, axis=-1, keepdims=True) for c in cells) / width
    cells = [c - mean for c in cells]
    variance = sum(jnp.sum(c * c, axis=-1, keepdims=True) for c in cells) / width
    joined_inverse = lax.rsqrt(variance + EPSILON)
    cells = [c * joined_inverse for c in cells]
    merged = jnp.zeros((TOK, merge_weight.shape[1]), F32)
    for g in range(4):
        merged += dot(cells[g].astype(BF16), merge_weight[g * 192 : (g + 1) * 192, :])
    merged = rounded(merged)
    pass_on(2)
    pass_on(3)

    coarse_masks = head_masks(96)
    for k in range(8, 12):
        loads[k].wait()
    upstream = dot(
        coarse_native[...], cotangent[...].astype(F32).reshape(TOK, 384).astype(BF16)
    )
    base_normed, base_inverse = layer_norm(merged)
    base_half = base_normed.astype(BF16)
    wait(cbias_copies)

    def arrive(k):
        owns[k].wait()
        to_core[k].wait_recv()
        passed[k].wait_recv()

    arrive(0)
    arrive(1)

    def coarse_attend(g, total):
        q, k, v = (
            rounded(dot_nt(base_half, got_qkv[g, n * 96 : (n + 1) * 96, :])) for n in range(3)
        )
        cqueries[g] = q
        ckeys[g] = k
        cvalues[g] = v
        stacked = stack_heads(q, coarse_masks)
        scores = dot_nt(stacked, k.astype(BF16)) * SCALING
        scores = scores + got_cbias[g].astype(F32)[: 3 * TOK, :TOK]
        weights = softmax(scores)
        cprobs[g] = weights
        seen = unstack_heads(dot(weights.astype(BF16), v.astype(BF16)), coarse_masks)
        return total + dot(seen.astype(BF16), got_proj[g])

    coarse_first = rounded(lax.fori_loop(0, 4, coarse_attend, merged, unroll=LOOP))
    up_normed, up_inverse = layer_norm(coarse_first)
    up_half = up_normed.astype(BF16)
    arrive(2)
    arrive(3)

    upstream_half = upstream.astype(BF16)

    def coarse_mlp(g, total):
        hidden, slopes = gelu_both(dot(up_half, got_up[g]))
        chidden[g] = hidden.astype(BF16)
        grad_pre = dot_nt(upstream_half, got_down[g]) * slopes
        return total + dot_nt(grad_pre.astype(BF16), got_up[g])

    blank = jnp.zeros((TOK, 384), F32)
    total = lax.fori_loop(0, 4, coarse_mlp, blank, unroll=LOOP)
    coarse_ref[...] = coarse_first

    grad_first = upstream + norm_back(up_normed, up_inverse, total)
    grad_half = grad_first.astype(BF16)

    def coarse_attend_back(g, total):
        stacked = stack_heads(cqueries[g], coarse_masks)
        weights = cprobs[g]
        outer = stack_heads(rounded(dot_nt(grad_half, got_proj[g])), coarse_masks)
        grad_probs = dot_nt(outer, cvalues[g].astype(BF16))
        grad_scores = weights * (
            grad_probs - jnp.sum(grad_probs * weights, axis=-1, keepdims=True)
        )
        low_bit = lax.rem(group + g, 2)
        high_bit = lax.rem(lax.div(group, 2) + lax.div(g, 2), 2)
        at = pl.multiple_of((2 * high_bit + low_bit) * (3 * TOK), 8)
        grads_coarse[pl.ds(at, 3 * TOK), :TOK] = grad_scores
        grad_scores = grad_scores.astype(BF16)
        grad_v = dot_tn(weights.astype(BF16), outer)
        grad_q = unstack_heads(dot(grad_scores, ckeys[g].astype(BF16)), coarse_masks) * SCALING
        grad_k = dot_tn(grad_scores, stacked) * SCALING
        for n, grad in enumerate((grad_q, grad_k, grad_v)):
            total = total + dot(grad.astype(BF16), got_qkv[g, n * 96 : (n + 1) * 96, :])
        return total

    total = lax.fori_loop(0, 4, coarse_attend_back, blank, unroll=LOOP)
    grad_merged = (grad_first + norm_back(base_normed, base_inverse, total)).astype(BF16)

    joined = [dot_nt(grad_merged, merge_weight[g * 192 : (g + 1) * 192, :]) for g in range(4)]
    mean_up = sum(jnp.sum(j, axis=-1, keepdims=True) for j in joined) / width
    mean_cross = (
        sum(jnp.sum(j * c, axis=-1, keepdims=True) for j, c in zip(joined, cells)) / width
    )
    grad_second = jnp.concatenate(
        [joined_inverse * (j - mean_up - c * mean_cross) for j, c in zip(joined, cells)], axis=0
    )
    grad_pre = dot(grad_second.astype(BF16), fine_down[...]) * slope[...]
    grad_normed = dot_nt(grad_pre.astype(BF16), fine_up[...])
    normed, inverse = layer_norm(first_ref[...])
    grad_fine = grad_second + norm_back(normed, inverse, grad_normed)
    first_ref[...] = grad_fine
    grad_half = grad_fine.astype(BF16)
    pending = send_halo(2, before, dot(merge_send[...], grad_half))

    share = BLOCKS * ROWS // rings

    def sum_start(sums, part, got, sems):
        sums = sums.astype(BF16)
        blank = jnp.zeros((BLOCKS * ROWS - HIGH * ROWS, LANES), BF16)
        part[...] = jnp.concatenate([sums, blank], axis=0).reshape(rings, share, LANES)
        copies = []
        for step in range(1, rings):
            peer = lax.rem(ring + step, rings)
            copies.append(
                remote(
                    part.at[peer], got.at[step], sems.at[0, step], sems.at[1, step], {"lon": peer}
                )
            )
        return copies

    def sum_group(copies, part, got, grouped, sems):
        wait(copies)
        total = part[ring].astype(F32)
        for step in range(1, rings):
            total += got[step].astype(F32)
        grouped[group] = total
        return [
            remote(
                grouped.at[group], grouped.at[group], sems.at[2, k], sems.at[3, k], {"grp": mate}
            )
            for k, mate in enumerate(mates)
        ]

    def sum_spread(copies, grouped, final, sems):
        wait(copies)
        total = grouped[0] + grouped[1] + grouped[2] + grouped[3]
        final[ring] = total.astype(BF16)
        copies = []
        for step in range(1, rings):
            peer = lax.rem(ring + step, rings)
            copies.append(
                remote(
                    final.at[ring], final.at[ring], sems.at[4, step], sems.at[5, step], {"lon": peer}
                )
            )
        return copies

    def sum_end(copies, final):
        wait(copies)
        return final[...].reshape(BLOCKS * ROWS, LANES)

    coarse_copies = sum_start(
        table_scatter(grads_coarse, chosen, high), part_coarse, ring_coarse, coarse_sems
    )

    local = dot(merge_to_window[:, :FINE], grad_half)
    wait(pending)
    grad_branch = local + dot(merge_to_window[:, FINE:], halo_in[2])
    outer_all = rounded(dot_nt(grad_branch.astype(BF16), fine_proj[...]))
    outer_ref[...] = outer_all

    def attend_back(w, carry):
        weights = probs[w]
        span = window_span(w)
        outer = stack_heads(outer_ref[span, :], fine_masks)
        grad_probs = dot_nt(outer, values[span, :].astype(BF16))
        score_grads[w] = weights * (
            grad_probs - jnp.sum(grad_probs * weights, axis=-1, keepdims=True)
        )
        return carry

    lax.fori_loop(0, 4, attend_back, 0, unroll=LOOP)
    for kind in range(2):
        both = score_grads[2 * kind] + score_grads[2 * kind + 1]
        for h in range(6):
            at = (2 * h + kind) * TOK
            grads_fine[at : at + TOK, :TOK] = both[h * TOK : (h + 1) * TOK]
    coarse_copies = sum_group(coarse_copies, part_coarse, ring_coarse, group_coarse, coarse_sems)
    fine_copies = sum_start(
        table_scatter(grads_fine, chosen, high), part_fine, ring_fine, fine_sems
    )

    def project_back(w, carry):
        span = window_span(w)
        outer = stack_heads(outer_ref[span, :], fine_masks)
        stacked = stack_heads(queries[span, :], fine_masks)
        grad_scores = score_grads[w].astype(BF16)
        grad_q = unstack_heads(dot(grad_scores, keys[span, :].astype(BF16)), fine_masks)
        qkv_grads[0, span, :] = grad_q * SCALING
        qkv_grads[1, span, :] = dot_tn(grad_scores, stacked) * SCALING
        qkv_grads[2, span, :] = dot_tn(probs[w].astype(BF16), outer)
        return carry

    lax.fori_loop(0, 4, project_back, 0, unroll=LOOP)
    fine_copies = sum_group(fine_copies, part_fine, ring_fine, group_fine, fine_sems)
    coarse_copies = sum_spread(coarse_copies, group_coarse, final_coarse, coarse_sems)
    grad_normed = jnp.zeros((FINE, 192), F32)
    for n in range(3):
        grad_normed += dot_nt(qkv_grads[n].astype(BF16), fine_qkv[n])
    grad_shifted = norm_back(fine_normed, fine_inverse, grad_normed).astype(BF16)
    pending = send_halo(3, after, dot(window_send[...], grad_shifted))
    fine_copies = sum_spread(fine_copies, group_fine, final_fine, fine_sems)

    total = coarse_ref[...]
    for g in range(4):
        total = total + dot(chidden[g], got_down[g])
    coarse_result[...] = dot(coarse_back[...], total.astype(BF16))
    local = first_ref[...] + dot(window_to_merge[:, :FINE], grad_shifted)
    wait(pending)
    grad = local + dot(window_to_merge[:, FINE:], halo_in[3])
    upper = grad.astype(BF16)
    lower = (grad - upper.astype(F32)).astype(BF16)
    grad_result[...] = dot(merge_to_native[...], upper) + dot(merge_to_native[...], lower)

    sums = sum_end(coarse_copies, final_coarse)
    row = lax.broadcasted_iota(jnp.int32, (8, ROWS), 0)
    col = lax.broadcasted_iota(jnp.int32, (8, ROWS), 1)
    chooser = jnp.where(col == row + 3 * group, 1.0, 0.0).astype(BF16)
    for h in range(HIGH):
        coarse_sums[h] = dot(chooser, sums[h * ROWS : (h + 1) * ROWS])
    for k in range(4):
        for copy in to_chip[k]:
            copy.wait_send()
        to_core[k].wait_send()
        passed[k].wait_send()
    fine_sums[...] = sum_end(fine_copies, final_fine)


def finish(
    grad_result, coarse_result, fine_sums, coarse_sums,
    coarse_out, grad_fields, grad_fine_bias, grad_coarse_bias,
):
    grad_fields[...] = grad_result[...].reshape(SIDE, SIDE, 2, 192)
    coarse_out[...] = coarse_result[...].reshape(6, 6, 2, 384).astype(BF16)
    length = grad_fine_bias.shape[2]
    sums = fine_sums[...].astype(F32)
    for h in range(HIGH):
        size = min(LANES, length - h * LANES)
        span = slice(h * LANES, h * LANES + size)
        for head in range(6):
            at = h * ROWS + 2 * head
            grad_fine_bias[head, :, span] = sums[at : at + 2, :size]
        for head in range(3):
            grad_coarse_bias[head, :, span] = coarse_sums[h, head : head + 1, :size]


def shards(
    fields, region, bias_index, fine_bias, coarse_bias, fine_qkv, fine_proj, fine_up, fine_down,
    merge_weight, coarse_qkv, coarse_proj, coarse_up, coarse_down, out_cotangent,
):
    lats = lax.axis_size("lat")
    rings = lax.axis_size("lon")
    share = BLOCKS * ROWS // rings
    (
        native_to_merge, merge_to_native, merge_send, merge_to_window, window_send,
        window_to_merge, coarse_native, coarse_back, label_row, label_col,
    ) = (jnp.asarray(c, BF16) for c in permutations())
    early = (
        jnp.transpose(fields, (1, 2, 0, 3)), native_to_merge, merge_send,
        jnp.transpose(region, (1, 0, 2)), bias_index,
        jnp.transpose(fine_bias, (2, 0, 1)), jnp.transpose(coarse_bias, (0, 2, 1)),
        label_row, label_col,
    )
    owns = (
        jnp.transpose(coarse_qkv, (1, 2, 0)).reshape(3 * 96, 384), coarse_proj, coarse_up,
        coarse_down,
    )
    late = (
        merge_to_window, jnp.transpose(fine_qkv, (1, 0, 2)), fine_proj, window_send,
        window_to_merge, fine_up, fine_down.T, merge_weight,
        jnp.transpose(out_cotangent, (1, 2, 0, 3)), coarse_native, coarse_back,
        merge_to_native,
    )
    vmem = pltpu.VMEM
    dma = pltpu.SemaphoreType.DMA
    sum_buffers = [
        vmem((rings, share, LANES), BF16),
        vmem((rings, share, LANES), BF16),
        vmem((4, share, LANES), F32),
        vmem((rings, share, LANES), BF16),
    ]
    scratch = [vmem(a.shape, a.dtype) for a in early + late]
    scratch += [
        vmem((4, HALO_ROWS, 192), BF16),
        vmem((4, HALO_ROWS, 192), BF16),
        vmem((4, 3 * 96, 384), BF16),
        vmem((4, 96, 384), BF16),
        vmem((4, 384, 384), BF16),
        vmem((4, 384, 384), BF16),
        vmem((4, 224, LANES), BF16),
        vmem((2 * SIDE, SIDE), F32),
        vmem((TOK, LANES), jnp.int32),
        vmem((TOK // 2, 2 * LANES, LANES), BF16),
        vmem((HIGH * ROWS, LANES), F32),
        vmem((ROWS * TOK, LANES), F32),
        vmem((ROWS * TOK, LANES), F32),
        vmem((ROWS * TOK, LANES), F32),
        vmem((FINE, 192), F32),
        vmem((FINE, 192), F32),
        vmem((FINE, 192), F32),
        vmem((4, 6 * TOK, TOK), F32),
        vmem((4, 6 * TOK, TOK), F32),
        vmem((FINE, 768), F32),
        vmem((FINE, 192), F32),
        vmem((4, 3 * TOK, TOK), F32),
        vmem((4, TOK, 384), BF16),
        vmem((TOK, 384), F32),
        vmem((FINE, SIDE), F32),
        vmem((FINE, 1), F32),
        vmem((FINE, 192), F32),
        vmem((FINE, 192), F32),
        vmem((3, FINE, 192), F32),
        vmem((4, TOK, 96), F32),
        vmem((4, TOK, 96), F32),
        vmem((4, TOK, 96), F32),
    ]
    scratch += sum_buffers + sum_buffers
    scratch += [
        dma((FETCHED + 4,)), dma((4, 3)), dma((4, 3)), dma((4, 4)), dma((4, 4)), dma((3,)), dma((3,)),
        dma((6, BLOCKS)), dma((6, BLOCKS)),
    ]
    whole = pl.BlockSpec(memory_space=pltpu.VMEM)
    hbm = pl.BlockSpec(memory_space=pl.ANY)
    coarse_result, grad_result, fine_sums, coarse_sums = pl.pallas_call(
        functools.partial(kernel, lats, rings),
        out_shape=(
            jax.ShapeDtypeStruct((TOK, 384), F32),
            jax.ShapeDtypeStruct((FINE, 192), F32),
            jax.ShapeDtypeStruct((BLOCKS * ROWS, LANES), BF16),
            jax.ShapeDtypeStruct((HIGH, 8, LANES), F32),
        ),
        in_specs=[hbm] * (len(owns) + FETCHED),
        out_specs=(whole,) * 4,
        scratch_shapes=scratch,
        compiler_params=pltpu.CompilerParams(
            collective_id=0, has_side_effects=True, vmem_limit_bytes=56 * 1024 * 1024
        ),
    )(*owns, *early, *late)
    outs = pl.pallas_call(
        finish,
        out_shape=(
            jax.ShapeDtypeStruct((6, 6, 2, 384), BF16),
            jax.ShapeDtypeStruct((SIDE, SIDE, 2, 192), F32),
            jax.ShapeDtypeStruct((6, 2, fine_bias.shape[1]), F32),
            jax.ShapeDtypeStruct((3, 1, fine_bias.shape[1]), F32),
        ),
        in_specs=[whole] * 4,
        out_specs=(whole,) * 4,
        compiler_params=pltpu.CompilerParams(vmem_limit_bytes=60 * 1024 * 1024),
    )(grad_result, coarse_result, fine_sums, coarse_sums)
    return (
        jnp.transpose(outs[0], (2, 0, 1, 3)),
        jnp.transpose(outs[1], (2, 0, 1, 3)),
        jnp.transpose(outs[2], (1, 2, 0)),
        jnp.transpose(outs[3], (1, 2, 0)),
    )


def solution(mesh):
    return jax.shard_map(
        shards,
        mesh=mesh,
        in_specs=(
            P(None, "lat", ("lon", "grp"), None),
            P(None, "lat", ("lon", "grp")),
            P(),
            P("lat", None, None),
            P("lat", None, "grp"),
            P(),
            P(),
            P(),
            P(),
            P(),
            P(None, None, "grp"),
            P("grp", None),
            P(None, "grp"),
            P("grp", None),
            P(None, "lat", ("lon", "grp"), None),
        ),
        out_specs=(
            P(None, "lat", ("lon", "grp"), None),
            P(None, "lat", ("lon", "grp"), None),
            P("lat", None, None),
            P("lat", None, "grp"),
        ),
        check_vma=False,
    )
```

```python
import functools
import math

import jax
import jax.numpy as jnp
import numpy as np
from jax import lax
from jax.experimental import pallas as pl
from jax.experimental.pallas import tpu as pltpu
from jax.sharding import PartitionSpec as P

MESH = pl.DeviceIdType.MESH
F32 = jnp.float32
BF16 = jnp.bfloat16
EPSILON = 1e-05
NEGATIVE = -1e30
HALF_ROOT = 1.0 / math.sqrt(2.0)
DENSITY = 1.0 / math.sqrt(2.0 * math.pi)
SCALING = 32 ** (-0.5)
WIN = 6
HALF = 3
TOK = 72
SIDE = 12
FINE = 4 * TOK
LANES = 128
HIGH = 13
BLOCKS = 16
KEYS = 80
ROWS = 16
UNROLL = 12
LOOP = 4
FETCHED = 21
EARLY = 9
HALO = ((0, 64), (64, 64), (128, 32))
HALO_ROWS = 160


def merge_row(level, row, col):
    group = (row % 2) + 2 * (col % 2)
    return group * TOK + level * 36 + (row // 2) * 6 + col // 2


def window_row(level, row, col):
    window = (row // WIN) * 2 + col // WIN
    return window * TOK + level * 36 + (row % WIN) * 6 + col % WIN


def native_row(level, row, col):
    return (row * SIDE + col) * 2 + level


def permutations():
    cells = [(z, i, j) for z in range(2) for i in range(SIDE) for j in range(SIDE)]
    native_to_merge = np.zeros((FINE, FINE), np.float32)
    merge_send = np.zeros((HALO_ROWS, FINE), np.float32)
    merge_to_window = np.zeros((FINE, FINE + HALO_ROWS), np.float32)
    window_send = np.zeros((HALO_ROWS, FINE), np.float32)
    window_to_merge = np.zeros((FINE, FINE + HALO_ROWS), np.float32)
    label_row = np.zeros((FINE, 2 * SIDE), np.float32)
    label_col = np.zeros((FINE, SIDE), np.float32)
    ahead = [0, 0, 0]
    for z, i, j in cells:
        native_to_merge[merge_row(z, i, j), native_row(z, i, j)] = 1
        target = window_row(z, i, j)
        label_row[target, 2 * i + z] = 1
        label_col[target, j] = 1
        source = merge_row((z + 1) % 2, (i + HALF) % SIDE, (j + HALF) % SIDE)
        over_row, over_col = i + HALF >= SIDE, j + HALF >= SIDE
        if not over_row and not over_col:
            merge_to_window[target, source] = 1
            window_to_merge[source, target] = 1
            continue
        kind = 2 if over_row and over_col else (0 if over_row else 1)
        slot = HALO[kind][0] + ahead[kind]
        ahead[kind] += 1
        merge_send[slot, source] = 1
        merge_to_window[target, FINE + slot] = 1
        window_send[slot, target] = 1
        window_to_merge[source, FINE + slot] = 1
    coarse_native = np.zeros((TOK, TOK), np.float32)
    for z in range(2):
        for i in range(6):
            for j in range(6):
                coarse_native[z * 36 + i * 6 + j, (i * 6 + j) * 2 + z] = 1
    return (
        native_to_merge, native_to_merge.T, merge_send, merge_to_window,
        window_send, window_to_merge, coarse_native, coarse_native.T, label_row, label_col,
    )


def dot(a, b):
    return lax.dot_general(a, b, (((1,), (0,)), ((), ())), preferred_element_type=F32)


def dot_nt(a, b):
    return lax.dot_general(a, b, (((1,), (1,)), ((), ())), preferred_element_type=F32)


def dot_tn(a, b):
    return lax.dot_general(a, b, (((0,), (0,)), ((), ())), preferred_element_type=F32)


def rounded(values):
    return values.astype(BF16).astype(F32)


def layer_norm(values):
    centred = values - jnp.mean(values, axis=-1, keepdims=True)
    inverse = lax.rsqrt(jnp.mean(centred * centred, axis=-1, keepdims=True) + EPSILON)
    return centred * inverse, inverse


def norm_back(normed, inverse, upstream):
    mean_up = jnp.mean(upstream, axis=-1, keepdims=True)
    mean_cross = jnp.mean(upstream * normed, axis=-1, keepdims=True)
    return inverse * (upstream - mean_up - normed * mean_cross)


def gelu_both(pre_act):
    decay = jnp.exp(-0.5 * pre_act * pre_act)
    t = 1.0 / (1.0 + (0.3275911 * HALF_ROOT) * jnp.abs(pre_act))
    poly = 0.5 * 1.061405429
    for factor in (-1.453152027, 1.421413741, -0.284496736, 0.254829592):
        poly = poly * t + 0.5 * factor
    tail = poly * t * decay
    half = jnp.where(pre_act < 0.0, tail, 1.0 - tail)
    return pre_act * half, half + pre_act * decay * DENSITY


def head_masks(width):
    lane = lax.broadcasted_iota(jnp.int32, (1, width), 1)
    return [(lane >= 32 * h) & (lane < 32 * h + 32) for h in range(width // 32)]


def stack_heads(values, masks):
    return jnp.concatenate([jnp.where(m, values, 0.0) for m in masks], axis=0).astype(BF16)


def unstack_heads(values, masks):
    total = jnp.where(masks[0], values[:TOK], 0.0)
    for h in range(1, len(masks)):
        total = jnp.where(masks[h], values[h * TOK : (h + 1) * TOK], total)
    return total


def softmax(scores):
    weights = jnp.exp(scores - jnp.max(scores, axis=-1, keepdims=True))
    return weights * (1.0 / jnp.sum(weights, axis=-1, keepdims=True))


def table_scatter(grads, chosen, high):
    def step(p, total):
        parts = []
        for half in range(2):
            i = 2 * p + half
            rows = grads[pl.ds(i, ROWS, stride=TOK), :].astype(BF16)
            picked = jnp.broadcast_to(high[pl.ds(i, 1), :], (ROWS, LANES)).astype(BF16)
            zero = jnp.zeros_like(rows)
            parts.append(
                jnp.concatenate(
                    [jnp.where(picked == jnp.asarray(h, BF16), rows, zero) for h in range(HIGH)],
                    axis=0,
                )
            )
        return total + dot(jnp.concatenate(parts, axis=1), chosen[p])

    return lax.fori_loop(0, TOK // 2, step, jnp.zeros((HIGH * ROWS, LANES), F32), unroll=UNROLL)


def table_gather(table, out, chosen, high):
    entries = table[...].astype(BF16)

    def step(p, carry):
        spread = dot_nt(entries, chosen[p])
        for half in range(2):
            i = 2 * p + half
            picked = jnp.broadcast_to(high[pl.ds(i, 1), :], (ROWS, LANES))
            span = slice(half * LANES, (half + 1) * LANES)
            found = spread[:ROWS, span]
            for h in range(1, HIGH):
                found = jnp.where(picked == h, spread[h * ROWS : (h + 1) * ROWS, span], found)
            out[pl.ds(i, ROWS, stride=TOK), :] = found
        return carry

    lax.fori_loop(0, TOK // 2, step, 0, unroll=UNROLL)


def kernel(
    lats,
    rings,
    own_qkv, own_proj, own_up, own_down, *rest,
):
    stored, rest = rest[:FETCHED], rest[FETCHED:]
    outs, rest = rest[:4], rest[4:]
    held, rest = rest[:FETCHED], rest[FETCHED:]
    body(
        lats, rings, own_qkv, own_proj, own_up, own_down, stored, held, *held, *outs, *rest
    )


def body(
    lats, rings, own_qkv, own_proj, own_up, own_down, stored, held,
    fields, native_to_merge, merge_send, region, bias_index, fine_bias, coarse_bias,
    label_row, label_col,
    merge_to_window, fine_qkv, fine_proj, window_send, window_to_merge, fine_up, fine_down,
    merge_weight, cotangent, coarse_native, coarse_back, merge_to_native,
    coarse_result, grad_result, fine_sums, coarse_sums,
    halo_out, halo_in, got_qkv, got_proj, got_up, got_down, got_cbias,
    label_rows, high, chosen, table, bias, grads_fine, grads_coarse,
    queries, keys, values, probs, score_grads, slope, first_ref, cprobs, chidden, coarse_ref,
    spread_ref, label_ref, attended, outer_ref, qkv_grads, cqueries, ckeys, cvalues,
    part_fine, ring_fine, group_fine, final_fine,
    part_coarse, ring_coarse, group_coarse, final_coarse,
    late_sems, halo_send, halo_recv, weight_send, weight_recv, cbias_send, cbias_recv,
    fine_sems, coarse_sems,
):
    lat = lax.axis_index("lat")
    ring = lax.axis_index("lon")
    group = lax.axis_index("grp")
    column = ring * 4 + group
    columns = rings * 4

    def place(row_shift, col_shift):
        row = lax.rem(lat + row_shift + lats, lats)
        col = lax.rem(column + col_shift + columns, columns)
        return {"lat": row, "lon": lax.div(col, 4), "grp": lax.rem(col, 4)}

    before = (place(-1, 0), place(0, -1), place(-1, -1))
    after = (place(1, 0), place(0, 1), place(1, 1))
    core_mate = group + 1 - 2 * lax.rem(group, 2)
    chip_mate = lax.rem(group + 2, 4)
    far_mate = lax.rem(core_mate + 2, 4)
    mates = (core_mate, chip_mate, far_mate)

    copies = [
        pltpu.make_async_copy(source, target, late_sems.at[k])
        for k, (source, target) in enumerate(zip(stored, held))
    ]
    early, loads = copies[:EARLY], copies[EARLY:]
    owns = [
        pltpu.make_async_copy(own, got.at[0], late_sems.at[FETCHED + k])
        for k, (own, got) in enumerate(
            ((own_qkv, got_qkv), (own_proj, got_proj), (own_up, got_up), (own_down, got_down))
        )
    ]
    for copy in copies:
        copy.start()
    barrier = pltpu.get_barrier_semaphore()
    for device in before + after:
        pl.semaphore_signal(barrier, 1, device_id=device, device_id_type=MESH)
    for mate in mates:
        pl.semaphore_signal(barrier, 1, device_id={"grp": mate}, device_id_type=MESH)
    far_lat = lax.rem(lat + lats // 2, lats)
    neighbours = ({"grp": chip_mate}, {"lat": far_lat, "grp": chip_mate})
    pl.semaphore_signal(barrier, 1, device_id=neighbours[1], device_id_type=MESH)
    for step in range(1, rings):
        pl.semaphore_signal(
            barrier, 1, device_id={"lon": lax.rem(ring + step, rings)}, device_id_type=MESH
        )

    def remote(source, target, send, recv, device):
        copy = pltpu.make_async_remote_copy(
            source, target, send, recv, device_id=device, device_id_type=MESH
        )
        copy.start()
        return copy

    def together(sent, got, send, recv):
        return pltpu.make_async_remote_copy(
            sent, got, send, recv, device_id={"grp": core_mate}, device_id_type=MESH
        )

    def send_halo(number, devices, block):
        halo_out[number] = block.astype(BF16)
        for kind, (start, size) in enumerate(HALO):
            rows = pl.ds(start, size)
            remote(
                halo_out.at[number, rows], halo_in.at[number, rows],
                halo_send.at[number], halo_recv.at[number], devices[kind],
            )
        return [
            together(
                halo_out.at[number], halo_in.at[number], halo_send.at[number], halo_recv.at[number]
            )
        ]

    def wait(copies):
        for copy in copies:
            copy.wait()

    for copy in owns:
        copy.start()
    for copy in early[:3]:
        copy.wait()

    tokens = dot(native_to_merge[...], fields[...].astype(F32).reshape(FINE, 192).astype(BF16))
    tokens_half = tokens.astype(BF16)
    first_block = dot(merge_send[...], tokens_half)
    pl.semaphore_wait(barrier, 10 + rings - 1)
    pending = send_halo(0, before, first_block)

    shares = ((own_qkv, got_qkv), (own_proj, got_proj), (own_up, got_up), (own_down, got_down))
    to_chip, to_core, passed = [], [], []

    def half_of(ref, half):
        rows = ref.shape[0] // 2
        return ref.at[pl.ds(half * rows, rows)]

    for k, (own, got) in enumerate(shares):
        to_chip.append(
            [
                remote(
                    half_of(own, half), half_of(got.at[2], half),
                    weight_send.at[k, half], weight_recv.at[k, half], neighbours[half],
                )
                for half in range(2)
            ]
        )
    for k, (own, got) in enumerate(shares):
        to_core.append(
            remote(own, got.at[1], weight_send.at[k, 2], weight_recv.at[k, 2], {"grp": core_mate})
        )

    def pass_on(k):
        got = shares[k][1]
        for copy in to_chip[k]:
            copy.wait_recv()
        passed.append(
            remote(
                got.at[2], got.at[3], weight_send.at[k, 3], weight_recv.at[k, 3], {"grp": core_mate}
            )
        )

    for copy in early[3:]:
        copy.wait()
    index = bias_index[...]
    high[...] = jnp.zeros_like(high)
    high[:, :TOK] = lax.shift_right_logical(index, 7)
    low = (index & (LANES - 1)).astype(F32).astype(BF16)
    key_row = lax.broadcasted_iota(jnp.int32, (LANES, TOK), 0)
    key_col = lax.broadcasted_iota(jnp.int32, (LANES, TOK), 1)
    identity = jnp.where(key_row == key_col, 1.0, 0.0).astype(BF16)
    low_keys = jnp.where(key_row < TOK, dot_nt(identity, low), -1.0)[:KEYS].astype(BF16)
    query = lax.broadcasted_iota(jnp.int32, (TOK, 2 * LANES), 0)
    lane = lax.broadcasted_iota(jnp.int32, (TOK, 2 * LANES), 1)
    target_query = query - lax.shift_right_logical(lane, 7)
    lane = (lax.broadcasted_iota(jnp.int32, (KEYS, 2 * LANES), 1) & (LANES - 1)).astype(F32)
    blank = jnp.zeros((LANES - KEYS, LANES), BF16)

    def choose(p, carry):
        pick = jnp.where(target_query == 2 * p, 1.0, 0.0).astype(BF16)
        found = jnp.where(dot(low_keys, pick) == lane, 1.0, 0.0).astype(BF16)
        for half in range(2):
            at = half * LANES
            chosen[p, at : at + KEYS, :] = found[:, at : at + LANES]
            chosen[p, at + KEYS : at + LANES, :] = blank
        return carry

    lax.fori_loop(0, TOK // 2, choose, 0, unroll=UNROLL)
    table[...] = jnp.zeros_like(table)
    length = fine_bias.shape[2]
    for h in range(HIGH):
        size = min(LANES, length - h * LANES)
        span = slice(h * LANES, h * LANES + size)
        for head in range(6):
            at = h * ROWS + 2 * head
            table[at : at + 2, :size] = fine_bias[head, :, span].astype(F32)
        at = h * ROWS + 12
        table[at : at + 3, :size] = coarse_bias[0, :, span].astype(F32)
    table_gather(table, bias, chosen, high)
    got_cbias[0] = bias[12 * TOK : 12 * TOK + 224, :].astype(BF16)
    cbias_copies = [
        remote(got_cbias.at[0], got_cbias.at[k + 1], cbias_send.at[k], cbias_recv.at[k], {"grp": mate})
        for k, mate in enumerate(mates)
    ]
    grads_fine[...] = jnp.zeros_like(grads_fine)
    grads_coarse[...] = jnp.zeros_like(grads_coarse)

    fine_masks = head_masks(192)
    for i in range(SIDE):
        label_rows[2 * i : 2 * i + 2, :] = region[i].astype(F32)
    spread_labels = dot(label_row[...], label_rows[...].astype(BF16)) * label_col[...].astype(F32)
    col_labels = jnp.sum(spread_labels, axis=-1, keepdims=True)
    ones = jnp.ones((8, SIDE), BF16)
    spread_ref[...] = spread_labels
    label_ref[...] = col_labels
    loads[0].wait()
    loads[1].wait()
    local = dot(merge_to_window[:, :FINE], tokens_half)
    wait(pending)
    shifted = local + dot(merge_to_window[:, FINE:], halo_in[0])
    fine_normed, fine_inverse = layer_norm(shifted)
    fine_half = fine_normed.astype(BF16)
    for k, ref in enumerate((queries, keys, values)):
        ref[...] = rounded(dot(fine_half, fine_qkv[k]))

    def window_span(w):
        return pl.ds(pl.multiple_of(w * TOK, 8), TOK)

    def attend(w, carry):
        span = window_span(w)
        stacked = stack_heads(queries[span, :], fine_masks)
        scores = dot_nt(stacked, keys[span, :].astype(BF16)) * SCALING
        kind = w // 2
        scores = scores + jnp.concatenate(
            [bias[window_span(2 * h + kind), :TOK] for h in range(6)], axis=0
        )
        row_labels = dot_nt(ones, spread_ref[span, :].astype(BF16))[:1]
        allowed = label_ref[span, :] == row_labels
        scores = jnp.where(allowed[None], scores.reshape(6, TOK, TOK), NEGATIVE)
        weights = softmax(scores.reshape(6 * TOK, TOK))
        probs[w] = weights
        attended[span, :] = unstack_heads(
            dot(weights.astype(BF16), values[span, :].astype(BF16)), fine_masks
        )
        return carry

    lax.fori_loop(0, 4, attend, 0, unroll=LOOP)
    for k in range(2, 5):
        loads[k].wait()
    branch = dot(attended[...].astype(BF16), fine_proj[...]).astype(BF16)
    pending = send_halo(1, after, dot(window_send[...], branch))
    local = tokens + dot(window_to_merge[:, :FINE], branch)
    pass_on(0)
    pass_on(1)
    wait(pending)
    first = rounded(local + dot(window_to_merge[:, FINE:], halo_in[1]))
    first_ref[...] = first

    for k in range(5, 8):
        loads[k].wait()
    normed, inverse = layer_norm(first)
    hidden, slopes = gelu_both(dot(normed.astype(BF16), fine_up[...]))
    slope[...] = slopes
    second = rounded(first + dot_nt(hidden.astype(BF16), fine_down[...]))
    cells = [second[g * TOK : (g + 1) * TOK] for g in range(4)]
    width = 4 * second.shape[1]
    mean = sum(jnp.sum(c, axis=-1, keepdims=True) for c in cells) / width
    cells = [c - mean for c in cells]
    variance = sum(jnp.sum(c * c, axis=-1, keepdims=True) for c in cells) / width
    joined_inverse = lax.rsqrt(variance + EPSILON)
    cells = [c * joined_inverse for c in cells]
    merged = jnp.zeros((TOK, merge_weight.shape[1]), F32)
    for g in range(4):
        merged += dot(cells[g].astype(BF16), merge_weight[g * 192 : (g + 1) * 192, :])
    merged = rounded(merged)
    pass_on(2)
    pass_on(3)

    coarse_masks = head_masks(96)
    for k in range(8, 12):
        loads[k].wait()
    upstream = dot(
        coarse_native[...], cotangent[...].astype(F32).reshape(TOK, 384).astype(BF16)
    )
    base_normed, base_inverse = layer_norm(merged)
    base_half = base_normed.astype(BF16)
    wait(cbias_copies)

    def arrive(k):
        owns[k].wait()
        to_core[k].wait_recv()
        passed[k].wait_recv()

    arrive(0)
    arrive(1)

    def coarse_attend(g, total):
        q, k, v = (
            rounded(dot_nt(base_half, got_qkv[g, n * 96 : (n + 1) * 96, :])) for n in range(3)
        )
        cqueries[g] = q
        ckeys[g] = k
        cvalues[g] = v
        stacked = stack_heads(q, coarse_masks)
        scores = dot_nt(stacked, k.astype(BF16)) * SCALING
        scores = scores + got_cbias[g].astype(F32)[: 3 * TOK, :TOK]
        weights = softmax(scores)
        cprobs[g] = weights
        seen = unstack_heads(dot(weights.astype(BF16), v.astype(BF16)), coarse_masks)
        return total + dot(seen.astype(BF16), got_proj[g])

    coarse_first = rounded(lax.fori_loop(0, 4, coarse_attend, merged, unroll=LOOP))
    up_normed, up_inverse = layer_norm(coarse_first)
    up_half = up_normed.astype(BF16)
    arrive(2)
    arrive(3)

    upstream_half = upstream.astype(BF16)

    def coarse_mlp(g, total):
        hidden, slopes = gelu_both(dot(up_half, got_up[g]))
        chidden[g] = hidden.astype(BF16)
        grad_pre = dot_nt(upstream_half, got_down[g]) * slopes
        return total + dot_nt(grad_pre.astype(BF16), got_up[g])

    blank = jnp.zeros((TOK, 384), F32)
    total = lax.fori_loop(0, 4, coarse_mlp, blank, unroll=LOOP)
    coarse_ref[...] = coarse_first

    grad_first = upstream + norm_back(up_normed, up_inverse, total)
    grad_half = grad_first.astype(BF16)

    def coarse_attend_back(g, total):
        stacked = stack_heads(cqueries[g], coarse_masks)
        weights = cprobs[g]
        outer = stack_heads(rounded(dot_nt(grad_half, got_proj[g])), coarse_masks)
        grad_probs = dot_nt(outer, cvalues[g].astype(BF16))
        grad_scores = weights * (
            grad_probs - jnp.sum(grad_probs * weights, axis=-1, keepdims=True)
        )
        low_bit = lax.rem(group + g, 2)
        high_bit = lax.rem(lax.div(group, 2) + lax.div(g, 2), 2)
        at = pl.multiple_of((2 * high_bit + low_bit) * (3 * TOK), 8)
        grads_coarse[pl.ds(at, 3 * TOK), :TOK] = grad_scores
        grad_scores = grad_scores.astype(BF16)
        grad_v = dot_tn(weights.astype(BF16), outer)
        grad_q = unstack_heads(dot(grad_scores, ckeys[g].astype(BF16)), coarse_masks) * SCALING
        grad_k = dot_tn(grad_scores, stacked) * SCALING
        for n, grad in enumerate((grad_q, grad_k, grad_v)):
            total = total + dot(grad.astype(BF16), got_qkv[g, n * 96 : (n + 1) * 96, :])
        return total

    total = lax.fori_loop(0, 4, coarse_attend_back, blank, unroll=LOOP)
    grad_merged = (grad_first + norm_back(base_normed, base_inverse, total)).astype(BF16)

    joined = [dot_nt(grad_merged, merge_weight[g * 192 : (g + 1) * 192, :]) for g in range(4)]
    mean_up = sum(jnp.sum(j, axis=-1, keepdims=True) for j in joined) / width
    mean_cross = (
        sum(jnp.sum(j * c, axis=-1, keepdims=True) for j, c in zip(joined, cells)) / width
    )
    grad_second = jnp.concatenate(
        [joined_inverse * (j - mean_up - c * mean_cross) for j, c in zip(joined, cells)], axis=0
    )
    grad_pre = dot(grad_second.astype(BF16), fine_down[...]) * slope[...]
    grad_normed = dot_nt(grad_pre.astype(BF16), fine_up[...])
    normed, inverse = layer_norm(first_ref[...])
    grad_fine = grad_second + norm_back(normed, inverse, grad_normed)
    first_ref[...] = grad_fine
    grad_half = grad_fine.astype(BF16)
    pending = send_halo(2, before, dot(merge_send[...], grad_half))

    share = BLOCKS * ROWS // rings

    def sum_start(sums, part, got, sems):
        sums = sums.astype(BF16)
        blank = jnp.zeros((BLOCKS * ROWS - HIGH * ROWS, LANES), BF16)
        part[...] = jnp.concatenate([sums, blank], axis=0).reshape(rings, share, LANES)
        for step in range(1, rings):
            peer = lax.rem(ring + step, rings)
            remote(part.at[peer], got.at[step], sems.at[0], sems.at[1], {"lon": peer})
        others = pl.ds(1, rings - 1)
        return [together(part.at[others], got.at[others], sems.at[0], sems.at[1])]

    def sum_group(copies, part, got, grouped, sems):
        wait(copies)
        total = part[ring].astype(F32) + jnp.sum(got[1:].astype(F32), axis=0)
        grouped[group] = total
        for mate in mates:
            remote(grouped.at[group], grouped.at[group], sems.at[2], sems.at[3], {"grp": mate})
        others = pl.ds(0, 3)
        return [together(grouped.at[others], grouped.at[others], sems.at[2], sems.at[3])]

    def sum_spread(copies, grouped, final, sems):
        wait(copies)
        total = grouped[0] + grouped[1] + grouped[2] + grouped[3]
        final[ring] = total.astype(BF16)
        for step in range(1, rings):
            peer = lax.rem(ring + step, rings)
            remote(final.at[ring], final.at[ring], sems.at[4], sems.at[5], {"lon": peer})
        others = pl.ds(0, rings - 1)
        return [together(final.at[others], final.at[others], sems.at[4], sems.at[5])]

    def sum_end(copies, final):
        wait(copies)
        return final[...].reshape(BLOCKS * ROWS, LANES)

    coarse_copies = sum_start(
        table_scatter(grads_coarse, chosen, high), part_coarse, ring_coarse, coarse_sems
    )

    local = dot(merge_to_window[:, :FINE], grad_half)
    wait(pending)
    grad_branch = local + dot(merge_to_window[:, FINE:], halo_in[2])
    outer_all = rounded(dot_nt(grad_branch.astype(BF16), fine_proj[...]))
    outer_ref[...] = outer_all

    def attend_back(w, carry):
        weights = probs[w]
        span = window_span(w)
        outer = stack_heads(outer_ref[span, :], fine_masks)
        grad_probs = dot_nt(outer, values[span, :].astype(BF16))
        score_grads[w] = weights * (
            grad_probs - jnp.sum(grad_probs * weights, axis=-1, keepdims=True)
        )
        return carry

    lax.fori_loop(0, 4, attend_back, 0, unroll=LOOP)
    for kind in range(2):
        both = score_grads[2 * kind] + score_grads[2 * kind + 1]
        for h in range(6):
            at = (2 * h + kind) * TOK
            grads_fine[at : at + TOK, :TOK] = both[h * TOK : (h + 1) * TOK]
    coarse_copies = sum_group(coarse_copies, part_coarse, ring_coarse, group_coarse, coarse_sems)
    fine_copies = sum_start(
        table_scatter(grads_fine, chosen, high), part_fine, ring_fine, fine_sems
    )

    def project_back(w, carry):
        span = window_span(w)
        outer = stack_heads(outer_ref[span, :], fine_masks)
        stacked = stack_heads(queries[span, :], fine_masks)
        grad_scores = score_grads[w].astype(BF16)
        grad_q = unstack_heads(dot(grad_scores, keys[span, :].astype(BF16)), fine_masks)
        qkv_grads[0, span, :] = grad_q * SCALING
        qkv_grads[1, span, :] = dot_tn(grad_scores, stacked) * SCALING
        qkv_grads[2, span, :] = dot_tn(probs[w].astype(BF16), outer)
        return carry

    lax.fori_loop(0, 4, project_back, 0, unroll=LOOP)
    fine_copies = sum_group(fine_copies, part_fine, ring_fine, group_fine, fine_sems)
    coarse_copies = sum_spread(coarse_copies, group_coarse, final_coarse, coarse_sems)
    grad_normed = jnp.zeros((FINE, 192), F32)
    for n in range(3):
        grad_normed += dot_nt(qkv_grads[n].astype(BF16), fine_qkv[n])
    grad_shifted = norm_back(fine_normed, fine_inverse, grad_normed).astype(BF16)
    pending = send_halo(3, after, dot(window_send[...], grad_shifted))
    fine_copies = sum_spread(fine_copies, group_fine, final_fine, fine_sems)

    total = coarse_ref[...]
    for g in range(4):
        total = total + dot(chidden[g], got_down[g])
    coarse_result[...] = dot(coarse_back[...], total.astype(BF16))
    local = first_ref[...] + dot(window_to_merge[:, :FINE], grad_shifted)
    wait(pending)
    grad = local + dot(window_to_merge[:, FINE:], halo_in[3])
    upper = grad.astype(BF16)
    lower = (grad - upper.astype(F32)).astype(BF16)
    grad_result[...] = dot(merge_to_native[...], upper) + dot(merge_to_native[...], lower)

    sums = sum_end(coarse_copies, final_coarse)
    row = lax.broadcasted_iota(jnp.int32, (8, ROWS), 0)
    col = lax.broadcasted_iota(jnp.int32, (8, ROWS), 1)
    chooser = jnp.where(col == row + 3 * group, 1.0, 0.0).astype(BF16)
    for h in range(HIGH):
        coarse_sums[h] = dot(chooser, sums[h * ROWS : (h + 1) * ROWS])
    for k in range(4):
        for copy in to_chip[k]:
            copy.wait_send()
        to_core[k].wait_send()
        passed[k].wait_send()
    fine_sums[...] = sum_end(fine_copies, final_fine)


def finish(
    grad_result, coarse_result, fine_sums, coarse_sums,
    coarse_out, grad_fields, grad_fine_bias, grad_coarse_bias,
):
    grad_fields[...] = grad_result[...].reshape(SIDE, SIDE, 2, 192)
    coarse_out[...] = coarse_result[...].reshape(6, 6, 2, 384).astype(BF16)
    length = grad_fine_bias.shape[2]
    sums = fine_sums[...].astype(F32)
    for h in range(HIGH):
        size = min(LANES, length - h * LANES)
        span = slice(h * LANES, h * LANES + size)
        for head in range(6):
            at = h * ROWS + 2 * head
            grad_fine_bias[head, :, span] = sums[at : at + 2, :size]
        for head in range(3):
            grad_coarse_bias[head, :, span] = coarse_sums[h, head : head + 1, :size]


def shards(
    fields, region, bias_index, fine_bias, coarse_bias, fine_qkv, fine_proj, fine_up, fine_down,
    merge_weight, coarse_qkv, coarse_proj, coarse_up, coarse_down, out_cotangent,
):
    lats = lax.axis_size("lat")
    rings = lax.axis_size("lon")
    share = BLOCKS * ROWS // rings
    (
        native_to_merge, merge_to_native, merge_send, merge_to_window, window_send,
        window_to_merge, coarse_native, coarse_back, label_row, label_col,
    ) = (jnp.asarray(c, BF16) for c in permutations())
    early = (
        jnp.transpose(fields, (1, 2, 0, 3)), native_to_merge, merge_send,
        jnp.transpose(region, (1, 0, 2)), bias_index,
        jnp.transpose(fine_bias, (2, 0, 1)), jnp.transpose(coarse_bias, (0, 2, 1)),
        label_row, label_col,
    )
    owns = (
        jnp.transpose(coarse_qkv, (1, 2, 0)).reshape(3 * 96, 384), coarse_proj, coarse_up,
        coarse_down,
    )
    late = (
        merge_to_window, jnp.transpose(fine_qkv, (1, 0, 2)), fine_proj, window_send,
        window_to_merge, fine_up, fine_down.T, merge_weight,
        jnp.transpose(out_cotangent, (1, 2, 0, 3)), coarse_native, coarse_back,
        merge_to_native,
    )
    vmem = pltpu.VMEM
    dma = pltpu.SemaphoreType.DMA
    sum_buffers = [
        vmem((rings, share, LANES), BF16),
        vmem((rings, share, LANES), BF16),
        vmem((4, share, LANES), F32),
        vmem((rings, share, LANES), BF16),
    ]
    scratch = [vmem(a.shape, a.dtype) for a in early + late]
    scratch += [
        vmem((4, HALO_ROWS, 192), BF16),
        vmem((4, HALO_ROWS, 192), BF16),
        vmem((4, 3 * 96, 384), BF16),
        vmem((4, 96, 384), BF16),
        vmem((4, 384, 384), BF16),
        vmem((4, 384, 384), BF16),
        vmem((4, 224, LANES), BF16),
        vmem((2 * SIDE, SIDE), F32),
        vmem((TOK, LANES), jnp.int32),
        vmem((TOK // 2, 2 * LANES, LANES), BF16),
        vmem((HIGH * ROWS, LANES), F32),
        vmem((ROWS * TOK, LANES), F32),
        vmem((ROWS * TOK, LANES), F32),
        vmem((ROWS * TOK, LANES), F32),
        vmem((FINE, 192), F32),
        vmem((FINE, 192), F32),
        vmem((FINE, 192), F32),
        vmem((4, 6 * TOK, TOK), F32),
        vmem((4, 6 * TOK, TOK), F32),
        vmem((FINE, 768), F32),
        vmem((FINE, 192), F32),
        vmem((4, 3 * TOK, TOK), F32),
        vmem((4, TOK, 384), BF16),
        vmem((TOK, 384), F32),
        vmem((FINE, SIDE), F32),
        vmem((FINE, 1), F32),
        vmem((FINE, 192), F32),
        vmem((FINE, 192), F32),
        vmem((3, FINE, 192), F32),
        vmem((4, TOK, 96), F32),
        vmem((4, TOK, 96), F32),
        vmem((4, TOK, 96), F32),
    ]
    scratch += sum_buffers + sum_buffers
    scratch += [
        dma((FETCHED + 4,)), dma((4,)), dma((4,)), dma((4, 4)), dma((4, 4)), dma((3,)), dma((3,)),
        dma((6,)), dma((6,)),
    ]
    whole = pl.BlockSpec(memory_space=pltpu.VMEM)
    hbm = pl.BlockSpec(memory_space=pl.ANY)
    coarse_result, grad_result, fine_sums, coarse_sums = pl.pallas_call(
        functools.partial(kernel, lats, rings),
        out_shape=(
            jax.ShapeDtypeStruct((TOK, 384), F32),
            jax.ShapeDtypeStruct((FINE, 192), F32),
            jax.ShapeDtypeStruct((BLOCKS * ROWS, LANES), BF16),
            jax.ShapeDtypeStruct((HIGH, 8, LANES), F32),
        ),
        in_specs=[hbm] * (len(owns) + FETCHED),
        out_specs=(whole,) * 4,
        scratch_shapes=scratch,
        compiler_params=pltpu.CompilerParams(
            collective_id=0, has_side_effects=True, vmem_limit_bytes=56 * 1024 * 1024
        ),
    )(*owns, *early, *late)
    outs = pl.pallas_call(
        finish,
        out_shape=(
            jax.ShapeDtypeStruct((6, 6, 2, 384), BF16),
            jax.ShapeDtypeStruct((SIDE, SIDE, 2, 192), F32),
            jax.ShapeDtypeStruct((6, 2, fine_bias.shape[1]), F32),
            jax.ShapeDtypeStruct((3, 1, fine_bias.shape[1]), F32),
        ),
        in_specs=[whole] * 4,
        out_specs=(whole,) * 4,
        compiler_params=pltpu.CompilerParams(vmem_limit_bytes=60 * 1024 * 1024),
    )(grad_result, coarse_result, fine_sums, coarse_sums)
    return (
        jnp.transpose(outs[0], (2, 0, 1, 3)),
        jnp.transpose(outs[1], (2, 0, 1, 3)),
        jnp.transpose(outs[2], (1, 2, 0)),
        jnp.transpose(outs[3], (1, 2, 0)),
    )


def solution(mesh):
    return jax.shard_map(
        shards,
        mesh=mesh,
        in_specs=(
            P(None, "lat", ("lon", "grp"), None),
            P(None, "lat", ("lon", "grp")),
            P(),
            P("lat", None, None),
            P("lat", None, "grp"),
            P(),
            P(),
            P(),
            P(),
            P(),
            P(None, None, "grp"),
            P("grp", None),
            P(None, "grp"),
            P("grp", None),
            P(None, "lat", ("lon", "grp"), None),
        ),
        out_specs=(
            P(None, "lat", ("lon", "grp"), None),
            P(None, "lat", ("lon", "grp"), None),
            P("lat", None, None),
            P("lat", None, "grp"),
        ),
        check_vma=False,
    )
```

```python
import functools
import math

import jax
import jax.numpy as jnp
import numpy as np
from jax import lax
from jax.experimental import pallas as pl
from jax.experimental.pallas import tpu as pltpu
from jax.sharding import PartitionSpec as P

MESH = pl.DeviceIdType.MESH
F32 = jnp.float32
BF16 = jnp.bfloat16
EPSILON = 1e-05
NEGATIVE = -1e30
HALF_ROOT = 1.0 / math.sqrt(2.0)
DENSITY = 1.0 / math.sqrt(2.0 * math.pi)
SCALING = 32 ** (-0.5)
WIN = 6
HALF = 3
TOK = 72
SIDE = 12
FINE = 4 * TOK
LANES = 128
HIGH = 13
BLOCKS = 16
KEYS = 80
ROWS = 16
SHARE = 64
UNROLL = 12
LOOP = 4
FETCHED = 23
EARLY = 9
HALO = ((0, 64), (64, 64), (128, 32))
HALO_ROWS = 160


def merge_row(level, row, col):
    group = (row % 2) + 2 * (col % 2)
    return group * TOK + level * 36 + (row // 2) * 6 + col // 2


def window_row(level, row, col):
    window = (row // WIN) * 2 + col // WIN
    return window * TOK + level * 36 + (row % WIN) * 6 + col % WIN


def native_row(level, row, col):
    return (row * SIDE + col) * 2 + level


def permutations():
    cells = [(z, i, j) for z in range(2) for i in range(SIDE) for j in range(SIDE)]
    native_to_merge = np.zeros((FINE, FINE), np.float32)
    merge_send = np.zeros((HALO_ROWS, FINE), np.float32)
    merge_to_window = np.zeros((FINE, FINE + HALO_ROWS), np.float32)
    window_send = np.zeros((HALO_ROWS, FINE), np.float32)
    window_to_merge = np.zeros((FINE, FINE + HALO_ROWS), np.float32)
    label_row = np.zeros((FINE, 2 * SIDE), np.float32)
    label_col = np.zeros((FINE, SIDE), np.float32)
    ahead = [0, 0, 0]
    for z, i, j in cells:
        native_to_merge[merge_row(z, i, j), native_row(z, i, j)] = 1
        target = window_row(z, i, j)
        label_row[target, 2 * i + z] = 1
        label_col[target, j] = 1
        source = merge_row((z + 1) % 2, (i + HALF) % SIDE, (j + HALF) % SIDE)
        over_row, over_col = i + HALF >= SIDE, j + HALF >= SIDE
        if not over_row and not over_col:
            merge_to_window[target, source] = 1
            window_to_merge[source, target] = 1
            continue
        kind = 2 if over_row and over_col else (0 if over_row else 1)
        slot = HALO[kind][0] + ahead[kind]
        ahead[kind] += 1
        merge_send[slot, source] = 1
        merge_to_window[target, FINE + slot] = 1
        window_send[slot, target] = 1
        window_to_merge[source, FINE + slot] = 1
    by_slot = np.zeros((4 * SHARE, HIGH * ROWS), np.float32)
    into_fine = np.zeros((HIGH * ROWS, SHARE), np.float32)
    for h in range(HIGH):
        for head in range(3):
            into_fine[h * ROWS + 12 + head, 4 * h + head] = 1
            for slot in range(4):
                by_slot[slot * SHARE + 4 * h + head, h * ROWS + 4 * slot + head] = 1
    coarse_native = np.zeros((TOK, TOK), np.float32)
    for z in range(2):
        for i in range(6):
            for j in range(6):
                coarse_native[z * 36 + i * 6 + j, (i * 6 + j) * 2 + z] = 1
    return (
        native_to_merge, native_to_merge.T, merge_send, merge_to_window,
        window_send, window_to_merge, coarse_native, coarse_native.T, label_row, label_col,
        by_slot, into_fine,
    )


def dot(a, b):
    return lax.dot_general(a, b, (((1,), (0,)), ((), ())), preferred_element_type=F32)


def dot_nt(a, b):
    return lax.dot_general(a, b, (((1,), (1,)), ((), ())), preferred_element_type=F32)


def dot_tn(a, b):
    return lax.dot_general(a, b, (((0,), (0,)), ((), ())), preferred_element_type=F32)


def rounded(values):
    return values.astype(BF16).astype(F32)


def layer_norm(values):
    centred = values - jnp.mean(values, axis=-1, keepdims=True)
    inverse = lax.rsqrt(jnp.mean(centred * centred, axis=-1, keepdims=True) + EPSILON)
    return centred * inverse, inverse


def norm_back(normed, inverse, upstream):
    mean_up = jnp.mean(upstream, axis=-1, keepdims=True)
    mean_cross = jnp.mean(upstream * normed, axis=-1, keepdims=True)
    return inverse * (upstream - mean_up - normed * mean_cross)


def gelu_both(pre_act):
    decay = jnp.exp(-0.5 * pre_act * pre_act)
    t = 1.0 / (1.0 + (0.3275911 * HALF_ROOT) * jnp.abs(pre_act))
    poly = 0.5 * 1.061405429
    for factor in (-1.453152027, 1.421413741, -0.284496736, 0.254829592):
        poly = poly * t + 0.5 * factor
    tail = poly * t * decay
    half = jnp.where(pre_act < 0.0, tail, 1.0 - tail)
    return pre_act * half, half + pre_act * decay * DENSITY


def head_masks(width):
    lane = lax.broadcasted_iota(jnp.int32, (1, width), 1)
    return [(lane >= 32 * h) & (lane < 32 * h + 32) for h in range(width // 32)]


def stack_heads(values, masks):
    return jnp.concatenate([jnp.where(m, values, 0.0) for m in masks], axis=0).astype(BF16)


def unstack_heads(values, masks):
    total = jnp.where(masks[0], values[:TOK], 0.0)
    for h in range(1, len(masks)):
        total = jnp.where(masks[h], values[h * TOK : (h + 1) * TOK], total)
    return total


def softmax(scores):
    weights = jnp.exp(scores - jnp.max(scores, axis=-1, keepdims=True))
    return weights * (1.0 / jnp.sum(weights, axis=-1, keepdims=True))


def table_scatter(grads, chosen, high):
    def step(p, total):
        parts = []
        for half in range(2):
            i = 2 * p + half
            rows = grads[pl.ds(i, ROWS, stride=TOK), :].astype(BF16)
            picked = jnp.broadcast_to(high[pl.ds(i, 1), :], (ROWS, LANES)).astype(BF16)
            zero = jnp.zeros_like(rows)
            parts.append(
                jnp.concatenate(
                    [jnp.where(picked == jnp.asarray(h, BF16), rows, zero) for h in range(HIGH)],
                    axis=0,
                )
            )
        return total + dot(jnp.concatenate(parts, axis=1), chosen[p])

    return lax.fori_loop(0, TOK // 2, step, jnp.zeros((HIGH * ROWS, LANES), F32), unroll=UNROLL)


def table_gather(table, out, chosen, high):
    entries = table[...].astype(BF16)

    def step(p, carry):
        spread = dot_nt(entries, chosen[p])
        for half in range(2):
            i = 2 * p + half
            picked = jnp.broadcast_to(high[pl.ds(i, 1), :], (ROWS, LANES))
            span = slice(half * LANES, (half + 1) * LANES)
            found = spread[:ROWS, span]
            for h in range(1, HIGH):
                found = jnp.where(picked == h, spread[h * ROWS : (h + 1) * ROWS, span], found)
            out[pl.ds(i, ROWS, stride=TOK), :] = found
        return carry

    lax.fori_loop(0, TOK // 2, step, 0, unroll=UNROLL)


def kernel(
    lats,
    rings,
    own_qkv, own_proj, own_up, own_down, *rest,
):
    stored, rest = rest[:FETCHED], rest[FETCHED:]
    outs, rest = rest[:3], rest[3:]
    held, rest = rest[:FETCHED], rest[FETCHED:]
    body(
        lats, rings, own_qkv, own_proj, own_up, own_down, stored, held, *held, *outs, *rest
    )


def body(
    lats, rings, own_qkv, own_proj, own_up, own_down, stored, held,
    fields, native_to_merge, merge_send, region, bias_index, fine_bias, coarse_bias,
    label_row, label_col,
    merge_to_window, fine_qkv, fine_proj, window_send, window_to_merge, fine_up, fine_down,
    merge_weight, cotangent, coarse_native, coarse_back, merge_to_native,
    by_slot, into_fine,
    coarse_result, grad_result, table_sums,
    halo_out, halo_in, got_qkv, got_proj, got_up, got_down, got_cbias,
    label_rows, high, chosen, table, bias, grads_fine, grads_coarse,
    queries, keys, values, probs, score_grads, slope, first_ref, cprobs, chidden, coarse_ref,
    spread_ref, label_ref, attended, outer_ref, qkv_grads, cqueries, ckeys, cvalues,
    part_fine, ring_fine, group_fine, final_fine,
    part_coarse, got_coarse,
    late_sems, halo_send, halo_recv, weight_send, weight_recv, cbias_send, cbias_recv,
    fine_sems, coarse_sems,
):
    lat = lax.axis_index("lat")
    ring = lax.axis_index("lon")
    group = lax.axis_index("grp")
    column = ring * 4 + group
    columns = rings * 4

    def place(row_shift, col_shift):
        row = lax.rem(lat + row_shift + lats, lats)
        col = lax.rem(column + col_shift + columns, columns)
        return {"lat": row, "lon": lax.div(col, 4), "grp": lax.rem(col, 4)}

    before = (place(-1, 0), place(0, -1), place(-1, -1))
    after = (place(1, 0), place(0, 1), place(1, 1))
    core_mate = group + 1 - 2 * lax.rem(group, 2)
    chip_mate = lax.rem(group + 2, 4)
    far_mate = lax.rem(core_mate + 2, 4)
    mates = (core_mate, chip_mate, far_mate)

    copies = [
        pltpu.make_async_copy(source, target, late_sems.at[k])
        for k, (source, target) in enumerate(zip(stored, held))
    ]
    early, loads = copies[:EARLY], copies[EARLY:]
    owns = [
        pltpu.make_async_copy(own, got.at[0], late_sems.at[FETCHED + k])
        for k, (own, got) in enumerate(
            ((own_qkv, got_qkv), (own_proj, got_proj), (own_up, got_up), (own_down, got_down))
        )
    ]
    for copy in copies:
        copy.start()
    barrier = pltpu.get_barrier_semaphore()
    for device in before + after:
        pl.semaphore_signal(barrier, 1, device_id=device, device_id_type=MESH)
    for mate in mates:
        pl.semaphore_signal(barrier, 1, device_id={"grp": mate}, device_id_type=MESH)
    far_lat = lax.rem(lat + lats // 2, lats)
    neighbours = ({"grp": chip_mate}, {"lat": far_lat, "grp": chip_mate})
    pl.semaphore_signal(barrier, 1, device_id=neighbours[1], device_id_type=MESH)
    for step in range(1, rings):
        pl.semaphore_signal(
            barrier, 1, device_id={"lon": lax.rem(ring + step, rings)}, device_id_type=MESH
        )

    def remote(source, target, send, recv, device):
        copy = pltpu.make_async_remote_copy(
            source, target, send, recv, device_id=device, device_id_type=MESH
        )
        copy.start()
        return copy

    def together(sent, got, send, recv):
        return pltpu.make_async_remote_copy(
            sent, got, send, recv, device_id={"grp": core_mate}, device_id_type=MESH
        )

    def send_halo(number, devices, block):
        halo_out[number] = block.astype(BF16)
        for kind, (start, size) in enumerate(HALO):
            rows = pl.ds(start, size)
            remote(
                halo_out.at[number, rows], halo_in.at[number, rows],
                halo_send.at[number], halo_recv.at[number], devices[kind],
            )
        return [
            together(
                halo_out.at[number], halo_in.at[number], halo_send.at[number], halo_recv.at[number]
            )
        ]

    def wait(copies):
        for copy in copies:
            copy.wait()

    for copy in owns:
        copy.start()
    for copy in early[:3]:
        copy.wait()

    tokens = dot(native_to_merge[...], fields[...].astype(F32).reshape(FINE, 192).astype(BF16))
    tokens_half = tokens.astype(BF16)
    first_block = dot(merge_send[...], tokens_half)
    pl.semaphore_wait(barrier, 10 + rings - 1)
    pending = send_halo(0, before, first_block)

    shares = ((own_qkv, got_qkv), (own_proj, got_proj), (own_up, got_up), (own_down, got_down))
    to_chip, to_core, passed = [], [], []

    def half_of(ref, half):
        rows = ref.shape[0] // 2
        return ref.at[pl.ds(half * rows, rows)]

    for k, (own, got) in enumerate(shares):
        to_chip.append(
            [
                remote(
                    half_of(own, half), half_of(got.at[2], half),
                    weight_send.at[k, half], weight_recv.at[k, half], neighbours[half],
                )
                for half in range(2)
            ]
        )
    for k, (own, got) in enumerate(shares):
        to_core.append(
            remote(own, got.at[1], weight_send.at[k, 2], weight_recv.at[k, 2], {"grp": core_mate})
        )

    def pass_on(k):
        got = shares[k][1]
        for copy in to_chip[k]:
            copy.wait_recv()
        passed.append(
            remote(
                got.at[2], got.at[3], weight_send.at[k, 3], weight_recv.at[k, 3], {"grp": core_mate}
            )
        )

    for copy in early[3:]:
        copy.wait()
    index = bias_index[...]
    high[...] = jnp.zeros_like(high)
    high[:, :TOK] = lax.shift_right_logical(index, 7)
    low = (index & (LANES - 1)).astype(F32).astype(BF16)
    key_row = lax.broadcasted_iota(jnp.int32, (LANES, TOK), 0)
    key_col = lax.broadcasted_iota(jnp.int32, (LANES, TOK), 1)
    identity = jnp.where(key_row == key_col, 1.0, 0.0).astype(BF16)
    low_keys = jnp.where(key_row < TOK, dot_nt(identity, low), -1.0)[:KEYS].astype(BF16)
    query = lax.broadcasted_iota(jnp.int32, (TOK, 2 * LANES), 0)
    lane = lax.broadcasted_iota(jnp.int32, (TOK, 2 * LANES), 1)
    target_query = query - lax.shift_right_logical(lane, 7)
    lane = (lax.broadcasted_iota(jnp.int32, (KEYS, 2 * LANES), 1) & (LANES - 1)).astype(F32)
    blank = jnp.zeros((LANES - KEYS, LANES), BF16)

    def choose(p, carry):
        pick = jnp.where(target_query == 2 * p, 1.0, 0.0).astype(BF16)
        found = jnp.where(dot(low_keys, pick) == lane, 1.0, 0.0).astype(BF16)
        for half in range(2):
            at = half * LANES
            chosen[p, at : at + KEYS, :] = found[:, at : at + LANES]
            chosen[p, at + KEYS : at + LANES, :] = blank
        return carry

    lax.fori_loop(0, TOK // 2, choose, 0, unroll=UNROLL)
    table[...] = jnp.zeros_like(table)
    length = fine_bias.shape[2]
    for h in range(HIGH):
        size = min(LANES, length - h * LANES)
        span = slice(h * LANES, h * LANES + size)
        for head in range(6):
            at = h * ROWS + 2 * head
            table[at : at + 2, :size] = fine_bias[head, :, span].astype(F32)
        at = h * ROWS + 12
        table[at : at + 3, :size] = coarse_bias[0, :, span].astype(F32)
    table_gather(table, bias, chosen, high)
    got_cbias[0] = bias[12 * TOK : 12 * TOK + 224, :].astype(BF16)
    cbias_copies = [
        remote(got_cbias.at[0], got_cbias.at[k + 1], cbias_send.at[k], cbias_recv.at[k], {"grp": mate})
        for k, mate in enumerate(mates)
    ]
    grads_fine[...] = jnp.zeros_like(grads_fine)
    grads_coarse[...] = jnp.zeros_like(grads_coarse)

    fine_masks = head_masks(192)
    for i in range(SIDE):
        label_rows[2 * i : 2 * i + 2, :] = region[i].astype(F32)
    spread_labels = dot(label_row[...], label_rows[...].astype(BF16)) * label_col[...].astype(F32)
    col_labels = jnp.sum(spread_labels, axis=-1, keepdims=True)
    ones = jnp.ones((8, SIDE), BF16)
    spread_ref[...] = spread_labels
    label_ref[...] = col_labels
    loads[0].wait()
    loads[1].wait()
    local = dot(merge_to_window[:, :FINE], tokens_half)
    wait(pending)
    shifted = local + dot(merge_to_window[:, FINE:], halo_in[0])
    fine_normed, fine_inverse = layer_norm(shifted)
    fine_half = fine_normed.astype(BF16)
    for k, ref in enumerate((queries, keys, values)):
        ref[...] = rounded(dot(fine_half, fine_qkv[k]))

    def window_span(w):
        return pl.ds(pl.multiple_of(w * TOK, 8), TOK)

    def attend(w, carry):
        span = window_span(w)
        stacked = stack_heads(queries[span, :], fine_masks)
        scores = dot_nt(stacked, keys[span, :].astype(BF16)) * SCALING
        kind = w // 2
        scores = scores + jnp.concatenate(
            [bias[window_span(2 * h + kind), :TOK] for h in range(6)], axis=0
        )
        row_labels = dot_nt(ones, spread_ref[span, :].astype(BF16))[:1]
        allowed = label_ref[span, :] == row_labels
        scores = jnp.where(allowed[None], scores.reshape(6, TOK, TOK), NEGATIVE)
        weights = softmax(scores.reshape(6 * TOK, TOK))
        probs[w] = weights
        attended[span, :] = unstack_heads(
            dot(weights.astype(BF16), values[span, :].astype(BF16)), fine_masks
        )
        return carry

    lax.fori_loop(0, 4, attend, 0, unroll=LOOP)
    for k in range(2, 5):
        loads[k].wait()
    branch = dot(attended[...].astype(BF16), fine_proj[...]).astype(BF16)
    pending = send_halo(1, after, dot(window_send[...], branch))
    local = tokens + dot(window_to_merge[:, :FINE], branch)
    for k in range(8, 14):
        loads[k].wait()
    upstream = dot(
        coarse_native[...], cotangent[...].astype(F32).reshape(TOK, 384).astype(BF16)
    )
    pass_on(0)
    pass_on(1)
    wait(pending)
    first = rounded(local + dot(window_to_merge[:, FINE:], halo_in[1]))
    first_ref[...] = first

    for k in range(5, 8):
        loads[k].wait()
    normed, inverse = layer_norm(first)
    hidden, slopes = gelu_both(dot(normed.astype(BF16), fine_up[...]))
    slope[...] = slopes
    second = rounded(first + dot_nt(hidden.astype(BF16), fine_down[...]))
    cells = [second[g * TOK : (g + 1) * TOK] for g in range(4)]
    width = 4 * second.shape[1]
    mean = sum(jnp.sum(c, axis=-1, keepdims=True) for c in cells) / width
    cells = [c - mean for c in cells]
    variance = sum(jnp.sum(c * c, axis=-1, keepdims=True) for c in cells) / width
    joined_inverse = lax.rsqrt(variance + EPSILON)
    cells = [c * joined_inverse for c in cells]
    merged = jnp.zeros((TOK, merge_weight.shape[1]), F32)
    for g in range(4):
        merged += dot(cells[g].astype(BF16), merge_weight[g * 192 : (g + 1) * 192, :])
    merged = rounded(merged)
    pass_on(2)
    pass_on(3)

    coarse_masks = head_masks(96)
    base_normed, base_inverse = layer_norm(merged)
    base_half = base_normed.astype(BF16)
    wait(cbias_copies)

    def arrive(k):
        owns[k].wait()
        to_core[k].wait_recv()
        passed[k].wait_recv()

    arrive(0)
    arrive(1)

    def coarse_attend(g, total):
        q, k, v = (
            rounded(dot_nt(base_half, got_qkv[g, n * 96 : (n + 1) * 96, :])) for n in range(3)
        )
        cqueries[g] = q
        ckeys[g] = k
        cvalues[g] = v
        stacked = stack_heads(q, coarse_masks)
        scores = dot_nt(stacked, k.astype(BF16)) * SCALING
        scores = scores + got_cbias[g].astype(F32)[: 3 * TOK, :TOK]
        weights = softmax(scores)
        cprobs[g] = weights
        seen = unstack_heads(dot(weights.astype(BF16), v.astype(BF16)), coarse_masks)
        return total + dot(seen.astype(BF16), got_proj[g])

    coarse_first = rounded(lax.fori_loop(0, 4, coarse_attend, merged, unroll=LOOP))
    up_normed, up_inverse = layer_norm(coarse_first)
    up_half = up_normed.astype(BF16)
    arrive(2)
    arrive(3)

    upstream_half = upstream.astype(BF16)

    def coarse_mlp(g, total):
        hidden, slopes = gelu_both(dot(up_half, got_up[g]))
        chidden[g] = hidden.astype(BF16)
        grad_pre = dot_nt(upstream_half, got_down[g]) * slopes
        return total + dot_nt(grad_pre.astype(BF16), got_up[g])

    blank = jnp.zeros((TOK, 384), F32)
    total = lax.fori_loop(0, 4, coarse_mlp, blank, unroll=LOOP)
    coarse_ref[...] = coarse_first

    grad_first = upstream + norm_back(up_normed, up_inverse, total)
    grad_half = grad_first.astype(BF16)

    def coarse_attend_back(g, total):
        stacked = stack_heads(cqueries[g], coarse_masks)
        weights = cprobs[g]
        outer = stack_heads(rounded(dot_nt(grad_half, got_proj[g])), coarse_masks)
        grad_probs = dot_nt(outer, cvalues[g].astype(BF16))
        grad_scores = weights * (
            grad_probs - jnp.sum(grad_probs * weights, axis=-1, keepdims=True)
        )
        for h in range(3):
            at = window_span(4 * g + h)
            grads_coarse[at, :TOK] = grad_scores[h * TOK : (h + 1) * TOK]
        grad_scores = grad_scores.astype(BF16)
        grad_v = dot_tn(weights.astype(BF16), outer)
        grad_q = unstack_heads(dot(grad_scores, ckeys[g].astype(BF16)), coarse_masks) * SCALING
        grad_k = dot_tn(grad_scores, stacked) * SCALING
        for n, grad in enumerate((grad_q, grad_k, grad_v)):
            total = total + dot(grad.astype(BF16), got_qkv[g, n * 96 : (n + 1) * 96, :])
        return total

    total = lax.fori_loop(0, 4, coarse_attend_back, blank, unroll=LOOP)
    grad_merged = (grad_first + norm_back(base_normed, base_inverse, total)).astype(BF16)

    joined = [dot_nt(grad_merged, merge_weight[g * 192 : (g + 1) * 192, :]) for g in range(4)]
    mean_up = sum(jnp.sum(j, axis=-1, keepdims=True) for j in joined) / width
    mean_cross = (
        sum(jnp.sum(j * c, axis=-1, keepdims=True) for j, c in zip(joined, cells)) / width
    )
    grad_second = jnp.concatenate(
        [joined_inverse * (j - mean_up - c * mean_cross) for j, c in zip(joined, cells)], axis=0
    )
    grad_pre = dot(grad_second.astype(BF16), fine_down[...]) * slope[...]
    grad_normed = dot_nt(grad_pre.astype(BF16), fine_up[...])
    normed, inverse = layer_norm(first_ref[...])
    grad_fine = grad_second + norm_back(normed, inverse, grad_normed)
    first_ref[...] = grad_fine
    grad_half = grad_fine.astype(BF16)
    pending = send_halo(2, before, dot(merge_send[...], grad_half))

    share = BLOCKS * ROWS // rings

    def sum_start(sums, part, got, sems):
        sums = sums.astype(BF16)
        blank = jnp.zeros((BLOCKS * ROWS - HIGH * ROWS, LANES), BF16)
        part[...] = jnp.concatenate([sums, blank], axis=0).reshape(rings, share, LANES)
        for step in range(1, rings):
            peer = lax.rem(ring + step, rings)
            remote(part.at[peer], got.at[step], sems.at[0], sems.at[1], {"lon": peer})
        others = pl.ds(1, rings - 1)
        return [together(part.at[others], got.at[others], sems.at[0], sems.at[1])]

    def sum_group(copies, part, got, grouped, sems):
        wait(copies)
        total = part[ring].astype(F32) + jnp.sum(got[1:].astype(F32), axis=0)
        grouped[group] = total
        for mate in mates:
            remote(grouped.at[group], grouped.at[group], sems.at[2], sems.at[3], {"grp": mate})
        others = pl.ds(0, 3)
        return [together(grouped.at[others], grouped.at[others], sems.at[2], sems.at[3])]

    def sum_spread(copies, grouped, final, sems):
        wait(copies)
        total = grouped[0] + grouped[1] + grouped[2] + grouped[3]
        row = lax.broadcasted_iota(jnp.int32, total.shape, 0)
        total = jnp.where(lax.rem(row, ROWS) < 12, total, grouped[group])
        final[ring] = total.astype(BF16)
        for step in range(1, rings):
            peer = lax.rem(ring + step, rings)
            remote(final.at[ring], final.at[ring], sems.at[4], sems.at[5], {"lon": peer})
        others = pl.ds(0, rings - 1)
        return [together(final.at[others], final.at[others], sems.at[4], sems.at[5])]

    def sum_end(copies, final):
        wait(copies)
        return final[...].reshape(BLOCKS * ROWS, LANES)

    sums = table_scatter(grads_coarse, chosen, high).astype(BF16)
    part_coarse[...] = dot(by_slot[...], sums).astype(BF16).reshape(4, SHARE, LANES)
    for k, mate in enumerate(mates):
        remote(
            part_coarse.at[k + 1], got_coarse.at[k + 1], coarse_sems.at[0], coarse_sems.at[1],
            {"grp": mate},
        )
    others = pl.ds(1, 3)
    coarse_copies = [
        together(
            part_coarse.at[others], got_coarse.at[others], coarse_sems.at[0], coarse_sems.at[1]
        )
    ]

    local = dot(merge_to_window[:, :FINE], grad_half)
    wait(pending)
    grad_branch = local + dot(merge_to_window[:, FINE:], halo_in[2])
    outer_all = rounded(dot_nt(grad_branch.astype(BF16), fine_proj[...]))
    outer_ref[...] = outer_all

    def attend_back(w, carry):
        weights = probs[w]
        span = window_span(w)
        outer = stack_heads(outer_ref[span, :], fine_masks)
        grad_probs = dot_nt(outer, values[span, :].astype(BF16))
        score_grads[w] = weights * (
            grad_probs - jnp.sum(grad_probs * weights, axis=-1, keepdims=True)
        )
        return carry

    lax.fori_loop(0, 4, attend_back, 0, unroll=LOOP)
    for kind in range(2):
        both = score_grads[2 * kind] + score_grads[2 * kind + 1]
        for h in range(6):
            at = (2 * h + kind) * TOK
            grads_fine[at : at + TOK, :TOK] = both[h * TOK : (h + 1) * TOK]
    sums = table_scatter(grads_fine, chosen, high)
    wait(coarse_copies)
    own_heads = part_coarse[0].astype(F32) + jnp.sum(got_coarse[1:].astype(F32), axis=0)
    sums = sums + dot(into_fine[...], own_heads.astype(BF16))
    fine_copies = sum_start(sums, part_fine, ring_fine, fine_sems)

    def project_back(w, carry):
        span = window_span(w)
        outer = stack_heads(outer_ref[span, :], fine_masks)
        stacked = stack_heads(queries[span, :], fine_masks)
        grad_scores = score_grads[w].astype(BF16)
        grad_q = unstack_heads(dot(grad_scores, keys[span, :].astype(BF16)), fine_masks)
        qkv_grads[0, span, :] = grad_q * SCALING
        qkv_grads[1, span, :] = dot_tn(grad_scores, stacked) * SCALING
        qkv_grads[2, span, :] = dot_tn(probs[w].astype(BF16), outer)
        return carry

    lax.fori_loop(0, 4, project_back, 0, unroll=LOOP)
    fine_copies = sum_group(fine_copies, part_fine, ring_fine, group_fine, fine_sems)
    grad_normed = jnp.zeros((FINE, 192), F32)
    for n in range(3):
        grad_normed += dot_nt(qkv_grads[n].astype(BF16), fine_qkv[n])
    grad_shifted = norm_back(fine_normed, fine_inverse, grad_normed).astype(BF16)
    pending = send_halo(3, after, dot(window_send[...], grad_shifted))
    fine_copies = sum_spread(fine_copies, group_fine, final_fine, fine_sems)

    total = coarse_ref[...]
    for g in range(4):
        total = total + dot(chidden[g], got_down[g])
    coarse_result[...] = dot(coarse_back[...], total.astype(BF16))
    local = first_ref[...] + dot(window_to_merge[:, :FINE], grad_shifted)
    wait(pending)
    grad = local + dot(window_to_merge[:, FINE:], halo_in[3])
    upper = grad.astype(BF16)
    lower = (grad - upper.astype(F32)).astype(BF16)
    grad_result[...] = dot(merge_to_native[...], upper) + dot(merge_to_native[...], lower)

    for k in range(4):
        for copy in to_chip[k]:
            copy.wait_send()
        to_core[k].wait_send()
        passed[k].wait_send()
    table_sums[...] = sum_end(fine_copies, final_fine)


def finish(
    grad_result, coarse_result, table_sums,
    coarse_out, grad_fields, grad_fine_bias, grad_coarse_bias,
):
    grad_fields[...] = grad_result[...].reshape(SIDE, SIDE, 2, 192)
    coarse_out[...] = coarse_result[...].reshape(6, 6, 2, 384).astype(BF16)
    length = grad_fine_bias.shape[2]
    sums = table_sums[...].astype(F32)
    for h in range(HIGH):
        size = min(LANES, length - h * LANES)
        span = slice(h * LANES, h * LANES + size)
        for head in range(6):
            at = h * ROWS + 2 * head
            grad_fine_bias[head, :, span] = sums[at : at + 2, :size]
        for head in range(3):
            at = h * ROWS + 12 + head
            grad_coarse_bias[head, :, span] = sums[at : at + 1, :size]


def shards(
    fields, region, bias_index, fine_bias, coarse_bias, fine_qkv, fine_proj, fine_up, fine_down,
    merge_weight, coarse_qkv, coarse_proj, coarse_up, coarse_down, out_cotangent,
):
    lats = lax.axis_size("lat")
    rings = lax.axis_size("lon")
    share = BLOCKS * ROWS // rings
    (
        native_to_merge, merge_to_native, merge_send, merge_to_window, window_send,
        window_to_merge, coarse_native, coarse_back, label_row, label_col, by_slot, into_fine,
    ) = (jnp.asarray(c, BF16) for c in permutations())
    early = (
        jnp.transpose(fields, (1, 2, 0, 3)), native_to_merge, merge_send,
        jnp.transpose(region, (1, 0, 2)), bias_index,
        jnp.transpose(fine_bias, (2, 0, 1)), jnp.transpose(coarse_bias, (0, 2, 1)),
        label_row, label_col,
    )
    owns = (
        jnp.transpose(coarse_qkv, (1, 2, 0)).reshape(3 * 96, 384), coarse_proj, coarse_up,
        coarse_down,
    )
    late = (
        merge_to_window, jnp.transpose(fine_qkv, (1, 0, 2)), fine_proj, window_send,
        window_to_merge, fine_up, fine_down.T, merge_weight,
        jnp.transpose(out_cotangent, (1, 2, 0, 3)), coarse_native, coarse_back,
        merge_to_native, by_slot, into_fine,
    )
    vmem = pltpu.VMEM
    dma = pltpu.SemaphoreType.DMA
    sum_buffers = [
        vmem((rings, share, LANES), BF16),
        vmem((rings, share, LANES), BF16),
        vmem((4, share, LANES), F32),
        vmem((rings, share, LANES), BF16),
    ]
    scratch = [vmem(a.shape, a.dtype) for a in early + late]
    scratch += [
        vmem((4, HALO_ROWS, 192), BF16),
        vmem((4, HALO_ROWS, 192), BF16),
        vmem((4, 3 * 96, 384), BF16),
        vmem((4, 96, 384), BF16),
        vmem((4, 384, 384), BF16),
        vmem((4, 384, 384), BF16),
        vmem((4, 224, LANES), BF16),
        vmem((2 * SIDE, SIDE), F32),
        vmem((TOK, LANES), jnp.int32),
        vmem((TOK // 2, 2 * LANES, LANES), BF16),
        vmem((HIGH * ROWS, LANES), F32),
        vmem((ROWS * TOK, LANES), F32),
        vmem((ROWS * TOK, LANES), F32),
        vmem((ROWS * TOK, LANES), F32),
        vmem((FINE, 192), F32),
        vmem((FINE, 192), F32),
        vmem((FINE, 192), F32),
        vmem((4, 6 * TOK, TOK), F32),
        vmem((4, 6 * TOK, TOK), F32),
        vmem((FINE, 768), F32),
        vmem((FINE, 192), F32),
        vmem((4, 3 * TOK, TOK), F32),
        vmem((4, TOK, 384), BF16),
        vmem((TOK, 384), F32),
        vmem((FINE, SIDE), F32),
        vmem((FINE, 1), F32),
        vmem((FINE, 192), F32),
        vmem((FINE, 192), F32),
        vmem((3, FINE, 192), F32),
        vmem((4, TOK, 96), F32),
        vmem((4, TOK, 96), F32),
        vmem((4, TOK, 96), F32),
    ]
    scratch += sum_buffers + [vmem((4, SHARE, LANES), BF16), vmem((4, SHARE, LANES), BF16)]
    scratch += [
        dma((FETCHED + 4,)), dma((4,)), dma((4,)), dma((4, 4)), dma((4, 4)), dma((3,)), dma((3,)),
        dma((6,)), dma((2,)),
    ]
    whole = pl.BlockSpec(memory_space=pltpu.VMEM)
    hbm = pl.BlockSpec(memory_space=pl.ANY)
    coarse_result, grad_result, table_sums = pl.pallas_call(
        functools.partial(kernel, lats, rings),
        out_shape=(
            jax.ShapeDtypeStruct((TOK, 384), F32),
            jax.ShapeDtypeStruct((FINE, 192), F32),
            jax.ShapeDtypeStruct((BLOCKS * ROWS, LANES), BF16),
        ),
        in_specs=[hbm] * (len(owns) + FETCHED),
        out_specs=(whole,) * 3,
        scratch_shapes=scratch,
        compiler_params=pltpu.CompilerParams(
            collective_id=0, has_side_effects=True, vmem_limit_bytes=56 * 1024 * 1024
        ),
    )(*owns, *early, *late)
    outs = pl.pallas_call(
        finish,
        out_shape=(
            jax.ShapeDtypeStruct((6, 6, 2, 384), BF16),
            jax.ShapeDtypeStruct((SIDE, SIDE, 2, 192), F32),
            jax.ShapeDtypeStruct((6, 2, fine_bias.shape[1]), F32),
            jax.ShapeDtypeStruct((3, 1, fine_bias.shape[1]), F32),
        ),
        in_specs=[whole] * 3,
        out_specs=(whole,) * 4,
        compiler_params=pltpu.CompilerParams(vmem_limit_bytes=60 * 1024 * 1024),
    )(grad_result, coarse_result, table_sums)
    return (
        jnp.transpose(outs[0], (2, 0, 1, 3)),
        jnp.transpose(outs[1], (2, 0, 1, 3)),
        jnp.transpose(outs[2], (1, 2, 0)),
        jnp.transpose(outs[3], (1, 2, 0)),
    )


def solution(mesh):
    return jax.shard_map(
        shards,
        mesh=mesh,
        in_specs=(
            P(None, "lat", ("lon", "grp"), None),
            P(None, "lat", ("lon", "grp")),
            P(),
            P("lat", None, None),
            P("lat", None, "grp"),
            P(),
            P(),
            P(),
            P(),
            P(),
            P(None, None, "grp"),
            P("grp", None),
            P(None, "grp"),
            P("grp", None),
            P(None, "lat", ("lon", "grp"), None),
        ),
        out_specs=(
            P(None, "lat", ("lon", "grp"), None),
            P(None, "lat", ("lon", "grp"), None),
            P("lat", None, None),
            P("lat", None, "grp"),
        ),
        check_vma=False,
    )
```

```python
import functools
import math

import jax
import jax.numpy as jnp
import numpy as np
from jax import lax
from jax.experimental import pallas as pl
from jax.experimental.pallas import tpu as pltpu
from jax.sharding import PartitionSpec as P

MESH = pl.DeviceIdType.MESH
F32 = jnp.float32
BF16 = jnp.bfloat16
EPSILON = 1e-05
NEGATIVE = -1e30
HALF_ROOT = 1.0 / math.sqrt(2.0)
DENSITY = 1.0 / math.sqrt(2.0 * math.pi)
SCALING = 32 ** (-0.5)
WIN = 6
HALF = 3
TOK = 72
SIDE = 12
FINE = 4 * TOK
LANES = 128
HIGH = 13
BLOCKS = 16
KEYS = 80
ROWS = 16
SHARE = 64
UNROLL = 12
LOOP = 4
FETCHED = 23
EARLY = 9
HALO = ((0, 64), (64, 64), (128, 32))
HALO_ROWS = 160


def merge_row(level, row, col):
    group = (row % 2) + 2 * (col % 2)
    return group * TOK + level * 36 + (row // 2) * 6 + col // 2


def window_row(level, row, col):
    window = (row // WIN) * 2 + col // WIN
    return window * TOK + level * 36 + (row % WIN) * 6 + col % WIN


def native_row(level, row, col):
    return (row * SIDE + col) * 2 + level


def permutations():
    cells = [(z, i, j) for z in range(2) for i in range(SIDE) for j in range(SIDE)]
    native_to_merge = np.zeros((FINE, FINE), np.float32)
    merge_send = np.zeros((HALO_ROWS, FINE), np.float32)
    merge_to_window = np.zeros((FINE, FINE + HALO_ROWS), np.float32)
    window_send = np.zeros((HALO_ROWS, FINE), np.float32)
    window_to_merge = np.zeros((FINE, FINE + HALO_ROWS), np.float32)
    label_row = np.zeros((FINE, 2 * SIDE), np.float32)
    label_col = np.zeros((FINE, SIDE), np.float32)
    ahead = [0, 0, 0]
    for z, i, j in cells:
        native_to_merge[merge_row(z, i, j), native_row(z, i, j)] = 1
        target = window_row(z, i, j)
        label_row[target, 2 * i + z] = 1
        label_col[target, j] = 1
        source = merge_row((z + 1) % 2, (i + HALF) % SIDE, (j + HALF) % SIDE)
        over_row, over_col = i + HALF >= SIDE, j + HALF >= SIDE
        if not over_row and not over_col:
            merge_to_window[target, source] = 1
            window_to_merge[source, target] = 1
            continue
        kind = 2 if over_row and over_col else (0 if over_row else 1)
        slot = HALO[kind][0] + ahead[kind]
        ahead[kind] += 1
        merge_send[slot, source] = 1
        merge_to_window[target, FINE + slot] = 1
        window_send[slot, target] = 1
        window_to_merge[source, FINE + slot] = 1
    by_slot = np.zeros((4 * SHARE, HIGH * ROWS), np.float32)
    into_fine = np.zeros((HIGH * ROWS, SHARE), np.float32)
    for h in range(HIGH):
        for head in range(3):
            into_fine[h * ROWS + 12 + head, 4 * h + head] = 1
            for slot in range(4):
                by_slot[slot * SHARE + 4 * h + head, h * ROWS + 4 * slot + head] = 1
    coarse_native = np.zeros((TOK, TOK), np.float32)
    for z in range(2):
        for i in range(6):
            for j in range(6):
                coarse_native[z * 36 + i * 6 + j, (i * 6 + j) * 2 + z] = 1
    return (
        native_to_merge, native_to_merge.T, merge_send, merge_to_window,
        window_send, window_to_merge, coarse_native, coarse_native.T, label_row, label_col,
        by_slot, into_fine,
    )


def dot(a, b):
    return lax.dot_general(a, b, (((1,), (0,)), ((), ())), preferred_element_type=F32)


def dot_nt(a, b):
    return lax.dot_general(a, b, (((1,), (1,)), ((), ())), preferred_element_type=F32)


def dot_tn(a, b):
    return lax.dot_general(a, b, (((0,), (0,)), ((), ())), preferred_element_type=F32)


def rounded(values):
    return values.astype(BF16).astype(F32)


def layer_norm(values):
    centred = values - jnp.mean(values, axis=-1, keepdims=True)
    inverse = lax.rsqrt(jnp.mean(centred * centred, axis=-1, keepdims=True) + EPSILON)
    return centred * inverse, inverse


def norm_back(normed, inverse, upstream):
    mean_up = jnp.mean(upstream, axis=-1, keepdims=True)
    mean_cross = jnp.mean(upstream * normed, axis=-1, keepdims=True)
    return inverse * (upstream - mean_up - normed * mean_cross)


def gelu_both(pre_act):
    decay = jnp.exp(-0.5 * pre_act * pre_act)
    t = 1.0 / (1.0 + (0.3275911 * HALF_ROOT) * jnp.abs(pre_act))
    poly = 0.5 * 1.061405429
    for factor in (-1.453152027, 1.421413741, -0.284496736, 0.254829592):
        poly = poly * t + 0.5 * factor
    tail = poly * t * decay
    half = jnp.where(pre_act < 0.0, tail, 1.0 - tail)
    return pre_act * half, half + pre_act * decay * DENSITY


def head_masks(width):
    lane = lax.broadcasted_iota(jnp.int32, (1, width), 1)
    return [(lane >= 32 * h) & (lane < 32 * h + 32) for h in range(width // 32)]


def stack_heads(values, masks):
    return jnp.concatenate([jnp.where(m, values, 0.0) for m in masks], axis=0).astype(BF16)


def unstack_heads(values, masks):
    total = jnp.where(masks[0], values[:TOK], 0.0)
    for h in range(1, len(masks)):
        total = jnp.where(masks[h], values[h * TOK : (h + 1) * TOK], total)
    return total


def softmax(scores):
    weights = jnp.exp(scores - jnp.max(scores, axis=-1, keepdims=True))
    return weights * (1.0 / jnp.sum(weights, axis=-1, keepdims=True))


def table_scatter(grads, chosen, high):
    def step(p, total):
        parts = []
        for half in range(2):
            i = 2 * p + half
            rows = grads[pl.ds(i, ROWS, stride=TOK), :].astype(BF16)
            picked = jnp.broadcast_to(high[pl.ds(i, 1), :], (ROWS, LANES)).astype(BF16)
            zero = jnp.zeros_like(rows)
            parts.append(
                jnp.concatenate(
                    [jnp.where(picked == jnp.asarray(h, BF16), rows, zero) for h in range(HIGH)],
                    axis=0,
                )
            )
        return total + dot(jnp.concatenate(parts, axis=1), chosen[p])

    return lax.fori_loop(0, TOK // 2, step, jnp.zeros((HIGH * ROWS, LANES), F32), unroll=UNROLL)


def table_gather(table, out, chosen, high):
    entries = table[...].astype(BF16)

    def step(p, carry):
        spread = dot_nt(entries, chosen[p])
        for half in range(2):
            i = 2 * p + half
            picked = jnp.broadcast_to(high[pl.ds(i, 1), :], (ROWS, LANES))
            span = slice(half * LANES, (half + 1) * LANES)
            found = spread[:ROWS, span]
            for h in range(1, HIGH):
                found = jnp.where(picked == h, spread[h * ROWS : (h + 1) * ROWS, span], found)
            out[pl.ds(i, ROWS, stride=TOK), :] = found
        return carry

    lax.fori_loop(0, TOK // 2, step, 0, unroll=UNROLL)


def kernel(
    lats,
    rings,
    own_qkv, own_proj, own_up, own_down, *rest,
):
    stored, rest = rest[:FETCHED], rest[FETCHED:]
    outs, rest = rest[:3], rest[3:]
    held, rest = rest[:FETCHED], rest[FETCHED:]
    body(
        lats, rings, own_qkv, own_proj, own_up, own_down, stored, held, *held, *outs, *rest
    )


def body(
    lats, rings, own_qkv, own_proj, own_up, own_down, stored, held,
    fields, native_to_merge, merge_send, region, bias_index, fine_bias, coarse_bias,
    label_row, label_col,
    merge_to_window, fine_qkv, fine_proj, window_send, window_to_merge, fine_up, fine_down,
    merge_weight, cotangent, coarse_native, coarse_back, merge_to_native,
    by_slot, into_fine,
    coarse_result, grad_result, table_sums,
    halo_out, halo_in, got_all, got_cbias,
    label_rows, high, chosen, table, bias, grads_fine, grads_coarse,
    queries, keys, values, probs, score_grads, slope, first_ref, cprobs, chidden, coarse_ref,
    spread_ref, label_ref, attended, outer_ref, qkv_grads, cqueries, ckeys, cvalues,
    part_fine, ring_fine, group_fine, final_fine,
    part_coarse, got_coarse,
    late_sems, halo_send, halo_recv, weight_send, weight_recv, cbias_send, cbias_recv,
    fine_sems, coarse_sems,
):
    got_qkv = got_all.at[:, pl.ds(0, 288)]
    got_proj = got_all.at[:, pl.ds(288, 96)]
    got_up = got_all.at[:, pl.ds(384, 384)]
    got_down = got_all.at[:, pl.ds(768, 384)]
    lat = lax.axis_index("lat")
    ring = lax.axis_index("lon")
    group = lax.axis_index("grp")
    column = ring * 4 + group
    columns = rings * 4

    def place(row_shift, col_shift):
        row = lax.rem(lat + row_shift + lats, lats)
        col = lax.rem(column + col_shift + columns, columns)
        return {"lat": row, "lon": lax.div(col, 4), "grp": lax.rem(col, 4)}

    before = (place(-1, 0), place(0, -1), place(-1, -1))
    after = (place(1, 0), place(0, 1), place(1, 1))
    core_mate = group + 1 - 2 * lax.rem(group, 2)
    chip_mate = lax.rem(group + 2, 4)
    far_mate = lax.rem(core_mate + 2, 4)
    mates = (core_mate, chip_mate, far_mate)

    copies = [
        pltpu.make_async_copy(source, target, late_sems.at[k])
        for k, (source, target) in enumerate(zip(stored, held))
    ]
    early, loads = copies[:EARLY], copies[EARLY:]
    owns = [
        pltpu.make_async_copy(own, got.at[0], late_sems.at[FETCHED + k])
        for k, (own, got) in enumerate(
            ((own_qkv, got_qkv), (own_proj, got_proj), (own_up, got_up), (own_down, got_down))
        )
    ]
    for copy in copies:
        copy.start()
    barrier = pltpu.get_barrier_semaphore()
    for device in before + after:
        pl.semaphore_signal(barrier, 1, device_id=device, device_id_type=MESH)
    for mate in mates:
        pl.semaphore_signal(barrier, 1, device_id={"grp": mate}, device_id_type=MESH)
    far_lat = lax.rem(lat + lats // 2, lats)
    neighbours = ({"grp": chip_mate}, {"lat": far_lat, "grp": chip_mate})
    pl.semaphore_signal(barrier, 1, device_id=neighbours[1], device_id_type=MESH)
    for step in range(1, rings):
        pl.semaphore_signal(
            barrier, 1, device_id={"lon": lax.rem(ring + step, rings)}, device_id_type=MESH
        )

    def remote(source, target, send, recv, device):
        copy = pltpu.make_async_remote_copy(
            source, target, send, recv, device_id=device, device_id_type=MESH
        )
        copy.start()
        return copy

    def together(sent, got, send, recv):
        return pltpu.make_async_remote_copy(
            sent, got, send, recv, device_id={"grp": core_mate}, device_id_type=MESH
        )

    def send_halo(number, devices, block):
        halo_out[number] = block.astype(BF16)
        for kind, (start, size) in enumerate(HALO):
            rows = pl.ds(start, size)
            remote(
                halo_out.at[number, rows], halo_in.at[number, rows],
                halo_send.at[number], halo_recv.at[number], devices[kind],
            )
        return [
            together(
                halo_out.at[number], halo_in.at[number], halo_send.at[number], halo_recv.at[number]
            )
        ]

    def wait(copies):
        for copy in copies:
            copy.wait()

    for copy in owns:
        copy.start()
    for copy in early[:3] + owns:
        copy.wait()

    tokens = dot(native_to_merge[...], fields[...].astype(F32).reshape(FINE, 192).astype(BF16))
    tokens_half = tokens.astype(BF16)
    first_block = dot(merge_send[...], tokens_half)
    pl.semaphore_wait(barrier, 10 + rings - 1)
    pending = send_halo(0, before, first_block)

    shares = tuple(
        tuple(got_all.at[slot, pl.ds(start, size)] for slot in range(4))
        for start, size in ((0, 384), (384, 768))
    )
    to_chip, to_core, passed = [], [], []

    def half_of(ref, half):
        rows = ref.shape[0] // 2
        return ref.at[pl.ds(half * rows, rows)]

    for k, (own, mate_slot, chip_slot, far_slot) in enumerate(shares):
        to_chip.append(
            [
                remote(
                    half_of(own, half), half_of(chip_slot, half),
                    weight_send.at[k, half], weight_recv.at[k, half], neighbours[half],
                )
                for half in range(2)
            ]
        )
    for k, (own, mate_slot, chip_slot, far_slot) in enumerate(shares):
        to_core.append(
            remote(own, mate_slot, weight_send.at[k, 2], weight_recv.at[k, 2], {"grp": core_mate})
        )

    def pass_on(k):
        chip_slot, far_slot = shares[k][2:]
        for copy in to_chip[k]:
            copy.wait_recv()
        passed.append(
            remote(
                chip_slot, far_slot, weight_send.at[k, 3], weight_recv.at[k, 3], {"grp": core_mate}
            )
        )

    for copy in early[3:]:
        copy.wait()
    index = bias_index[...]
    high[...] = jnp.zeros_like(high)
    high[:, :TOK] = lax.shift_right_logical(index, 7)
    low = (index & (LANES - 1)).astype(F32).astype(BF16)
    key_row = lax.broadcasted_iota(jnp.int32, (LANES, TOK), 0)
    key_col = lax.broadcasted_iota(jnp.int32, (LANES, TOK), 1)
    identity = jnp.where(key_row == key_col, 1.0, 0.0).astype(BF16)
    low_keys = jnp.where(key_row < TOK, dot_nt(identity, low), -1.0)[:KEYS].astype(BF16)
    query = lax.broadcasted_iota(jnp.int32, (TOK, 2 * LANES), 0)
    lane = lax.broadcasted_iota(jnp.int32, (TOK, 2 * LANES), 1)
    target_query = query - lax.shift_right_logical(lane, 7)
    lane = (lax.broadcasted_iota(jnp.int32, (KEYS, 2 * LANES), 1) & (LANES - 1)).astype(F32)
    blank = jnp.zeros((LANES - KEYS, LANES), BF16)

    def choose(p, carry):
        pick = jnp.where(target_query == 2 * p, 1.0, 0.0).astype(BF16)
        found = jnp.where(dot(low_keys, pick) == lane, 1.0, 0.0).astype(BF16)
        for half in range(2):
            at = half * LANES
            chosen[p, at : at + KEYS, :] = found[:, at : at + LANES]
            chosen[p, at + KEYS : at + LANES, :] = blank
        return carry

    lax.fori_loop(0, TOK // 2, choose, 0, unroll=UNROLL)
    table[...] = jnp.zeros_like(table)
    length = fine_bias.shape[2]
    for h in range(HIGH):
        size = min(LANES, length - h * LANES)
        span = slice(h * LANES, h * LANES + size)
        for head in range(6):
            at = h * ROWS + 2 * head
            table[at : at + 2, :size] = fine_bias[head, :, span].astype(F32)
        at = h * ROWS + 12
        table[at : at + 3, :size] = coarse_bias[0, :, span].astype(F32)
    table_gather(table, bias, chosen, high)
    got_cbias[0] = bias[12 * TOK : 12 * TOK + 224, :].astype(BF16)
    cbias_copies = [
        remote(got_cbias.at[0], got_cbias.at[k + 1], cbias_send.at[k], cbias_recv.at[k], {"grp": mate})
        for k, mate in enumerate(mates)
    ]
    grads_fine[...] = jnp.zeros_like(grads_fine)
    grads_coarse[...] = jnp.zeros_like(grads_coarse)

    fine_masks = head_masks(192)
    for i in range(SIDE):
        label_rows[2 * i : 2 * i + 2, :] = region[i].astype(F32)
    spread_labels = dot(label_row[...], label_rows[...].astype(BF16)) * label_col[...].astype(F32)
    col_labels = jnp.sum(spread_labels, axis=-1, keepdims=True)
    ones = jnp.ones((8, SIDE), BF16)
    spread_ref[...] = spread_labels
    label_ref[...] = col_labels
    loads[0].wait()
    loads[1].wait()
    local = dot(merge_to_window[:, :FINE], tokens_half)
    wait(pending)
    shifted = local + dot(merge_to_window[:, FINE:], halo_in[0])
    fine_normed, fine_inverse = layer_norm(shifted)
    fine_half = fine_normed.astype(BF16)
    for k, ref in enumerate((queries, keys, values)):
        ref[...] = rounded(dot(fine_half, fine_qkv[k]))

    def window_span(w):
        return pl.ds(pl.multiple_of(w * TOK, 8), TOK)

    def attend(w, carry):
        span = window_span(w)
        stacked = stack_heads(queries[span, :], fine_masks)
        scores = dot_nt(stacked, keys[span, :].astype(BF16)) * SCALING
        kind = w // 2
        scores = scores + jnp.concatenate(
            [bias[window_span(2 * h + kind), :TOK] for h in range(6)], axis=0
        )
        row_labels = dot_nt(ones, spread_ref[span, :].astype(BF16))[:1]
        allowed = label_ref[span, :] == row_labels
        scores = jnp.where(allowed[None], scores.reshape(6, TOK, TOK), NEGATIVE)
        weights = softmax(scores.reshape(6 * TOK, TOK))
        probs[w] = weights
        attended[span, :] = unstack_heads(
            dot(weights.astype(BF16), values[span, :].astype(BF16)), fine_masks
        )
        return carry

    lax.fori_loop(0, 4, attend, 0, unroll=LOOP)
    for k in range(2, 5):
        loads[k].wait()
    branch = dot(attended[...].astype(BF16), fine_proj[...]).astype(BF16)
    pending = send_halo(1, after, dot(window_send[...], branch))
    local = tokens + dot(window_to_merge[:, :FINE], branch)
    for k in range(8, 14):
        loads[k].wait()
    upstream = dot(
        coarse_native[...], cotangent[...].astype(F32).reshape(TOK, 384).astype(BF16)
    )
    pass_on(0)
    wait(pending)
    first = rounded(local + dot(window_to_merge[:, FINE:], halo_in[1]))
    first_ref[...] = first

    for k in range(5, 8):
        loads[k].wait()
    normed, inverse = layer_norm(first)
    hidden, slopes = gelu_both(dot(normed.astype(BF16), fine_up[...]))
    slope[...] = slopes
    second = rounded(first + dot_nt(hidden.astype(BF16), fine_down[...]))
    cells = [second[g * TOK : (g + 1) * TOK] for g in range(4)]
    width = 4 * second.shape[1]
    mean = sum(jnp.sum(c, axis=-1, keepdims=True) for c in cells) / width
    cells = [c - mean for c in cells]
    variance = sum(jnp.sum(c * c, axis=-1, keepdims=True) for c in cells) / width
    joined_inverse = lax.rsqrt(variance + EPSILON)
    cells = [c * joined_inverse for c in cells]
    merged = jnp.zeros((TOK, merge_weight.shape[1]), F32)
    for g in range(4):
        merged += dot(cells[g].astype(BF16), merge_weight[g * 192 : (g + 1) * 192, :])
    merged = rounded(merged)
    pass_on(1)

    coarse_masks = head_masks(96)
    base_normed, base_inverse = layer_norm(merged)
    base_half = base_normed.astype(BF16)
    wait(cbias_copies)

    def arrive(k):
        to_core[k].wait_recv()
        passed[k].wait_recv()

    arrive(0)

    def coarse_attend(g, total):
        q, k, v = (
            rounded(dot_nt(base_half, got_qkv[g, n * 96 : (n + 1) * 96, :])) for n in range(3)
        )
        cqueries[g] = q
        ckeys[g] = k
        cvalues[g] = v
        stacked = stack_heads(q, coarse_masks)
        scores = dot_nt(stacked, k.astype(BF16)) * SCALING
        scores = scores + got_cbias[g].astype(F32)[: 3 * TOK, :TOK]
        weights = softmax(scores)
        cprobs[g] = weights
        seen = unstack_heads(dot(weights.astype(BF16), v.astype(BF16)), coarse_masks)
        return total + dot(seen.astype(BF16), got_proj[g])

    coarse_first = rounded(lax.fori_loop(0, 4, coarse_attend, merged, unroll=LOOP))
    up_normed, up_inverse = layer_norm(coarse_first)
    up_half = up_normed.astype(BF16)
    arrive(1)

    upstream_half = upstream.astype(BF16)

    def coarse_mlp(g, total):
        hidden, slopes = gelu_both(dot(up_half, got_up[g]))
        chidden[g] = hidden.astype(BF16)
        grad_pre = dot_nt(upstream_half, got_down[g]) * slopes
        return total + dot_nt(grad_pre.astype(BF16), got_up[g])

    blank = jnp.zeros((TOK, 384), F32)
    total = lax.fori_loop(0, 4, coarse_mlp, blank, unroll=LOOP)
    coarse_ref[...] = coarse_first

    grad_first = upstream + norm_back(up_normed, up_inverse, total)
    grad_half = grad_first.astype(BF16)

    def coarse_attend_back(g, total):
        stacked = stack_heads(cqueries[g], coarse_masks)
        weights = cprobs[g]
        outer = stack_heads(rounded(dot_nt(grad_half, got_proj[g])), coarse_masks)
        grad_probs = dot_nt(outer, cvalues[g].astype(BF16))
        grad_scores = weights * (
            grad_probs - jnp.sum(grad_probs * weights, axis=-1, keepdims=True)
        )
        for h in range(3):
            at = window_span(4 * g + h)
            grads_coarse[at, :TOK] = grad_scores[h * TOK : (h + 1) * TOK]
        grad_scores = grad_scores.astype(BF16)
        grad_v = dot_tn(weights.astype(BF16), outer)
        grad_q = unstack_heads(dot(grad_scores, ckeys[g].astype(BF16)), coarse_masks) * SCALING
        grad_k = dot_tn(grad_scores, stacked) * SCALING
        for n, grad in enumerate((grad_q, grad_k, grad_v)):
            total = total + dot(grad.astype(BF16), got_qkv[g, n * 96 : (n + 1) * 96, :])
        return total

    total = lax.fori_loop(0, 4, coarse_attend_back, blank, unroll=LOOP)
    grad_merged = (grad_first + norm_back(base_normed, base_inverse, total)).astype(BF16)

    joined = [dot_nt(grad_merged, merge_weight[g * 192 : (g + 1) * 192, :]) for g in range(4)]
    mean_up = sum(jnp.sum(j, axis=-1, keepdims=True) for j in joined) / width
    mean_cross = (
        sum(jnp.sum(j * c, axis=-1, keepdims=True) for j, c in zip(joined, cells)) / width
    )
    grad_second = jnp.concatenate(
        [joined_inverse * (j - mean_up - c * mean_cross) for j, c in zip(joined, cells)], axis=0
    )
    grad_pre = dot(grad_second.astype(BF16), fine_down[...]) * slope[...]
    grad_normed = dot_nt(grad_pre.astype(BF16), fine_up[...])
    normed, inverse = layer_norm(first_ref[...])
    grad_fine = grad_second + norm_back(normed, inverse, grad_normed)
    first_ref[...] = grad_fine
    grad_half = grad_fine.astype(BF16)
    pending = send_halo(2, before, dot(merge_send[...], grad_half))

    share = BLOCKS * ROWS // rings

    def sum_start(sums, part, got, sems):
        sums = sums.astype(BF16)
        blank = jnp.zeros((BLOCKS * ROWS - HIGH * ROWS, LANES), BF16)
        part[...] = jnp.concatenate([sums, blank], axis=0).reshape(rings, share, LANES)
        for step in range(1, rings):
            peer = lax.rem(ring + step, rings)
            remote(part.at[peer], got.at[step], sems.at[0], sems.at[1], {"lon": peer})
        others = pl.ds(1, rings - 1)
        return [together(part.at[others], got.at[others], sems.at[0], sems.at[1])]

    def sum_group(copies, part, got, grouped, sems):
        wait(copies)
        total = part[ring].astype(F32) + jnp.sum(got[1:].astype(F32), axis=0)
        grouped[group] = total
        for mate in mates:
            remote(grouped.at[group], grouped.at[group], sems.at[2], sems.at[3], {"grp": mate})
        others = pl.ds(0, 3)
        return [together(grouped.at[others], grouped.at[others], sems.at[2], sems.at[3])]

    def sum_spread(copies, grouped, final, sems):
        wait(copies)
        total = grouped[0] + grouped[1] + grouped[2] + grouped[3]
        row = lax.broadcasted_iota(jnp.int32, total.shape, 0)
        total = jnp.where(lax.rem(row, ROWS) < 12, total, grouped[group])
        final[ring] = total.astype(BF16)
        for step in range(1, rings):
            peer = lax.rem(ring + step, rings)
            remote(final.at[ring], final.at[ring], sems.at[4], sems.at[5], {"lon": peer})
        others = pl.ds(0, rings - 1)
        return [together(final.at[others], final.at[others], sems.at[4], sems.at[5])]

    def sum_end(copies, final):
        wait(copies)
        return final[...].reshape(BLOCKS * ROWS, LANES)

    sums = table_scatter(grads_coarse, chosen, high).astype(BF16)
    part_coarse[...] = dot(by_slot[...], sums).astype(BF16).reshape(4, SHARE, LANES)
    for k, mate in enumerate(mates):
        remote(
            part_coarse.at[k + 1], got_coarse.at[k + 1], coarse_sems.at[0], coarse_sems.at[1],
            {"grp": mate},
        )
    others = pl.ds(1, 3)
    coarse_copies = [
        together(
            part_coarse.at[others], got_coarse.at[others], coarse_sems.at[0], coarse_sems.at[1]
        )
    ]

    local = dot(merge_to_window[:, :FINE], grad_half)
    wait(pending)
    grad_branch = local + dot(merge_to_window[:, FINE:], halo_in[2])
    outer_all = rounded(dot_nt(grad_branch.astype(BF16), fine_proj[...]))
    outer_ref[...] = outer_all

    def attend_back(w, carry):
        weights = probs[w]
        span = window_span(w)
        outer = stack_heads(outer_ref[span, :], fine_masks)
        grad_probs = dot_nt(outer, values[span, :].astype(BF16))
        score_grads[w] = weights * (
            grad_probs - jnp.sum(grad_probs * weights, axis=-1, keepdims=True)
        )
        return carry

    lax.fori_loop(0, 4, attend_back, 0, unroll=LOOP)
    for kind in range(2):
        both = score_grads[2 * kind] + score_grads[2 * kind + 1]
        for h in range(6):
            at = (2 * h + kind) * TOK
            grads_fine[at : at + TOK, :TOK] = both[h * TOK : (h + 1) * TOK]
    sums = table_scatter(grads_fine, chosen, high)
    wait(coarse_copies)
    own_heads = part_coarse[0].astype(F32) + jnp.sum(got_coarse[1:].astype(F32), axis=0)
    sums = sums + dot(into_fine[...], own_heads.astype(BF16))
    fine_copies = sum_start(sums, part_fine, ring_fine, fine_sems)

    def project_back(w, carry):
        span = window_span(w)
        outer = stack_heads(outer_ref[span, :], fine_masks)
        stacked = stack_heads(queries[span, :], fine_masks)
        grad_scores = score_grads[w].astype(BF16)
        grad_q = unstack_heads(dot(grad_scores, keys[span, :].astype(BF16)), fine_masks)
        qkv_grads[0, span, :] = grad_q * SCALING
        qkv_grads[1, span, :] = dot_tn(grad_scores, stacked) * SCALING
        qkv_grads[2, span, :] = dot_tn(probs[w].astype(BF16), outer)
        return carry

    lax.fori_loop(0, 4, project_back, 0, unroll=LOOP)
    fine_copies = sum_group(fine_copies, part_fine, ring_fine, group_fine, fine_sems)
    grad_normed = jnp.zeros((FINE, 192), F32)
    for n in range(3):
        grad_normed += dot_nt(qkv_grads[n].astype(BF16), fine_qkv[n])
    grad_shifted = norm_back(fine_normed, fine_inverse, grad_normed).astype(BF16)
    pending = send_halo(3, after, dot(window_send[...], grad_shifted))
    fine_copies = sum_spread(fine_copies, group_fine, final_fine, fine_sems)

    total = coarse_ref[...]
    for g in range(4):
        total = total + dot(chidden[g], got_down[g])
    coarse_result[...] = dot(coarse_back[...], total.astype(BF16))
    local = first_ref[...] + dot(window_to_merge[:, :FINE], grad_shifted)
    wait(pending)
    grad = local + dot(window_to_merge[:, FINE:], halo_in[3])
    upper = grad.astype(BF16)
    lower = (grad - upper.astype(F32)).astype(BF16)
    grad_result[...] = dot(merge_to_native[...], upper) + dot(merge_to_native[...], lower)

    for k in range(2):
        for copy in to_chip[k]:
            copy.wait_send()
        to_core[k].wait_send()
        passed[k].wait_send()
    table_sums[...] = sum_end(fine_copies, final_fine)


def finish(
    grad_result, coarse_result, table_sums,
    coarse_out, grad_fields, grad_fine_bias, grad_coarse_bias,
):
    grad_fields[...] = grad_result[...].reshape(SIDE, SIDE, 2, 192)
    coarse_out[...] = coarse_result[...].reshape(6, 6, 2, 384).astype(BF16)
    length = grad_fine_bias.shape[2]
    sums = table_sums[...].astype(F32)
    for h in range(HIGH):
        size = min(LANES, length - h * LANES)
        span = slice(h * LANES, h * LANES + size)
        for head in range(6):
            at = h * ROWS + 2 * head
            grad_fine_bias[head, :, span] = sums[at : at + 2, :size]
        for head in range(3):
            at = h * ROWS + 12 + head
            grad_coarse_bias[head, :, span] = sums[at : at + 1, :size]


def shards(
    fields, region, bias_index, fine_bias, coarse_bias, fine_qkv, fine_proj, fine_up, fine_down,
    merge_weight, coarse_qkv, coarse_proj, coarse_up, coarse_down, out_cotangent,
):
    lats = lax.axis_size("lat")
    rings = lax.axis_size("lon")
    share = BLOCKS * ROWS // rings
    (
        native_to_merge, merge_to_native, merge_send, merge_to_window, window_send,
        window_to_merge, coarse_native, coarse_back, label_row, label_col, by_slot, into_fine,
    ) = (jnp.asarray(c, BF16) for c in permutations())
    early = (
        jnp.transpose(fields, (1, 2, 0, 3)), native_to_merge, merge_send,
        jnp.transpose(region, (1, 0, 2)), bias_index,
        jnp.transpose(fine_bias, (2, 0, 1)), jnp.transpose(coarse_bias, (0, 2, 1)),
        label_row, label_col,
    )
    owns = (
        jnp.transpose(coarse_qkv, (1, 2, 0)).reshape(3 * 96, 384), coarse_proj, coarse_up,
        coarse_down,
    )
    late = (
        merge_to_window, jnp.transpose(fine_qkv, (1, 0, 2)), fine_proj, window_send,
        window_to_merge, fine_up, fine_down.T, merge_weight,
        jnp.transpose(out_cotangent, (1, 2, 0, 3)), coarse_native, coarse_back,
        merge_to_native, by_slot, into_fine,
    )
    vmem = pltpu.VMEM
    dma = pltpu.SemaphoreType.DMA
    sum_buffers = [
        vmem((rings, share, LANES), BF16),
        vmem((rings, share, LANES), BF16),
        vmem((4, share, LANES), F32),
        vmem((rings, share, LANES), BF16),
    ]
    scratch = [vmem(a.shape, a.dtype) for a in early + late]
    scratch += [
        vmem((4, HALO_ROWS, 192), BF16),
        vmem((4, HALO_ROWS, 192), BF16),
        vmem((4, 1152, 384), BF16),
        vmem((4, 224, LANES), BF16),
        vmem((2 * SIDE, SIDE), F32),
        vmem((TOK, LANES), jnp.int32),
        vmem((TOK // 2, 2 * LANES, LANES), BF16),
        vmem((HIGH * ROWS, LANES), F32),
        vmem((ROWS * TOK, LANES), F32),
        vmem((ROWS * TOK, LANES), F32),
        vmem((ROWS * TOK, LANES), F32),
        vmem((FINE, 192), F32),
        vmem((FINE, 192), F32),
        vmem((FINE, 192), F32),
        vmem((4, 6 * TOK, TOK), F32),
        vmem((4, 6 * TOK, TOK), F32),
        vmem((FINE, 768), F32),
        vmem((FINE, 192), F32),
        vmem((4, 3 * TOK, TOK), F32),
        vmem((4, TOK, 384), BF16),
        vmem((TOK, 384), F32),
        vmem((FINE, SIDE), F32),
        vmem((FINE, 1), F32),
        vmem((FINE, 192), F32),
        vmem((FINE, 192), F32),
        vmem((3, FINE, 192), F32),
        vmem((4, TOK, 96), F32),
        vmem((4, TOK, 96), F32),
        vmem((4, TOK, 96), F32),
    ]
    scratch += sum_buffers + [vmem((4, SHARE, LANES), BF16), vmem((4, SHARE, LANES), BF16)]
    scratch += [
        dma((FETCHED + 4,)), dma((4,)), dma((4,)), dma((4, 4)), dma((4, 4)), dma((3,)), dma((3,)),
        dma((6,)), dma((2,)),
    ]
    whole = pl.BlockSpec(memory_space=pltpu.VMEM)
    hbm = pl.BlockSpec(memory_space=pl.ANY)
    coarse_result, grad_result, table_sums = pl.pallas_call(
        functools.partial(kernel, lats, rings),
        out_shape=(
            jax.ShapeDtypeStruct((TOK, 384), F32),
            jax.ShapeDtypeStruct((FINE, 192), F32),
            jax.ShapeDtypeStruct((BLOCKS * ROWS, LANES), BF16),
        ),
        in_specs=[hbm] * (len(owns) + FETCHED),
        out_specs=(whole,) * 3,
        scratch_shapes=scratch,
        compiler_params=pltpu.CompilerParams(
            collective_id=0, has_side_effects=True, vmem_limit_bytes=56 * 1024 * 1024
        ),
    )(*owns, *early, *late)
    outs = pl.pallas_call(
        finish,
        out_shape=(
            jax.ShapeDtypeStruct((6, 6, 2, 384), BF16),
            jax.ShapeDtypeStruct((SIDE, SIDE, 2, 192), F32),
            jax.ShapeDtypeStruct((6, 2, fine_bias.shape[1]), F32),
            jax.ShapeDtypeStruct((3, 1, fine_bias.shape[1]), F32),
        ),
        in_specs=[whole] * 3,
        out_specs=(whole,) * 4,
        compiler_params=pltpu.CompilerParams(vmem_limit_bytes=60 * 1024 * 1024),
    )(grad_result, coarse_result, table_sums)
    return (
        jnp.transpose(outs[0], (2, 0, 1, 3)),
        jnp.transpose(outs[1], (2, 0, 1, 3)),
        jnp.transpose(outs[2], (1, 2, 0)),
        jnp.transpose(outs[3], (1, 2, 0)),
    )


def solution(mesh):
    return jax.shard_map(
        shards,
        mesh=mesh,
        in_specs=(
            P(None, "lat", ("lon", "grp"), None),
            P(None, "lat", ("lon", "grp")),
            P(),
            P("lat", None, None),
            P("lat", None, "grp"),
            P(),
            P(),
            P(),
            P(),
            P(),
            P(None, None, "grp"),
            P("grp", None),
            P(None, "grp"),
            P("grp", None),
            P(None, "lat", ("lon", "grp"), None),
        ),
        out_specs=(
            P(None, "lat", ("lon", "grp"), None),
            P(None, "lat", ("lon", "grp"), None),
            P("lat", None, None),
            P("lat", None, "grp"),
        ),
        check_vma=False,
    )
```
